32 devices in a mesh: dp: 16 (over z, y, x), blk: 2 (over core).
Axes of the slice: x: 2, y: 2, z: 4, core: 2. Of those that a mesh axis runs over, the one named last changes fastest.
Arguments:
- inputs: bfloat16 [16, 784, 768], P('dp', 'blk'), may hold values from -6 to 6
- segments: int32 [16, 784], P('dp', 'blk'), may hold values from 0 to 7, never falling along the last dimension, each value on 1 to 196 neighbouring positions
- positions: int32 [16, 784], P('dp', 'blk'), may hold values from 0 to 195
- pos_table: bfloat16 [196, 768], replicated, may hold values from -3 to 3
- ln1_gain: float32 [768], replicated, may hold values from 0.5 to 1.5
- ln1_shift: float32 [768], replicated, may hold values from -1.5 to 1.5
- qkv_weight: bfloat16 [768, 2304], replicated, may hold values from -0.21875 to 0.21875
- query_bias: float32 [768], replicated, may hold values from -1.5 to 1.5
- value_bias: float32 [768], replicated, may hold values from -1.5 to 1.5
- out_weight: bfloat16 [768, 768], replicated, may hold values from -1.25 to 1.25
- out_bias: float32 [768], replicated, may hold values from -1.5 to 1.5
- ln2_gain: float32 [768], replicated, may hold values from 0.5 to 1.5
- ln2_shift: float32 [768], replicated, may hold values from -1.5 to 1.5
- fc1_weight: bfloat16 [768, 3072], replicated, may hold values from -0.21875 to 0.21875
- fc1_bias: float32 [3072], replicated, may hold values from -1.5 to 1.5
- fc2_weight: bfloat16 [3072, 768], replicated, may hold values from -0.109375 to 0.109375
- fc2_bias: float32 [768], replicated, may hold values from -1.5 to 1.5
- cotangent: bfloat16 [16, 784, 768], P('dp', 'blk'), may hold values from -6 to 6
Outputs:
- result: bfloat16 [16, 784, 768], P('dp', 'blk')
- input_grad: bfloat16 [16, 784, 768], P('dp', 'blk')
- table_grad: float32 [196, 768], replicated
- ln1_gain_grad: float32 [768], replicated
- ln1_shift_grad: float32 [768], replicated
- qkv_grad: float32 [768, 2304], P(('dp', 'blk'))
- query_bias_grad: float32 [768], replicated
- value_bias_grad: float32 [768], replicated
- out_grad: float32 [768, 768], P(('dp', 'blk'))
- out_bias_grad: float32 [768], replicated
- ln2_gain_grad: float32 [768], replicated
- ln2_shift_grad: float32 [768], replicated
- fc1_grad: float32 [768, 3072], P(('dp', 'blk'))
- fc1_bias_grad: float32 [3072], replicated
- fc2_grad: float32 [3072, 768], P(('dp', 'blk'))
- fc2_bias_grad: float32 [768], replicated
The draws below stay inside these ranges and needn't reach their ends.
Inputs may be any that keep to these rules, and one draw needn't show every extreme that they name: `segments`: crop ids of a row never fall, each crop has 1 to 196 tokens.
All inputs are finite; a program needn't handle non-finite values.
Results may differ from the reference program's by a relative error of at most 0.013.
Values may be sent and summed in bfloat16 or wider, within the bound.
No kernel may reach another device: no remote copies, remote signals or barrier semaphores. Data moves between devices by JAX's collectives and lax.ppermute only.
A program may use at most 192 MiB of HBM per device.

```python
import math
import jax
import jax.numpy as jnp
import numpy as np
from jax import lax

D = 768
FF = 3072
H = 12
HD = 64
POS = 196
L = 784
ROWS = 16
SEG_MOST = 196
CROPS = 8


def touch_ends(array, stream_key, low, top_value):
    dims = array.shape
    spot = [jax.random.randint(jax.random.fold_in(stream_key, axis), (), 0, dims[axis]) for axis in range(len(dims))]
    array = array.at[tuple(spot)].set(low)
    longest = dims.index(max(dims))
    spot[longest] = (spot[longest] + 1) % dims[longest]
    return array.at[tuple(spot)].set(top_value)


def level_of(stream_key, extent, split, smallest, largest):
    loudness = 1.0
    for position, blocks in split:
        heights = jax.random.uniform(jax.random.fold_in(jax.random.fold_in(stream_key, 6), position), (blocks,), jnp.float32, smallest / len(split), largest / len(split))
        loudness = loudness * jnp.repeat(jnp.exp(heights), extent[position] // blocks).reshape((-1,) + (1,) * (len(extent) - 1 - position))
    return loudness


def length_profile(number_of, total, reach, slope):
    loads = [(1 << 20) // math.isqrt(grade ** slope) + 1 for grade in range(2, number_of + 1)]
    surplus, given = total - reach - (number_of - 1), [1] * (number_of - 1)
    while surplus > 0:
        free = [i for i in range(number_of - 1) if given[i] < reach]
        mass, budget = sum([loads[i] for i in free]), surplus
        for i in free:
            more = min(reach - given[i], max(1, budget * loads[i] // mass), surplus)
            given[i] = given[i] + more
            surplus = surplus - more
    return np.array([reach] + given)


def ragged_sizes(rng, number_of, total, reach, slope):
    if number_of == 2:
        one = jax.random.randint(rng, (), max(1, total - reach), min(reach, total - 1) + 1)
        return jnp.stack([one, total - one])
    sizes = jnp.asarray(length_profile(number_of, total, reach, slope), jnp.int32)
    twos = (number_of - 1) // 2
    donor, taker = sizes[1:1 + 2 * twos:2], sizes[2:2 + 2 * twos:2]
    slack = jnp.minimum(donor - 1, reach - taker)
    passed = jax.random.randint(jax.random.fold_in(rng, 1), (twos,), 0, 1 << 20) % (slack + 1)
    sizes = sizes.at[1:1 + 2 * twos:2].set(donor - passed).at[2:2 + 2 * twos:2].set(taker + passed)
    return sizes[jax.random.permutation(jax.random.fold_in(rng, 2), number_of)]


def scatter_about(stream_key, extent, deviation, most, cuts=(), dtype=jnp.bfloat16):
    result = jax.random.normal(stream_key, extent, jnp.float32) * deviation
    if len(cuts) > 0:
        result = level_of(stream_key, extent, cuts, -0.22, 0.18) * result
    return jnp.clip(result, min=-most, max=most).astype(dtype)


def setup_inputs(seed: int = 0) -> dict:
    seeds = jax.random.split(jax.random.key(seed), 19)
    return {
        "inputs": scatter_about(seeds[0], (ROWS, L, D), 1.0, 6.0, ((0, 16), (1, 2))),
        "segments": jax.vmap(lambda own: jnp.searchsorted(jnp.cumsum(ragged_sizes(own, CROPS, L, SEG_MOST, 0)), jnp.arange(L), side="right"))(jax.random.split(seeds[1], ROWS)).reshape((ROWS, L)).astype(jnp.int32),
        "positions": touch_ends(jax.random.randint(seeds[2], (ROWS, L), 0, POS), jax.random.fold_in(seeds[2], 1), 0, POS - 1).astype(jnp.int32),
        "pos_table": scatter_about(seeds[3], (POS, D), 0.5, 3.0),
        "ln1_gain": jnp.clip(1.0 + 0.1 * jax.random.normal(seeds[4], (D,), jnp.float32), 0.5, 1.5),
        "ln1_shift": scatter_about(seeds[5], (D,), 0.3, 1.5, (), jnp.float32),
        "qkv_weight": scatter_about(seeds[6], (D, 3 * D), D ** -0.5, 0.21875),
        "query_bias": scatter_about(seeds[7], (D,), 0.3, 1.5, (), jnp.float32),
        "value_bias": scatter_about(seeds[8], (D,), 0.3, 1.5, (), jnp.float32),
        "out_weight": scatter_about(seeds[9], (D, D), (D // 32) ** -0.5, 1.25),
        "out_bias": scatter_about(seeds[10], (D,), 0.3, 1.5, (), jnp.float32),
        "ln2_gain": jnp.clip(1.0 + 0.1 * jax.random.normal(seeds[11], (D,), jnp.float32), 0.5, 1.5),
        "ln2_shift": scatter_about(seeds[12], (D,), 0.3, 1.5, (), jnp.float32),
        "fc1_weight": scatter_about(seeds[13], (D, FF), D ** -0.5, 0.21875),
        "fc1_bias": scatter_about(seeds[14], (FF,), 0.3, 1.5, (), jnp.float32),
        "fc2_weight": scatter_about(seeds[15], (FF, D), FF ** -0.5, 0.109375),
        "fc2_bias": scatter_about(seeds[16], (D,), 0.3, 1.5, (), jnp.float32),
        "cotangent": scatter_about(seeds[17], (ROWS, L, D), 1.0, 6.0, ((0, 16), (1, 2))),
    }


@jax.custom_vjp
def low(v):
    return lax.optimization_barrier(v.astype(jnp.bfloat16)).astype(jnp.float32)

@jax.custom_vjp
def low_back(v):
    return v

def low_keep(v):
    return (low(v), None)

def low_pass(kept, grad):
    return (grad,)

def back_keep(v):
    return (v, None)

def back_low(kept, grad):
    return (low(grad),)
low.defvjp(low_keep, low_pass)
low_back.defvjp(back_keep, back_low)

def layer_norm(hidden, gain, shift):
    mean = lax.optimization_barrier(jnp.mean(hidden, -1, keepdims=True))
    centred = hidden - mean
    variance = lax.optimization_barrier(jnp.mean(centred * centred, -1, keepdims=True))
    return centred * lax.rsqrt(variance + 1e-06) * gain + shift

def forward(params, inputs, segments, positions):
    table, gain_one, shift_one, w_qkv, bias_query, bias_value, w_out, bias_out, gain_two, shift_two, w_first, bias_first, w_second, bias_second = params
    rows, length, width = inputs.shape
    highest = lax.Precision.HIGHEST
    hidden0 = inputs + table[positions]
    normed1 = low(layer_norm(hidden0, gain_one, shift_one))
    joined_bias = jnp.concatenate([bias_query, jnp.zeros_like(bias_query), bias_value])
    joined = jnp.dot(normed1, w_qkv, precision=highest) + joined_bias
    joined = low_back(low(joined))
    query = joined[..., :width].reshape(rows, length, H, HD)
    keys = joined[..., width:2 * width].reshape(rows, length, H, HD)
    values = joined[..., 2 * width:].reshape(rows, length, H, HD)
    scores = jnp.einsum('rqhd,rkhd->rhqk', query, keys, precision=highest) * 0.125
    same = segments[:, None, :, None] == segments[:, None, None, :]
    scores = low_back(jnp.where(same, scores, -1000000000.0))
    top = lax.optimization_barrier(jnp.max(scores, -1, keepdims=True))
    log_total = top + jnp.log(lax.optimization_barrier(jnp.sum(jnp.exp(scores - top), -1, keepdims=True)))
    probs = low(jnp.exp(scores - log_total))
    attended = jnp.einsum('rhqk,rkhd->rqhd', probs, values, precision=highest).reshape(rows, length, width)
    attended = low_back(low(attended))
    branch = low_back(jnp.dot(attended, w_out, precision=highest) + bias_out)
    hidden1 = hidden0 + branch
    normed2 = low(layer_norm(hidden1, gain_two, shift_two))
    pre_act = low_back(jnp.dot(normed2, w_first, precision=highest) + bias_first)
    activated = low(jax.nn.gelu(pre_act, approximate=False))
    mixed = low_back(jnp.dot(activated, w_second, precision=highest) + bias_second)
    return hidden1 + mixed

def reference(inputs, segments, positions, pos_table, ln1_gain, ln1_shift, qkv_weight, query_bias, value_bias, out_weight, out_bias, ln2_gain, ln2_shift, fc1_weight, fc1_bias, fc2_weight, fc2_bias, cotangent):
    params = tuple((p.astype(jnp.float32) for p in (pos_table, ln1_gain, ln1_shift, qkv_weight, query_bias, value_bias, out_weight, out_bias, ln2_gain, ln2_shift, fc1_weight, fc1_bias, fc2_weight, fc2_bias)))
    group_rows = min(4, max(1, 4096 // L))
    while ROWS % group_rows != 0:
        group_rows = group_rows - 1
    count = ROWS // group_rows
    stacked_in = inputs.astype(jnp.float32).reshape(count, group_rows, L, D)
    stacked_cot = cotangent.astype(jnp.float32).reshape(count, group_rows, L, D)
    stacked_seg = segments.reshape(count, group_rows, L)
    stacked_pos = positions.reshape(count, group_rows, L)

    def step(totals, item):
        group_in, group_cot, group_seg, group_pos = item

        def local(params_now, inputs_now):
            return forward(params_now, inputs_now, group_seg, group_pos)
        output, pullback = jax.vjp(local, params, group_in)
        grad_params, grad_inputs = pullback(group_cot)
        totals = jax.tree.map(lambda a, b: a + b, totals, grad_params)
        return (totals, (output.astype(jnp.bfloat16), grad_inputs.astype(jnp.bfloat16)))
    start = jax.tree.map(jnp.zeros_like, params)
    totals, (outputs, grads_in) = lax.scan(step, start, (stacked_in, stacked_cot, stacked_seg, stacked_pos))
    return (outputs.reshape(ROWS, L, D), grads_in.reshape(ROWS, L, D), totals[0], totals[1], totals[2], totals[3], totals[4], totals[5], totals[6], totals[7], totals[8], totals[9], totals[10], totals[11], totals[12], totals[13])
```

```python
import functools

import jax
import jax.numpy as jnp
import numpy as np
from jax import lax
from jax.experimental import pallas as pl
from jax.experimental.pallas import tpu as pltpu
from jax.sharding import PartitionSpec as P

HD = 64
SEG_MOST = 196
EPS = 1e-06
inv_root_two = 0.7071067811865476
inv_root_two_pi = 0.3989422804014327
BF = jnp.bfloat16
F32 = jnp.float32
MIB = 1 << 20


def dot_nn(a, b):
    return jnp.dot(a, b, preferred_element_type=F32)


def dot_nt(a, b):
    return lax.dot_general(a, b, (((1,), (1,)), ((), ())), preferred_element_type=F32)


def dot_tn(a, b):
    return lax.dot_general(a, b, (((0,), (0,)), ((), ())), preferred_element_type=F32)


def normalise(hidden):
    mean = jnp.mean(hidden, -1, keepdims=True)
    centred = hidden - mean
    inv = lax.rsqrt(jnp.mean(centred * centred, -1, keepdims=True) + EPS)
    return centred * inv, inv


def norm_back(grad, normal, inv, gain):
    scaled = grad * gain
    centre = jnp.mean(scaled, -1, keepdims=True)
    along = jnp.mean(scaled * normal, -1, keepdims=True)
    return inv * (scaled - centre - normal * along)


def column_sum(v):
    return jnp.sum(v, axis=0, keepdims=True)


def params(vmem):
    return pltpu.CompilerParams(vmem_limit_bytes=vmem * MIB)


def cost(flops, bytes_accessed, trans=0):
    return pl.CostEstimate(
        flops=int(flops), bytes_accessed=int(bytes_accessed), transcendentals=int(trans)
    )


def whole(shape):
    return pl.BlockSpec(shape, lambda *_: (0,) * len(shape))


def embed_kernel(x_ref, seg_ref, pos_ref, table_ref, gain_ref, shift_ref, h0_ref, n1_ref):
    half, width = x_ref.shape
    places = table_ref.shape[0]
    hot = (lax.broadcasted_iota(jnp.int32, (places, half), 0) == pos_ref[...]).astype(F32).astype(BF)
    hidden0 = x_ref[...].astype(F32) + dot_tn(hot, table_ref[...])
    h0_ref[...] = hidden0
    normal, _ = normalise(hidden0)
    n1_ref[:, :width] = (normal * gain_ref[...] + shift_ref[...]).astype(BF)
    seg_hot = (lax.broadcasted_iota(jnp.int32, (8, half), 0) == seg_ref[...]).astype(F32).astype(BF)
    eye = (
        lax.broadcasted_iota(jnp.int32, (8, 128), 0) == lax.broadcasted_iota(jnp.int32, (8, 128), 1)
    ).astype(F32).astype(BF)
    n1_ref[:, width:] = dot_tn(seg_hot, eye).astype(BF)


def embed(x, seg, pos, table, gain, shift):
    half, width = x.shape
    return pl.pallas_call(
        embed_kernel,
        out_shape=(
            jax.ShapeDtypeStruct((half, width), F32),
            jax.ShapeDtypeStruct((half, width + 128), BF),
        ),
        compiler_params=params(24),
        cost_estimate=cost(2 * half * width * 256, half * width * 8),
        name="embed",
    )(x, seg, pos, table, gain, shift)


def qkv_kernel(n1_ref, w_ref, qb_ref, vb_ref, out_ref):
    j = pl.program_id(0)
    width = qb_ref.shape[1]
    product = dot_nn(n1_ref[:, :width], w_ref[...])

    @pl.when(j == 0)
    def _():
        out_ref[0] = ((product + qb_ref[...]).astype(BF).astype(F32) * 0.125).astype(BF)

    @pl.when(j == 1)
    def _():
        out_ref[0] = product.astype(BF)

    @pl.when(j == 2)
    def _():
        out_ref[0] = (product + vb_ref[...]).astype(BF)


def qkv_own(n1, w, qb, vb):
    half = n1.shape[0]
    width = w.shape[0]
    return pl.pallas_call(
        qkv_kernel,
        grid=(3,),
        in_specs=[
            whole(n1.shape),
            pl.BlockSpec((width, width), lambda j: (0, j)),
            whole(qb.shape),
            whole(vb.shape),
        ],
        out_specs=pl.BlockSpec((1, half, width), lambda j: (j, 0, 0)),
        out_shape=jax.ShapeDtypeStruct((3, half, width), BF),
        compiler_params=params(24),
        cost_estimate=cost(6 * half * width * width, 6 * width * width + 8 * half * width),
        name="qkv_own",
    )(n1, w, qb, vb)


def lanes_of(shape, head):
    return (lax.broadcasted_iota(jnp.int32, shape, 1) % 128 < HD) == (head % 2 == 0)


def attend_kernel(
    blk_ref, q_ref, k_ref, v_ref, wk_ref, wv_ref, vb_ref, hot_ref, n1o_ref,
    att_ref, p_ref, kh_ref, vh_ref, bias_ref, kcat_ref, vcat_ref,
):
    half = q_ref.shape[1]
    halo = kh_ref.shape[0]
    width = wk_ref.shape[0]
    group = q_ref.shape[2]
    start = pl.multiple_of(blk_ref[0] * (half - halo), 16)

    @pl.when(pl.program_id(0) == 0)
    def _():
        hot = hot_ref[...]
        bias_ref[:, :half] = (dot_nt(hot, hot) - 1.0) * 1e9
        bias_ref[:, half:] = (dot_nt(hot, n1o_ref[pl.ds(start, halo), width:]) - 1.0) * 1e9

    n1h = n1o_ref[pl.ds(start, halo), :width]
    kh = dot_nn(n1h, wk_ref[...]).astype(BF)
    vh = (dot_nn(n1h, wv_ref[...]) + vb_ref[...]).astype(BF)
    kh_ref[...] = kh
    vh_ref[...] = vh
    kcat_ref[:half, :] = k_ref[0]
    kcat_ref[half:, :] = kh
    vcat_ref[:half, :] = v_ref[0]
    vcat_ref[half:, :] = vh
    for pair in range(group // 128):
        cols = slice(pair * 128, pair * 128 + 128)
        q = q_ref[0, :, cols]
        keys = kcat_ref[:, cols]
        values = vcat_ref[:, cols]
        outs = []
        for head in range(2):
            q_one = jnp.where(lanes_of(q.shape, head), q, jnp.zeros_like(q))
            scores = dot_nt(q_one, keys) + bias_ref[...]
            top = jnp.max(scores, -1, keepdims=True)
            weight = jnp.exp(scores - top)
            probs = (weight * (1.0 / jnp.sum(weight, -1, keepdims=True))).astype(BF)
            p_ref[2 * pair + head] = probs
            outs.append(dot_nn(probs, values))
        att_ref[:, cols] = jnp.where(lanes_of(outs[0].shape, 0), outs[0], outs[1]).astype(BF)


def attend(blk, qkv, w, vb, n1, n1o, halo):
    _, half, width = qkv.shape
    group = 256
    steps = width // group
    heads = width // HD
    keys = half + halo
    return pl.pallas_call(
        attend_kernel,
        grid_spec=pltpu.PrefetchScalarGridSpec(
            num_scalar_prefetch=1,
            grid=(steps,),
            in_specs=[
                pl.BlockSpec((1, half, group), lambda g, b: (0, 0, g)),
                pl.BlockSpec((1, half, group), lambda g, b: (1, 0, g)),
                pl.BlockSpec((1, half, group), lambda g, b: (2, 0, g)),
                pl.BlockSpec((width, group), lambda g, b: (0, steps + g)),
                pl.BlockSpec((width, group), lambda g, b: (0, 2 * steps + g)),
                pl.BlockSpec((1, group), lambda g, b: (0, g)),
                pl.BlockSpec((half, 128), lambda g, b: (0, width // 128)),
                whole(n1o.shape),
            ],
            out_specs=[
                pl.BlockSpec((half, group), lambda g, b: (0, g)),
                pl.BlockSpec((group // HD, half, keys), lambda g, b: (g, 0, 0)),
                pl.BlockSpec((halo, group), lambda g, b: (0, g)),
                pl.BlockSpec((halo, group), lambda g, b: (0, g)),
            ],
            scratch_shapes=[
                pltpu.VMEM((half, keys), F32),
                pltpu.VMEM((keys, group), BF),
                pltpu.VMEM((keys, group), BF),
            ],
        ),
        out_shape=(
            jax.ShapeDtypeStruct((half, width), BF),
            jax.ShapeDtypeStruct((heads, half, keys), BF),
            jax.ShapeDtypeStruct((halo, width), BF),
            jax.ShapeDtypeStruct((halo, width), BF),
        ),
        compiler_params=params(40),
        cost_estimate=cost(16 * half * keys * width, 2 * heads * half * keys, heads * half * keys),
        name="attend",
    )(blk, qkv, qkv, qkv, w, w, vb, n1, n1o)


def feed_kernel(
    blk_ref, att_ref, h0_ref, cot_ref, wo_ref, bo_ref, g2_ref, s2_ref, w1_ref, b1_ref, w2_ref, b2_ref,
    res_ref, h1_ref, n2_ref, act_ref, gs_ref, gk_ref, gn_ref, b1g_ref, mixed_ref,
):
    i = pl.program_id(0)
    steps = pl.num_programs(0)

    @pl.when(i == 0)
    def _():
        hidden1 = h0_ref[...] + dot_nn(att_ref[...], wo_ref[...]) + bo_ref[...]
        h1_ref[...] = hidden1
        normal, _ = normalise(hidden1)
        n2_ref[...] = (normal * g2_ref[...] + s2_ref[...]).astype(BF)
        mixed_ref[...] = hidden1 + b2_ref[...]
        gn_ref[...] = jnp.zeros_like(gn_ref)

    pre = dot_nn(n2_ref[...], w1_ref[...]) + b1_ref[...]
    grad_act = dot_nt(cot_ref[...], w2_ref[...])
    cdf = 0.5 + 0.5 * lax.erf(pre * inv_root_two)
    act = (pre * cdf).astype(BF)
    act_ref[...] = act
    slope = cdf + pre * jnp.exp(-0.5 * pre * pre) * inv_root_two_pi
    grad32 = grad_act * slope
    grad_pre = grad32.astype(BF)
    b1g_ref[...] = column_sum(grad_pre.astype(F32))

    @pl.when(i < steps // 2)
    def _():
        gs_ref[...] = grad_pre

    @pl.when(i >= steps // 2)
    def _():
        gk_ref[...] = grad_pre

    mixed_ref[...] += dot_nn(act, w2_ref[...])
    gn_ref[...] += dot_nt(grad_pre, w1_ref[...])

    @pl.when(i == steps - 1)
    def _():
        res_ref[...] = mixed_ref[...].astype(BF)


def feed(blk, att, h0, cot, wo, bo, g2, s2, w1, b1, w2, b2):
    half, width = h0.shape
    hidden = w1.shape[1]
    chunk = 384
    steps = hidden // chunk
    per = steps // 2

    def place(i, b):
        return jnp.where(i < per, (1 - b[0]) * per + i, b[0] * per + i - per)

    return pl.pallas_call(
        feed_kernel,
        grid_spec=pltpu.PrefetchScalarGridSpec(
            num_scalar_prefetch=1,
            grid=(steps,),
            in_specs=[
                whole(att.shape),
                whole(h0.shape),
                whole(cot.shape),
                whole(wo.shape),
                whole(bo.shape),
                whole(g2.shape),
                whole(s2.shape),
                pl.BlockSpec((width, chunk), lambda i, b: (0, place(i, b))),
                pl.BlockSpec((1, chunk), lambda i, b: (0, place(i, b))),
                pl.BlockSpec((chunk, width), lambda i, b: (place(i, b), 0)),
                whole(b2.shape),
            ],
            out_specs=[
                whole((half, width)),
                whole((half, width)),
                whole((half, width)),
                pl.BlockSpec((half, chunk), lambda i, b: (0, place(i, b))),
                pl.BlockSpec((half, chunk), lambda i, b: (0, jnp.minimum(i, per - 1))),
                pl.BlockSpec((half, chunk), lambda i, b: (0, jnp.maximum(i - per, 0))),
                whole((half, width)),
                pl.BlockSpec((1, chunk), lambda i, b: (0, place(i, b))),
            ],
            scratch_shapes=[pltpu.VMEM((half, width), F32)],
        ),
        out_shape=(
            jax.ShapeDtypeStruct((half, width), BF),
            jax.ShapeDtypeStruct((half, width), F32),
            jax.ShapeDtypeStruct((half, width), BF),
            jax.ShapeDtypeStruct((half, hidden), BF),
            jax.ShapeDtypeStruct((half, hidden // 2), BF),
            jax.ShapeDtypeStruct((half, hidden // 2), BF),
            jax.ShapeDtypeStruct((half, width), F32),
            jax.ShapeDtypeStruct((1, hidden), F32),
        ),
        compiler_params=params(40),
        cost_estimate=cost(
            8 * half * width * hidden + 2 * half * width * width, 4 * width * hidden, 2 * half * hidden
        ),
        name="feed",
    )(blk, att, h0, cot, wo, bo, g2, s2, w1, b1, w2, b2)


def mid_kernel(gn_ref, h1_ref, cot_ref, wo_ref, g2_ref, gh_ref, gb_ref, ga_ref, sums_ref):
    normal, inv = normalise(h1_ref[...])
    grad = gn_ref[...]
    cot = cot_ref[...].astype(F32)
    sums_ref[0:1, :] = column_sum(grad * normal)
    sums_ref[1:2, :] = column_sum(grad)
    grad_hidden1 = cot + norm_back(grad, normal, inv, g2_ref[...])
    gh_ref[...] = grad_hidden1
    branch = grad_hidden1.astype(BF)
    gb_ref[...] = branch
    sums_ref[2:3, :] = column_sum(branch.astype(F32))
    sums_ref[3:4, :] = column_sum(cot)
    ga_ref[...] = dot_nt(branch, wo_ref[...]).astype(BF)


def mid(gn, h1, cot, wo, g2):
    half, width = h1.shape
    return pl.pallas_call(
        mid_kernel,
        out_shape=(
            jax.ShapeDtypeStruct((half, width), F32),
            jax.ShapeDtypeStruct((half, width), BF),
            jax.ShapeDtypeStruct((half, width), BF),
            jax.ShapeDtypeStruct((4, width), F32),
        ),
        compiler_params=params(24),
        cost_estimate=cost(2 * half * width * width, 14 * half * width),
        name="mid",
    )(gn, h1, cot, wo, g2)


class Plan:
    def __init__(self, ndp):
        self.groups = min(16, ndp)
        self.bits = self.groups.bit_length() - 1
        self.rest = ndp // self.groups
        order = list(range(self.bits))
        swapped = order[:2][::-1] + order[2:]
        self.orders = (order, swapped)
        self.index = tuple(self.rank(o) for o in self.orders)

    def rank(self, order):
        table = []
        for p in range(self.groups):
            code = 0
            for bit in order:
                code = 2 * code + ((p >> bit) & 1)
            table.append(self.groups - 1 - code)
        return table


def store_block(refs, plan, piece, p, row, block):
    place = plan.index[piece][p]
    first = plan.groups // 2
    ref = refs[2 * piece + (place >= first)]
    ref[place % first, row : row + block.shape[0], :] = block


def feed_weights_kernel(
    plan, own_ref, act_ref, acto_ref, cot_ref, coto_ref, n2_ref, n2o_ref, g_ref, go_ref, *rest
):
    outs, acc_ref = rest[:4], rest[4]
    i = pl.program_id(0)
    own = own_ref[0]
    chunk = act_ref.shape[1]
    steps = pl.num_programs(0)
    per = plan.groups // steps
    rows2 = chunk // per
    rows1 = n2_ref.shape[1] // plan.groups
    acc_ref[...] = dot_tn(act_ref[...], cot_ref[...]) + dot_tn(acto_ref[...], coto_ref[...])
    for step in range(steps):

        @pl.when(i == step)
        def _():
            for low in range(per):
                source = pl.multiple_of(((own % per) ^ low) * rows2, 16)
                for piece in range(2):
                    block = acc_ref[pl.ds(source + piece * (rows2 // 2), rows2 // 2), :]
                    store_block(outs, plan, piece, step * per + low, 0, block.astype(BF))

    acc_ref[...] = dot_tn(n2_ref[...], g_ref[...]) + dot_tn(n2o_ref[...], go_ref[...])
    for step in range(steps):

        @pl.when(i == step)
        def _():
            for p in range(plan.groups):
                source = pl.multiple_of((own ^ p) * rows1, 16)
                block = acc_ref[pl.ds(source, rows1), :]
                store_block(
                    outs, plan, step // (steps // 2), p,
                    rows2 // 2 + (step % (steps // 2)) * rows1, block.astype(BF),
                )


def feed_weights(plan, own, blk, act, acto, cot, coto, n2, n2o, g, go):
    half, hidden = act.shape
    width = n2.shape[1]
    cols = width // 2
    steps = 4
    chunk = hidden // steps
    per = plan.groups // steps
    rows = hidden // plan.groups // 2 + (steps // 2) * (width // plan.groups)
    part = jax.ShapeDtypeStruct((plan.groups // 2, rows, cols), BF)

    def place(i, o, b):
        return (0, (o[0] // per) ^ i)

    return pl.pallas_call(
        functools.partial(wrap_two, feed_weights_kernel, plan),
        grid_spec=pltpu.PrefetchScalarGridSpec(
            num_scalar_prefetch=2,
            grid=(steps,),
            in_specs=[
                pl.BlockSpec((half, chunk), place),
                pl.BlockSpec((half, chunk), place),
                pl.BlockSpec((half, cols), lambda i, o, b: (0, b[0])),
                pl.BlockSpec((half, cols), lambda i, o, b: (0, b[0])),
                whole(n2.shape),
                whole(n2o.shape),
                pl.BlockSpec((half, cols), lambda i, o, b: (0, i)),
                pl.BlockSpec((half, cols), lambda i, o, b: (0, i)),
            ],
            out_specs=[whole(part.shape)] * 4,
            scratch_shapes=[pltpu.VMEM((width, cols), F32)],
        ),
        out_shape=(part,) * 4,
        compiler_params=params(40),
        cost_estimate=cost(4 * half * width * hidden, 2 * width * hidden + 8 * half * hidden),
        name="feed_weights",
    )(own, blk, act, acto, cot, coto, n2, n2o, g, go)


def wrap_two(kernel, plan, own_ref, blk_ref, *refs):
    kernel(plan, own_ref, *refs)


def attend_back_kernel(
    blk_ref, q_ref, k_ref, v_ref, kh_ref, vh_ref, p_ref, ga_ref, d_ref, dh_ref, kcat_ref, vcat_ref
):
    half = q_ref.shape[1]
    kcat_ref[:half, :] = k_ref[0]
    kcat_ref[half:, :] = kh_ref[...]
    vcat_ref[:half, :] = v_ref[0]
    vcat_ref[half:, :] = vh_ref[...]
    q = q_ref[0]
    grad = ga_ref[...]
    dqs, dks, dvs = [], [], []
    for head in range(2):
        grad_one = jnp.where(lanes_of(grad.shape, head), grad, jnp.zeros_like(grad))
        grad_probs = dot_nt(grad_one, vcat_ref[...])
        probs = p_ref[head].astype(F32)
        row = jnp.sum(probs * grad_probs, -1, keepdims=True)
        grad_scores = (probs * (grad_probs - row)).astype(BF)
        dqs.append(dot_nn(grad_scores, kcat_ref[...]))
        dks.append(dot_tn(grad_scores, q))
        dvs.append(dot_tn(p_ref[head], grad))
    first = lanes_of(dqs[0].shape, 0)
    d_ref[0] = (jnp.where(first, dqs[0], dqs[1]) * 0.125).astype(BF)
    first = lanes_of(dks[0].shape, 0)
    dk = jnp.where(first, dks[0], dks[1]).astype(BF)
    dv = jnp.where(first, dvs[0], dvs[1]).astype(BF)
    d_ref[1] = dk[:half]
    d_ref[2] = dv[:half]
    dh_ref[0] = dk[half:]
    dh_ref[1] = dv[half:]


def attend_back(side, qkv, kh, vh, probs, ga):
    _, half, width = qkv.shape
    halo = kh.shape[0]
    keys = half + halo
    steps = width // 256

    def col(i, s):
        return s[0] * steps + i

    return pl.pallas_call(
        attend_back_kernel,
        grid_spec=pltpu.PrefetchScalarGridSpec(
            num_scalar_prefetch=1,
            grid=(steps,),
            in_specs=[
                pl.BlockSpec((1, half, 128), lambda i, s: (0, 0, col(i, s))),
                pl.BlockSpec((1, half, 128), lambda i, s: (1, 0, col(i, s))),
                pl.BlockSpec((1, half, 128), lambda i, s: (2, 0, col(i, s))),
                pl.BlockSpec((halo, 128), lambda i, s: (0, col(i, s))),
                pl.BlockSpec((halo, 128), lambda i, s: (0, col(i, s))),
                pl.BlockSpec((2, half, keys), lambda i, s: (col(i, s), 0, 0)),
                pl.BlockSpec((half, 128), lambda i, s: (0, col(i, s))),
            ],
            out_specs=[
                pl.BlockSpec((3, half, 128), lambda i, s: (0, 0, i)),
                pl.BlockSpec((2, halo, 128), lambda i, s: (0, 0, i)),
            ],
            scratch_shapes=[pltpu.VMEM((keys, 128), BF), pltpu.VMEM((keys, 128), BF)],
        ),
        out_shape=(
            jax.ShapeDtypeStruct((3, half, width // 2), BF),
            jax.ShapeDtypeStruct((2, halo, width // 2), BF),
        ),
        compiler_params=params(40),
        cost_estimate=cost(16 * half * keys * width, half * keys * width // HD),
        name="attend_back",
    )(side, qkv, qkv, qkv, kh, vh, probs, ga)


def add_rows(ref, which, start, halo, extra):
    part = ref[which, pl.ds(start, halo), :].astype(F32) + extra.astype(F32)
    ref[which, pl.ds(start, halo), :] = part.astype(BF)


def attend_weights_kernel(
    plan, own_ref, blk_ref, n1_ref, n1o_ref, d_ref, dh_ref, do_ref, dho_ref, att_ref, atto_ref,
    gb_ref, gbo_ref, *rest
):
    outs, acc_ref, mine_ref, other_ref = rest[:4], rest[4], rest[5], rest[6]
    half = n1_ref.shape[0]
    halo = dh_ref.shape[1]
    width = att_ref.shape[1]
    own = own_ref[0]
    rows = width // plan.groups
    start = pl.multiple_of((1 - blk_ref[0]) * (half - halo), 16)
    start_other = pl.multiple_of(blk_ref[0] * (half - halo), 16)
    mine_ref[...] = d_ref[...]
    other_ref[...] = do_ref[...]
    for which in range(2):
        add_rows(mine_ref, 1 + which, start, halo, dho_ref[which])
        add_rows(other_ref, 1 + which, start_other, halo, dh_ref[which])
    for panel in range(4):
        if panel < 3:
            acc_ref[...] = dot_tn(n1_ref[:, :width], mine_ref[panel]) + dot_tn(
                n1o_ref[:, :width], other_ref[panel]
            )
        else:
            acc_ref[...] = dot_tn(att_ref[...], gb_ref[...]) + dot_tn(atto_ref[...], gbo_ref[...])
        for p in range(plan.groups):
            source = pl.multiple_of((own ^ p) * rows, 16)
            block = acc_ref[pl.ds(source, rows), :]
            store_block(outs, plan, panel // 2, p, (panel % 2) * rows, block.astype(BF))


def attend_weights(plan, own, blk, n1, n1o, d, dh, do, dho, att, atto, gb, gbo):
    half, width = att.shape
    cols = width // 2
    rows = 2 * (width // plan.groups)
    part = jax.ShapeDtypeStruct((plan.groups // 2, rows, cols), BF)
    return pl.pallas_call(
        functools.partial(attend_weights_kernel, plan),
        grid_spec=pltpu.PrefetchScalarGridSpec(
            num_scalar_prefetch=2,
            grid=(1,),
            in_specs=[
                whole(n1.shape),
                whole(n1o.shape),
                whole(d.shape),
                whole(dh.shape),
                whole(do.shape),
                whole(dho.shape),
                whole(att.shape),
                whole(atto.shape),
                pl.BlockSpec((half, cols), lambda i, o, b: (0, b[0])),
                pl.BlockSpec((half, cols), lambda i, o, b: (0, b[0])),
            ],
            out_specs=[whole(part.shape)] * 4,
            scratch_shapes=[
                pltpu.VMEM((width, cols), F32),
                pltpu.VMEM(d.shape, BF),
                pltpu.VMEM(do.shape, BF),
            ],
        ),
        out_shape=(part,) * 4,
        compiler_params=params(40),
        cost_estimate=cost(8 * half * width * width, 4 * width * width + 24 * half * width),
        name="attend_weights",
    )(own, blk, n1, n1o, d, dh, do, dho, att, atto, gb, gbo)


def front_back_kernel(
    blk_ref, da_ref, db_ref, ha_ref, hb_ref, w_ref, h0_ref, gh_ref, g1_ref, pos_ref, sums_ref, b1_ref,
    gx_ref, small_ref, acc_ref,
):
    half, width = h0_ref.shape
    halo = ha_ref.shape[1]
    cols = width // 2
    places = small_ref.shape[0] - 12
    start = pl.multiple_of((1 - blk_ref[0]) * (half - halo), 16)
    acc_ref[0] = da_ref[...]
    acc_ref[1] = db_ref[...]
    for which in range(2):
        add_rows(acc_ref.at[0], 1 + which, start, halo, ha_ref[which])
        add_rows(acc_ref.at[1], 1 + which, start, halo, hb_ref[which])
    total = jnp.zeros((half, width), F32)
    for which in range(3):
        for side, ref in enumerate((acc_ref.at[0], acc_ref.at[1])):
            at = which * width + side * cols
            panel = ref[which]
            total = total + dot_nt(panel, w_ref[:, at : at + cols])
            if which == 0:
                small_ref[places + 2 : places + 3, side * cols : side * cols + cols] = column_sum(panel.astype(F32))
            if which == 2:
                small_ref[places + 3 : places + 4, side * cols : side * cols + cols] = column_sum(panel.astype(F32))
    normal, inv = normalise(h0_ref[...])
    small_ref[places : places + 1, :] = column_sum(total * normal)
    small_ref[places + 1 : places + 2, :] = column_sum(total)
    grad = (gh_ref[...] + norm_back(total, normal, inv, g1_ref[...])).astype(BF)
    gx_ref[...] = grad
    hot = (lax.broadcasted_iota(jnp.int32, (places, half), 0) == pos_ref[...]).astype(F32).astype(BF)
    small_ref[:places, :] = dot_nn(hot, grad)
    small_ref[places + 4 : places + 8, :] = sums_ref[...]
    for k in range(4):
        small_ref[places + 8 + k : places + 9 + k, :] = b1_ref[:, k * width : (k + 1) * width]


def front_back(blk, da, db, ha, hb, w, h0, gh, g1, pos, sums, b1, places):
    half, width = h0.shape
    return pl.pallas_call(
        front_back_kernel,
        grid_spec=pltpu.PrefetchScalarGridSpec(
            num_scalar_prefetch=1,
            grid=(1,),
            in_specs=[whole(a.shape) for a in (da, db, ha, hb, w, h0, gh, g1, pos, sums, b1)],
            out_specs=[whole((half, width)), whole((places + 12, width))],
            scratch_shapes=[pltpu.VMEM((2,) + da.shape, BF)],
        ),
        out_shape=(
            jax.ShapeDtypeStruct((half, width), BF),
            jax.ShapeDtypeStruct((places + 12, width), F32),
        ),
        compiler_params=params(40),
        cost_estimate=cost(6 * half * width * width, 6 * width * width + 20 * half * width),
        name="front_back",
    )(blk, da, db, ha, hb, w, h0, gh, g1, pos, sums, b1)


def swap(v):
    return lax.ppermute(v, "blk", [(0, 1), (1, 0)])


def across(v, ndp, flip):
    return lax.ppermute(v, "dp", [(i, i ^ flip) for i in range(ndp)])


def wide(v):
    return v.astype(F32)


def scatter_pairs(plan, ndp, parts):
    later = []
    for piece in range(2):
        sent, kept = parts[2 * piece], parts[2 * piece + 1]
        terms = [kept, across(sent, ndp, plan.rest << plan.orders[piece][0])]
        later.append(terms)
    count = plan.groups // 2
    if plan.bits > 1:
        for piece in range(2):
            h = count // 2
            out = sum(wide(t[:h]) for t in later[piece]).astype(BF)
            got = across(out, ndp, plan.rest << plan.orders[piece][1])
            later[piece] = [t[h:] for t in later[piece]] + [got]
        count //= 2
    for bit in range(2, plan.bits):
        h = count // 2
        if bit == 2:
            merged = [jnp.stack([sum(wide(t) for t in later[piece]) for piece in range(2)])]
        out = sum(wide(t[:, :h]) for t in merged).astype(BF)
        got = across(out, ndp, plan.rest << bit)
        merged = [t[:, h:] for t in merged] + [got]
        count //= 2
    if plan.bits <= 2:
        merged = [jnp.stack([sum(wide(t) for t in later[piece]) for piece in range(2)])]
    return sum(wide(t) for t in merged)[:, 0]


def rest_of(plan, ndp, value, rows):
    if plan.rest == 1:
        return value
    groups = [[g * plan.rest + i for i in range(plan.rest)] for g in range(plan.groups)]
    value = lax.psum(value, "dp", axis_index_groups=groups)
    return lax.dynamic_slice_in_dim(value, (lax.axis_index("dp") % plan.rest) * rows, rows, axis=value.ndim - 2)


def total_small(small, ndp):
    rows, width = small.shape
    blk = lax.axis_index("blk")
    cols = width // 2
    small = small.astype(BF)
    mine = lax.dynamic_slice_in_dim(small, blk * cols, cols, axis=1)
    other = swap(lax.dynamic_slice_in_dim(small, (1 - blk) * cols, cols, axis=1))
    total = wide(mine) + wide(other)
    for bit in reversed(range(ndp.bit_length() - 1)):
        low = total.astype(BF)
        total = wide(low) + wide(across(low, ndp, 1 << bit))
    low = total.astype(BF)
    both = swap(low)
    return wide(jnp.where(blk == 0, jnp.concatenate([low, both], 1), jnp.concatenate([both, low], 1)))


def per_device(
    ndp, inputs, segments, positions, pos_table, ln1_gain, ln1_shift, qkv_weight, query_bias,
    value_bias, out_weight, out_bias, ln2_gain, ln2_shift, fc1_weight, fc1_bias, fc2_weight,
    fc2_bias, cotangent,
):
    plan = Plan(ndp)
    x, cot = inputs[0], cotangent[0]
    half, width = x.shape
    hidden = fc1_weight.shape[1]
    places = pos_table.shape[0]
    halo = next(h for h in range(SEG_MOST - 1, half + 1) if (half + h) % 128 == 0 and (half - h) % 16 == 0)
    blk = lax.axis_index("blk")
    dp = lax.axis_index("dp")
    blk1 = blk.astype(jnp.int32).reshape(1)
    own1 = (dp // plan.rest).astype(jnp.int32).reshape(1)
    row = lambda v: v.reshape(1, -1)

    cot_other = swap(cot)
    hidden0, n1 = embed(x, segments, positions, pos_table, row(ln1_gain), row(ln1_shift))
    n1_other = swap(n1)
    qkv = qkv_own(n1, qkv_weight, row(query_bias), row(value_bias))
    att, probs, kh, vh = attend(blk1, qkv, qkv_weight, row(value_bias), n1, n1_other, halo)
    att_other = swap(att)
    result, hidden1, n2, act, grad_send, grad_keep, gn2, b1_grad = feed(
        blk1, att, hidden0, cot, out_weight, row(out_bias), row(ln2_gain), row(ln2_shift),
        fc1_weight, row(fc1_bias), fc2_weight, row(fc2_bias),
    )
    act_other, n2_other, grad_other = swap(act), swap(n2), swap(grad_send)
    gh1, gb, ga, sums = mid(gn2, hidden1, cot, out_weight, row(ln2_gain))
    gb_other = swap(gb)
    first = feed_weights(plan, own1, blk1, act, act_other, cot, cot_other, n2, n2_other, grad_keep, grad_other)
    summed_first = scatter_pairs(plan, ndp, first)

    d_send, h_send = attend_back(1 - blk1, qkv, kh, vh, probs, ga)
    d_other, h_other = swap(d_send), swap(h_send)
    d_keep, h_keep = attend_back(blk1, qkv, kh, vh, probs, ga)
    h_late = swap(h_keep)
    second = attend_weights(
        plan, own1, blk1, n1, n1_other, d_keep, h_keep, d_other, h_other, att, att_other, gb, gb_other
    )
    summed_second = scatter_pairs(plan, ndp, second)
    is0 = blk == 0
    pick = lambda a, b: jnp.where(is0, a, b)
    grad_x, small = front_back(
        blk1, pick(d_keep, d_send), pick(d_send, d_keep), pick(h_other, h_late), pick(h_late, h_other),
        qkv_weight, hidden0, gh1, row(ln1_gain), positions, sums, b1_grad, places,
    )
    small = total_small(small, ndp)

    rg = width // ndp
    r1 = width // plan.groups
    cols = width // 2
    r2 = hidden // plan.groups // 2

    def finish(value, lead):
        parts = value.reshape(lead, 2, -1, cols)
        mine = lax.dynamic_index_in_dim(parts, blk, 1, keepdims=False)
        got = swap(lax.dynamic_index_in_dim(parts, 1 - blk, 1, keepdims=False))
        return pick(jnp.stack([mine, got], 2), jnp.stack([got, mine], 2))

    fc2_block = rest_of(plan, ndp, summed_first[:, :r2].reshape(1, 2 * r2, cols), hidden // ndp)
    fc1_block = rest_of(plan, ndp, summed_first[:, r2:].reshape(4, r1, cols), rg)
    att_block = rest_of(plan, ndp, summed_second.reshape(4, r1, cols), rg)
    fc2_grad = finish(fc2_block, 1).reshape(-1, width)
    fc1_own = finish(fc1_block, 4)
    fc1_grad = fc1_own.transpose(1, 2, 0, 3).reshape(rg // 2, hidden)
    att_own = finish(att_block, 4).reshape(4, rg // 2, width)
    qkv_grad = att_own[:3].transpose(1, 0, 2).reshape(rg // 2, 3 * width)
    out_grad = att_own[3]
    vec = lambda k: small[places + k]
    return (
        result[None], grad_x[None], small[:places], vec(0), vec(1), qkv_grad, vec(2), vec(3), out_grad,
        vec(6), vec(4), vec(5), fc1_grad, small[places + 8 :].reshape(-1), fc2_grad, vec(7),
    )


def solution(mesh):
    split = P("dp", "blk", None)
    ids = P("dp", "blk")
    both = P(("dp", "blk"), None)
    none = P()
    return jax.shard_map(
        functools.partial(per_device, mesh.shape["dp"]),
        mesh=mesh,
        in_specs=(split, ids, ids) + (none,) * 14 + (split,),
        out_specs=(
            split, split, none, none, none, both, none, none, both, none, none, none, both, none, both, none,
        ),
        check_vma=False,
    )
```

```python
import functools

import jax
import jax.numpy as jnp
from jax import lax
from jax.experimental import pallas as pl
from jax.experimental.pallas import tpu as pltpu
from jax.sharding import PartitionSpec as P

HD = 64
SEG_MOST = 196
EPS = 1e-06
inv_root_two = 0.7071067811865476
inv_root_two_pi = 0.3989422804014327
BF = jnp.bfloat16
F32 = jnp.float32
MIB = 1 << 20


def dot_nn(a, b):
    return jnp.dot(a, b, preferred_element_type=F32)


def dot_nt(a, b):
    return lax.dot_general(a, b, (((1,), (1,)), ((), ())), preferred_element_type=F32)


def dot_tn(a, b):
    return lax.dot_general(a, b, (((0,), (0,)), ((), ())), preferred_element_type=F32)


def normalise(hidden):
    mean = jnp.mean(hidden, -1, keepdims=True)
    centred = hidden - mean
    inv = lax.rsqrt(jnp.mean(centred * centred, -1, keepdims=True) + EPS)
    return centred * inv, inv


def norm_back(grad, normal, inv, gain):
    scaled = grad * gain
    centre = jnp.mean(scaled, -1, keepdims=True)
    along = jnp.mean(scaled * normal, -1, keepdims=True)
    return inv * (scaled - centre - normal * along)


def line(ref):
    return ref[...].reshape(1, -1)


def column_sum(v):
    return jnp.sum(v, axis=0, keepdims=True)


def params(vmem):
    return pltpu.CompilerParams(vmem_limit_bytes=vmem * MIB)


def cost(flops, bytes_accessed, trans=0):
    return pl.CostEstimate(
        flops=int(flops) // 100, bytes_accessed=int(bytes_accessed) // 100, transcendentals=int(trans) // 100
    )


def whole(shape):
    return pl.BlockSpec(shape, lambda *_: (0,) * len(shape))


def embed_kernel(x_ref, seg_ref, pos_ref, table_ref, gain_ref, shift_ref, h0_ref, n1_ref):
    half, width = x_ref.shape
    places = table_ref.shape[0]
    hot = (lax.broadcasted_iota(jnp.int32, (places, half), 0) == pos_ref[...]).astype(F32).astype(BF)
    hidden0 = x_ref[...].astype(F32) + dot_tn(hot, table_ref[...])
    h0_ref[...] = hidden0
    normal, _ = normalise(hidden0)
    n1_ref[:, :width] = (normal * line(gain_ref) + line(shift_ref)).astype(BF)
    seg_hot = (lax.broadcasted_iota(jnp.int32, (8, half), 0) == seg_ref[...]).astype(F32).astype(BF)
    eye = (
        lax.broadcasted_iota(jnp.int32, (8, 128), 0) == lax.broadcasted_iota(jnp.int32, (8, 128), 1)
    ).astype(F32).astype(BF)
    n1_ref[:, width:] = dot_tn(seg_hot, eye).astype(BF)


def embed(x, seg, pos, table, gain, shift):
    half, width = x.shape
    return pl.pallas_call(
        embed_kernel,
        out_shape=(
            jax.ShapeDtypeStruct((half, width), F32),
            jax.ShapeDtypeStruct((half, width + 128), BF),
        ),
        compiler_params=params(24),
        cost_estimate=cost(2 * half * width * 256, half * width * 8),
        name="embed",
    )(x, seg, pos, table, gain, shift)


def qkv_kernel(n1_ref, w_ref, qb_ref, vb_ref, out_ref):
    j = pl.program_id(0)
    width = qb_ref.shape[0]
    product = dot_nn(n1_ref[:, :width], w_ref[...])

    @pl.when(j == 0)
    def _():
        out_ref[0] = ((product + line(qb_ref)).astype(BF).astype(F32) * 0.125).astype(BF)

    @pl.when(j == 1)
    def _():
        out_ref[0] = product.astype(BF)

    @pl.when(j == 2)
    def _():
        out_ref[0] = (product + line(vb_ref)).astype(BF)


def qkv_own(n1, w, qb, vb):
    half = n1.shape[0]
    width = w.shape[0]
    return pl.pallas_call(
        qkv_kernel,
        grid=(3,),
        in_specs=[
            whole(n1.shape),
            pl.BlockSpec((width, width), lambda j: (0, j)),
            whole(qb.shape),
            whole(vb.shape),
        ],
        out_specs=pl.BlockSpec((1, half, width), lambda j: (j, 0, 0)),
        out_shape=jax.ShapeDtypeStruct((3, half, width), BF),
        compiler_params=params(24),
        cost_estimate=cost(6 * half * width * width, 6 * width * width + 8 * half * width),
        name="qkv_own",
    )(n1, w, qb, vb)


def lanes_of(shape, head):
    return (lax.broadcasted_iota(jnp.int32, shape, 1) % 128 < HD) == (head % 2 == 0)


def attend_kernel(
    blk_ref, q_ref, k_ref, v_ref, wk_ref, wv_ref, vb_ref, hot_ref, n1o_ref,
    att_ref, p_ref, kh_ref, vh_ref, bias_ref, kcat_ref, vcat_ref,
):
    half = q_ref.shape[1]
    halo = kh_ref.shape[0]
    width = wk_ref.shape[0]
    group = q_ref.shape[2]
    start = pl.multiple_of(blk_ref[0] * (half - halo), 16)

    @pl.when(pl.program_id(0) == 0)
    def _():
        hot = hot_ref[...]
        bias_ref[:, :half] = (dot_nt(hot, hot) - 1.0) * 1e9
        bias_ref[:, half:] = (dot_nt(hot, n1o_ref[pl.ds(start, halo), width:]) - 1.0) * 1e9

    n1h = n1o_ref[pl.ds(start, halo), :width]
    kh = dot_nn(n1h, wk_ref[...]).astype(BF)
    vh = (dot_nn(n1h, wv_ref[...]) + line(vb_ref)).astype(BF)
    kh_ref[...] = kh
    vh_ref[...] = vh
    kcat_ref[:half, :] = k_ref[0]
    kcat_ref[half:, :] = kh
    vcat_ref[:half, :] = v_ref[0]
    vcat_ref[half:, :] = vh
    for pair in range(group // 128):
        cols = slice(pair * 128, pair * 128 + 128)
        q = q_ref[0, :, cols]
        keys = kcat_ref[:, cols]
        values = vcat_ref[:, cols]
        outs = []
        for head in range(2):
            q_one = jnp.where(lanes_of(q.shape, head), q, jnp.zeros_like(q))
            scores = dot_nt(q_one, keys) + bias_ref[...]
            top = jnp.max(scores, -1, keepdims=True)
            weight = jnp.exp(scores - top)
            probs = (weight * (1.0 / jnp.sum(weight, -1, keepdims=True))).astype(BF)
            p_ref[2 * pair + head] = probs
            outs.append(dot_nn(probs, values))
        att_ref[:, cols] = jnp.where(lanes_of(outs[0].shape, 0), outs[0], outs[1]).astype(BF)


def attend(blk, qkv, w, vb, n1, n1o, halo):
    _, half, width = qkv.shape
    group = 256
    steps = width // group
    heads = width // HD
    keys = half + halo
    return pl.pallas_call(
        attend_kernel,
        grid_spec=pltpu.PrefetchScalarGridSpec(
            num_scalar_prefetch=1,
            grid=(steps,),
            in_specs=[
                pl.BlockSpec((1, half, group), lambda g, b: (0, 0, g)),
                pl.BlockSpec((1, half, group), lambda g, b: (1, 0, g)),
                pl.BlockSpec((1, half, group), lambda g, b: (2, 0, g)),
                pl.BlockSpec((width, group), lambda g, b: (0, steps + g)),
                pl.BlockSpec((width, group), lambda g, b: (0, 2 * steps + g)),
                pl.BlockSpec((group,), lambda g, b: (g,)),
                pl.BlockSpec((half, 128), lambda g, b: (0, width // 128)),
                whole(n1o.shape),
            ],
            out_specs=[
                pl.BlockSpec((half, group), lambda g, b: (0, g)),
                pl.BlockSpec((group // HD, half, keys), lambda g, b: (g, 0, 0)),
                pl.BlockSpec((halo, group), lambda g, b: (0, g)),
                pl.BlockSpec((halo, group), lambda g, b: (0, g)),
            ],
            scratch_shapes=[
                pltpu.VMEM((half, keys), F32),
                pltpu.VMEM((keys, group), BF),
                pltpu.VMEM((keys, group), BF),
            ],
        ),
        out_shape=(
            jax.ShapeDtypeStruct((half, width), BF),
            jax.ShapeDtypeStruct((heads, half, keys), BF),
            jax.ShapeDtypeStruct((halo, width), BF),
            jax.ShapeDtypeStruct((halo, width), BF),
        ),
        compiler_params=params(40),
        cost_estimate=cost(16 * half * keys * width, 2 * heads * half * keys, heads * half * keys),
        name="attend",
    )(blk, qkv, qkv, qkv, w, w, vb, n1, n1o)


def feed_kernel(
    blk_ref, att_ref, h0_ref, cot_ref, wo_ref, bo_ref, g2_ref, s2_ref, w1_ref, b1_ref, w2_ref,
    h1_ref, n2_ref, act_ref, gs_ref, gk_ref, b1g_ref,
):
    i = pl.program_id(0)
    steps = pl.num_programs(0)

    @pl.when(i == 0)
    def _():
        hidden1 = h0_ref[...] + dot_nn(att_ref[...], wo_ref[...]) + line(bo_ref)
        h1_ref[...] = hidden1
        normal, _ = normalise(hidden1)
        n2_ref[...] = (normal * line(g2_ref) + line(s2_ref)).astype(BF)

    pre = dot_nn(n2_ref[...], w1_ref[...]) + line(b1_ref)
    grad_act = dot_nt(cot_ref[...], w2_ref[...])
    cdf = 0.5 + 0.5 * lax.erf(pre * inv_root_two)
    act_ref[...] = (pre * cdf).astype(BF)
    slope = cdf + pre * jnp.exp(-0.5 * pre * pre) * inv_root_two_pi
    grad_pre = (grad_act * slope).astype(BF)
    b1g_ref[...] = column_sum(grad_pre.astype(F32))

    @pl.when(i < steps // 2)
    def _():
        gs_ref[...] = grad_pre

    @pl.when(i >= steps // 2)
    def _():
        gk_ref[...] = grad_pre


def relative(i, b, per):
    return jnp.where(i < per, (1 - b[0]) * per + i, b[0] * per + i - per)


def feed(blk, att, h0, cot, wo, bo, g2, s2, w1, b1, w2):
    half, width = h0.shape
    hidden = w1.shape[1]
    chunk = 512
    steps = hidden // chunk
    per = steps // 2
    return pl.pallas_call(
        feed_kernel,
        grid_spec=pltpu.PrefetchScalarGridSpec(
            num_scalar_prefetch=1,
            grid=(steps,),
            in_specs=[
                whole(att.shape),
                whole(h0.shape),
                whole(cot.shape),
                whole(wo.shape),
                whole(bo.shape),
                whole(g2.shape),
                whole(s2.shape),
                pl.BlockSpec((width, chunk), lambda i, b: (0, relative(i, b, per))),
                pl.BlockSpec((chunk,), lambda i, b: (relative(i, b, per),)),
                pl.BlockSpec((chunk, width), lambda i, b: (relative(i, b, per), 0)),
            ],
            out_specs=[
                whole((half, width)),
                whole((half, width)),
                pl.BlockSpec((half, chunk), lambda i, b: (0, relative(i, b, per))),
                pl.BlockSpec((half, chunk), lambda i, b: (0, jnp.minimum(i, per - 1))),
                pl.BlockSpec((half, chunk), lambda i, b: (0, jnp.maximum(i - per, 0))),
                pl.BlockSpec((1, chunk), lambda i, b: (0, relative(i, b, per))),
            ],
        ),
        out_shape=(
            jax.ShapeDtypeStruct((half, width), F32),
            jax.ShapeDtypeStruct((half, width), BF),
            jax.ShapeDtypeStruct((half, hidden), BF),
            jax.ShapeDtypeStruct((half, hidden // 2), BF),
            jax.ShapeDtypeStruct((half, hidden // 2), BF),
            jax.ShapeDtypeStruct((1, hidden), F32),
        ),
        compiler_params=params(40),
        cost_estimate=cost(
            4 * half * width * hidden + 2 * half * width * width, 4 * width * hidden, 2 * half * hidden
        ),
        name="feed",
    )(blk, att, h0, cot, wo, bo, g2, s2, w1, b1, w2)


def feed_back_kernel(
    blk_ref, act_ref, gs_ref, gk_ref, w1_ref, w2_ref, h1_ref, b2_ref, cot_ref, wo_ref, g2_ref,
    res_ref, gh_ref, gb_ref, ga_ref, sums_ref, mixed_ref, gn_ref,
):
    i = pl.program_id(0)
    steps = pl.num_programs(0)
    grad_pre = jnp.where(i < steps // 2, gs_ref[...], gk_ref[...])
    mixed = dot_nn(act_ref[...], w2_ref[...])
    grad = dot_nt(grad_pre, w1_ref[...])

    @pl.when(i == 0)
    def _():
        mixed_ref[...] = mixed
        gn_ref[...] = grad

    @pl.when(i > 0)
    def _():
        mixed_ref[...] += mixed
        gn_ref[...] += grad

    @pl.when(i == steps - 1)
    def _():
        res_ref[...] = (h1_ref[...] + mixed_ref[...] + line(b2_ref)).astype(BF)
        normal, inv = normalise(h1_ref[...])
        total = gn_ref[...]
        cot = cot_ref[...].astype(F32)
        sums_ref[0:1, :] = column_sum(total * normal)
        sums_ref[1:2, :] = column_sum(total)
        grad_hidden1 = cot + norm_back(total, normal, inv, line(g2_ref))
        gh_ref[...] = grad_hidden1
        branch = grad_hidden1.astype(BF)
        gb_ref[...] = branch
        sums_ref[2:3, :] = column_sum(branch.astype(F32))
        sums_ref[3:4, :] = column_sum(cot)
        ga_ref[...] = dot_nt(branch, wo_ref[...]).astype(BF)


def feed_back(blk, act, gs, gk, w1, w2, h1, b2, cot, wo, g2):
    half, width = h1.shape
    hidden = w1.shape[1]
    chunk = 768
    steps = hidden // chunk
    per = steps // 2
    return pl.pallas_call(
        feed_back_kernel,
        grid_spec=pltpu.PrefetchScalarGridSpec(
            num_scalar_prefetch=1,
            grid=(steps,),
            in_specs=[
                pl.BlockSpec((half, chunk), lambda i, b: (0, relative(i, b, per))),
                pl.BlockSpec((half, chunk), lambda i, b: (0, jnp.minimum(i, per - 1))),
                pl.BlockSpec((half, chunk), lambda i, b: (0, jnp.maximum(i - per, 0))),
                pl.BlockSpec((width, chunk), lambda i, b: (0, relative(i, b, per))),
                pl.BlockSpec((chunk, width), lambda i, b: (relative(i, b, per), 0)),
                whole(h1.shape),
                whole(b2.shape),
                whole(cot.shape),
                whole(wo.shape),
                whole(g2.shape),
            ],
            out_specs=[
                whole((half, width)),
                whole((half, width)),
                whole((half, width)),
                whole((half, width)),
                whole((4, width)),
            ],
            scratch_shapes=[pltpu.VMEM((half, width), F32), pltpu.VMEM((half, width), F32)],
        ),
        out_shape=(
            jax.ShapeDtypeStruct((half, width), BF),
            jax.ShapeDtypeStruct((half, width), F32),
            jax.ShapeDtypeStruct((half, width), BF),
            jax.ShapeDtypeStruct((half, width), BF),
            jax.ShapeDtypeStruct((4, width), F32),
        ),
        compiler_params=params(40),
        cost_estimate=cost(4 * half * width * hidden + 2 * half * width * width, 4 * width * hidden),
        name="feed_back",
    )(blk, act, gs, gk, w1, w2, h1, b2, cot, wo, g2)


class Plan:
    def __init__(self, ndp):
        self.groups = min(16, ndp)
        self.bits = self.groups.bit_length() - 1
        self.rest = ndp // self.groups
        order = list(range(self.bits))
        swapped = order[:2][::-1] + order[2:]
        self.orders = (order, swapped)
        self.index = tuple(self.rank(o) for o in self.orders)

    def rank(self, order):
        table = []
        for p in range(self.groups):
            code = 0
            for bit in order:
                code = 2 * code + ((p >> bit) & 1)
            table.append(self.groups - 1 - code)
        return table


def store_block(refs, plan, piece, p, row, block):
    place = plan.index[piece][p]
    first = plan.groups // 2
    refs[place >= first][place % first, row : row + block.shape[0], :] = block


def second_weights_kernel(plan, own_ref, blk_ref, act_ref, acto_ref, cot_ref, coto_ref, *rest):
    outs, acc_ref = rest[:2], rest[2]
    i = pl.program_id(0)
    own = own_ref[0]
    chunk = act_ref.shape[1]
    steps = pl.num_programs(0)
    per = plan.groups // steps
    rows = chunk // per
    acc_ref[...] = dot_tn(act_ref[...], cot_ref[...]) + dot_tn(acto_ref[...], coto_ref[...])
    for step in range(steps):

        @pl.when(i == step)
        def _():
            for low in range(per):
                source = pl.multiple_of(((own % per) ^ low) * rows, 16)
                block = acc_ref[pl.ds(source, rows), :]
                store_block(outs, plan, 0, step * per + low, 0, block.astype(BF))


def second_weights(plan, own, blk, act, acto, cot, coto):
    half, hidden = act.shape
    width = cot.shape[1]
    cols = width // 2
    steps = 4
    chunk = hidden // steps
    per = plan.groups // steps
    part = jax.ShapeDtypeStruct((plan.groups // 2, hidden // plan.groups, cols), BF)

    def place(i, o, b):
        return (0, (o[0] // per) ^ i)

    return pl.pallas_call(
        functools.partial(second_weights_kernel, plan),
        grid_spec=pltpu.PrefetchScalarGridSpec(
            num_scalar_prefetch=2,
            grid=(steps,),
            in_specs=[
                pl.BlockSpec((half, chunk), place),
                pl.BlockSpec((half, chunk), place),
                pl.BlockSpec((half, cols), lambda i, o, b: (0, b[0])),
                pl.BlockSpec((half, cols), lambda i, o, b: (0, b[0])),
            ],
            out_specs=[whole(part.shape)] * 2,
            scratch_shapes=[pltpu.VMEM((chunk, cols), F32)],
        ),
        out_shape=(part,) * 2,
        compiler_params=params(40),
        cost_estimate=cost(2 * half * width * hidden, width * hidden + 4 * half * hidden),
        name="second_weights",
    )(own, blk, act, acto, cot, coto)


def first_weights_kernel(plan, own_ref, n2_ref, n2o_ref, g_ref, go_ref, *rest):
    outs, acc_ref = rest[:2], rest[2]
    i = pl.program_id(0)
    own = own_ref[0]
    rows = n2_ref.shape[1] // plan.groups
    acc_ref[...] = dot_tn(n2_ref[...], g_ref[...]) + dot_tn(n2o_ref[...], go_ref[...])
    for step in range(4):

        @pl.when(i == step)
        def _():
            for p in range(plan.groups):
                source = pl.multiple_of((own ^ p) * rows, 16)
                block = acc_ref[pl.ds(source, rows), :]
                store_block(outs, plan, 1, p, step * rows, block.astype(BF))


def first_weights(plan, own, n2, n2o, g, go):
    half, width = n2.shape
    cols = width // 2
    steps = g.shape[1] // cols
    part = jax.ShapeDtypeStruct((plan.groups // 2, steps * (width // plan.groups), cols), BF)
    return pl.pallas_call(
        functools.partial(first_weights_kernel, plan),
        grid_spec=pltpu.PrefetchScalarGridSpec(
            num_scalar_prefetch=1,
            grid=(steps,),
            in_specs=[
                whole(n2.shape),
                whole(n2o.shape),
                pl.BlockSpec((half, cols), lambda i, o: (0, i)),
                pl.BlockSpec((half, cols), lambda i, o: (0, i)),
            ],
            out_specs=[whole(part.shape)] * 2,
            scratch_shapes=[pltpu.VMEM((width, cols), F32)],
        ),
        out_shape=(part,) * 2,
        compiler_params=params(40),
        cost_estimate=cost(4 * half * width * g.shape[1], 2 * width * g.shape[1] + 4 * half * g.shape[1]),
        name="first_weights",
    )(own, n2, n2o, g, go)


def attend_back_kernel(
    blk_ref, q_ref, k_ref, v_ref, kh_ref, vh_ref, p_ref, ga_ref, after_ref, d_ref, dh_ref, kcat_ref, vcat_ref
):
    half = q_ref.shape[1]
    kcat_ref[:half, :] = k_ref[0]
    kcat_ref[half:, :] = kh_ref[...]
    vcat_ref[:half, :] = v_ref[0]
    vcat_ref[half:, :] = vh_ref[...]
    q = q_ref[0]
    grad = ga_ref[...]
    dqs, dks, dvs = [], [], []
    for head in range(2):
        grad_one = jnp.where(lanes_of(grad.shape, head), grad, jnp.zeros_like(grad))
        grad_probs = dot_nt(grad_one, vcat_ref[...])
        probs = p_ref[head].astype(F32)
        row = jnp.sum(probs * grad_probs, -1, keepdims=True)
        grad_scores = (probs * (grad_probs - row)).astype(BF)
        dqs.append(dot_nn(grad_scores, kcat_ref[...]))
        dks.append(dot_tn(grad_scores, q))
        dvs.append(dot_tn(p_ref[head], grad))
    first = lanes_of(dqs[0].shape, 0)
    d_ref[0] = (jnp.where(first, dqs[0], dqs[1]) * 0.125).astype(BF)
    first = lanes_of(dks[0].shape, 0)
    dk = jnp.where(first, dks[0], dks[1]).astype(BF)
    dv = jnp.where(first, dvs[0], dvs[1]).astype(BF)
    d_ref[1] = dk[:half]
    d_ref[2] = dv[:half]
    dh_ref[0] = dk[half:]
    dh_ref[1] = dv[half:]


def attend_back(side, qkv, kh, vh, probs, ga, after):
    _, half, width = qkv.shape
    halo = kh.shape[0]
    keys = half + halo
    steps = width // 256

    def col(i, s):
        return s[0] * steps + i

    return pl.pallas_call(
        attend_back_kernel,
        grid_spec=pltpu.PrefetchScalarGridSpec(
            num_scalar_prefetch=1,
            grid=(steps,),
            in_specs=[
                pl.BlockSpec((1, half, 128), lambda i, s: (0, 0, col(i, s))),
                pl.BlockSpec((1, half, 128), lambda i, s: (1, 0, col(i, s))),
                pl.BlockSpec((1, half, 128), lambda i, s: (2, 0, col(i, s))),
                pl.BlockSpec((halo, 128), lambda i, s: (0, col(i, s))),
                pl.BlockSpec((halo, 128), lambda i, s: (0, col(i, s))),
                pl.BlockSpec((2, half, keys), lambda i, s: (col(i, s), 0, 0)),
                pl.BlockSpec((half, 128), lambda i, s: (0, col(i, s))),
                pl.BlockSpec(memory_space=pl.ANY),
            ],
            out_specs=[
                pl.BlockSpec((3, half, 128), lambda i, s: (0, 0, i)),
                pl.BlockSpec((2, halo, 128), lambda i, s: (0, 0, i)),
            ],
            scratch_shapes=[pltpu.VMEM((keys, 128), BF), pltpu.VMEM((keys, 128), BF)],
        ),
        out_shape=(
            jax.ShapeDtypeStruct((3, half, width // 2), BF),
            jax.ShapeDtypeStruct((2, halo, width // 2), BF),
        ),
        compiler_params=params(40),
        cost_estimate=cost(16 * half * keys * width, half * keys * width // HD),
        name="attend_back",
    )(side, qkv, qkv, qkv, kh, vh, probs, ga, after)


def add_rows(ref, which, start, halo, extra):
    part = ref[which, pl.ds(start, halo), :].astype(F32) + extra.astype(F32)
    ref[which, pl.ds(start, halo), :] = part.astype(BF)


def attend_weights_kernel(
    plan, own_ref, blk_ref, n1_ref, n1o_ref, d_ref, dh_ref, do_ref, dho_ref, att_ref, atto_ref,
    gb_ref, gbo_ref, *rest
):
    outs, acc_ref, mine_ref, other_ref = rest[:4], rest[4], rest[5], rest[6]
    half = n1_ref.shape[0]
    halo = dh_ref.shape[1]
    width = att_ref.shape[1]
    own = own_ref[0]
    rows = width // plan.groups
    start = pl.multiple_of((1 - blk_ref[0]) * (half - halo), 16)
    start_other = pl.multiple_of(blk_ref[0] * (half - halo), 16)
    mine_ref[...] = d_ref[...]
    other_ref[...] = do_ref[...]
    for which in range(2):
        add_rows(mine_ref, 1 + which, start, halo, dho_ref[which])
        add_rows(other_ref, 1 + which, start_other, halo, dh_ref[which])
    for panel in range(4):
        if panel < 3:
            acc_ref[...] = dot_tn(n1_ref[:, :width], mine_ref[panel]) + dot_tn(
                n1o_ref[:, :width], other_ref[panel]
            )
        else:
            acc_ref[...] = dot_tn(att_ref[...], gb_ref[...]) + dot_tn(atto_ref[...], gbo_ref[...])
        for p in range(plan.groups):
            source = pl.multiple_of((own ^ p) * rows, 16)
            block = acc_ref[pl.ds(source, rows), :]
            store_block(outs[2 * (panel // 2) :][:2], plan, panel // 2, p, (panel % 2) * rows, block.astype(BF))


def attend_weights(plan, own, blk, n1, n1o, d, dh, do, dho, att, atto, gb, gbo):
    half, width = att.shape
    cols = width // 2
    rows = 2 * (width // plan.groups)
    part = jax.ShapeDtypeStruct((plan.groups // 2, rows, cols), BF)
    return pl.pallas_call(
        functools.partial(attend_weights_kernel, plan),
        grid_spec=pltpu.PrefetchScalarGridSpec(
            num_scalar_prefetch=2,
            grid=(1,),
            in_specs=[
                whole(n1.shape),
                whole(n1o.shape),
                whole(d.shape),
                whole(dh.shape),
                whole(do.shape),
                whole(dho.shape),
                whole(att.shape),
                whole(atto.shape),
                pl.BlockSpec((half, cols), lambda i, o, b: (0, b[0])),
                pl.BlockSpec((half, cols), lambda i, o, b: (0, b[0])),
            ],
            out_specs=[whole(part.shape)] * 4,
            scratch_shapes=[
                pltpu.VMEM((width, cols), F32),
                pltpu.VMEM(d.shape, BF),
                pltpu.VMEM(do.shape, BF),
            ],
        ),
        out_shape=(part,) * 4,
        compiler_params=params(40),
        cost_estimate=cost(8 * half * width * width, 4 * width * width + 24 * half * width),
        name="attend_weights",
    )(own, blk, n1, n1o, d, dh, do, dho, att, atto, gb, gbo)


def front_back_kernel(
    blk_ref, da_ref, db_ref, ha_ref, hb_ref, w_ref, h0_ref, gh_ref, g1_ref, pos_ref, sums_ref, b1_ref,
    *rest,
):
    gx_ref, small_ref, acc_ref = rest[-3:]
    half, width = h0_ref.shape
    halo = ha_ref.shape[1]
    cols = width // 2
    places = small_ref.shape[0] - 12
    start = pl.multiple_of((1 - blk_ref[0]) * (half - halo), 16)
    acc_ref[0] = da_ref[...]
    acc_ref[1] = db_ref[...]
    for which in range(2):
        add_rows(acc_ref.at[0], 1 + which, start, halo, ha_ref[which])
        add_rows(acc_ref.at[1], 1 + which, start, halo, hb_ref[which])
    total = jnp.zeros((half, width), F32)
    for which in range(3):
        for side, ref in enumerate((acc_ref.at[0], acc_ref.at[1])):
            actual = blk_ref[0] if side == 0 else 1 - blk_ref[0]
            at = pl.multiple_of(actual * cols, 128)
            panel = ref[which]
            total = total + dot_nt(panel, w_ref[:, pl.ds(pl.multiple_of(which * width + at, 128), cols)])
            if which != 1:
                k = places + (2 if which == 0 else 3)
                small_ref[k : k + 1, pl.ds(at, cols)] = column_sum(panel.astype(F32))
    normal, inv = normalise(h0_ref[...])
    small_ref[places : places + 1, :] = column_sum(total * normal)
    small_ref[places + 1 : places + 2, :] = column_sum(total)
    grad = (gh_ref[...] + norm_back(total, normal, inv, line(g1_ref))).astype(BF)
    gx_ref[...] = grad
    hot = (lax.broadcasted_iota(jnp.int32, (places, half), 0) == pos_ref[...]).astype(F32).astype(BF)
    small_ref[:places, :] = dot_nn(hot, grad)
    small_ref[places + 4 : places + 8, :] = sums_ref[...]
    for k in range(4):
        small_ref[places + 8 + k : places + 9 + k, :] = b1_ref[:, k * width : (k + 1) * width]


def front_back(blk, da, db, ha, hb, w, h0, gh, g1, pos, sums, b1, places, after):
    half, width = h0.shape
    return pl.pallas_call(
        front_back_kernel,
        grid_spec=pltpu.PrefetchScalarGridSpec(
            num_scalar_prefetch=1,
            grid=(1,),
            in_specs=[whole(a.shape) for a in (da, db, ha, hb, w, h0, gh, g1, pos, sums, b1)]
            + [pl.BlockSpec(memory_space=pl.ANY)] * len(after),
            out_specs=[whole((half, width)), whole((places + 12, width))],
            scratch_shapes=[pltpu.VMEM((2,) + da.shape, BF)],
        ),
        out_shape=(
            jax.ShapeDtypeStruct((half, width), BF),
            jax.ShapeDtypeStruct((places + 12, width), F32),
        ),
        compiler_params=params(40),
        cost_estimate=cost(6 * half * width * width, 6 * width * width + 20 * half * width),
        name="front_back",
    )(blk, da, db, ha, hb, w, h0, gh, g1, pos, sums, b1, *after)


def swap(v):
    return lax.ppermute(v, "blk", [(0, 1), (1, 0)])


def across(v, ndp, flip):
    return lax.ppermute(v, "dp", [(i, i ^ flip) for i in range(ndp)])


def wide(v):
    return v.astype(F32)


def open_pairs(plan, ndp, parts):
    return [[parts[2 * k + 1], across(parts[2 * k], ndp, plan.rest << plan.orders[k][0])] for k in range(2)]


def next_pairs(plan, ndp, later):
    if plan.bits < 2:
        return later, ()
    h = plan.groups // 4
    outs = tuple(sum(wide(t[:h]) for t in terms).astype(BF) for terms in later)
    gots = [across(outs[k], ndp, plan.rest << plan.orders[k][1]) for k in range(2)]
    return [[t[h:] for t in later[k]] + [gots[k]] for k in range(2)], outs


def close_pairs(plan, ndp, later):
    count = max(1, plan.groups // 4)
    merged = [jnp.stack([sum(wide(t) for t in later[piece]) for piece in range(2)])]
    for bit in range(2, plan.bits):
        h = count // 2
        out = sum(wide(t[:, :h]) for t in merged).astype(BF)
        got = across(out, ndp, plan.rest << bit)
        merged = [t[:, h:] for t in merged] + [got]
        count //= 2
    return sum(wide(t) for t in merged)[:, 0]


def behind(values, *others):
    return lax.optimization_barrier((values, others))[0]


def rest_of(plan, ndp, value, rows):
    if plan.rest == 1:
        return value
    groups = [[g * plan.rest + i for i in range(plan.rest)] for g in range(plan.groups)]
    value = lax.psum(value, "dp", axis_index_groups=groups)
    return lax.dynamic_slice_in_dim(value, (lax.axis_index("dp") % plan.rest) * rows, rows, axis=value.ndim - 2)


def total_small(small, ndp):
    rows, width = small.shape
    blk = lax.axis_index("blk")
    cols = width // 2
    small = small.astype(BF)
    mine = lax.dynamic_slice_in_dim(small, blk * cols, cols, axis=1)
    other = swap(lax.dynamic_slice_in_dim(small, (1 - blk) * cols, cols, axis=1))
    total = wide(mine) + wide(other)
    for bit in reversed(range(ndp.bit_length() - 1)):
        low = total.astype(BF)
        total = wide(low) + wide(across(low, ndp, 1 << bit))
    low = total.astype(BF)
    both = swap(low)
    return wide(jnp.where(blk == 0, jnp.concatenate([low, both], 1), jnp.concatenate([both, low], 1)))


def per_device(
    ndp, inputs, segments, positions, pos_table, ln1_gain, ln1_shift, qkv_weight, query_bias,
    value_bias, out_weight, out_bias, ln2_gain, ln2_shift, fc1_weight, fc1_bias, fc2_weight,
    fc2_bias, cotangent,
):
    plan = Plan(ndp)
    x, cot = inputs[0], cotangent[0]
    half, width = x.shape
    hidden = fc1_weight.shape[1]
    places = pos_table.shape[0]
    halo = next(h for h in range(SEG_MOST - 1, half + 1) if (half + h) % 128 == 0 and (half - h) % 16 == 0)
    blk = lax.axis_index("blk")
    dp = lax.axis_index("dp")
    blk1 = blk.astype(jnp.int32).reshape(1)
    own1 = (dp // plan.rest).astype(jnp.int32).reshape(1)

    cot_other = swap(cot)
    hidden0, n1 = embed(x, segments, positions, pos_table, ln1_gain, ln1_shift)
    n1_other = swap(n1)
    qkv = qkv_own(n1, qkv_weight, query_bias, value_bias)
    att, probs, kh, vh = attend(blk1, qkv, qkv_weight, value_bias, n1, n1_other, halo)
    att_other = swap(att)
    hidden1, n2, act, grad_send, grad_keep, b1_grad = feed(
        blk1, att, hidden0, cot, out_weight, out_bias, ln2_gain, ln2_shift, fc1_weight, fc1_bias, fc2_weight
    )
    grad_other, n2_other, act_other = swap(grad_send), swap(n2), swap(act)
    result, gh1, gb, ga, sums = feed_back(
        blk1, act, grad_send, grad_keep, fc1_weight, fc2_weight, hidden1, fc2_bias, cot, out_weight, ln2_gain
    )
    gb_other = swap(gb)
    fc1_parts = first_weights(plan, own1, n2, n2_other, grad_keep, grad_other)
    fc2_parts = second_weights(plan, own1, blk1, act, act_other, cot, cot_other)
    open_first = open_pairs(plan, ndp, fc2_parts + fc1_parts)
    d_send, h_send = attend_back(1 - blk1, qkv, kh, vh, probs, ga, fc2_parts[0])
    d_other, h_other = swap(d_send), swap(h_send)
    d_keep, h_keep = attend_back(blk1, qkv, kh, vh, probs, ga, d_send)
    h_late = swap(h_keep)
    second = attend_weights(
        plan, own1, blk1, n1, n1_other, d_keep, h_keep, d_other, h_other, att, att_other, gb, gb_other
    )
    kept = behind((open_first[0][0], open_first[1][0]), second[0])
    open_first[0][0], open_first[1][0] = kept
    open_first, outs = next_pairs(plan, ndp, open_first)
    open_second = open_pairs(plan, ndp, behind(tuple(second), *outs))
    pick = lambda a, b: jnp.where(blk == 0, a, b)
    grad_x, small = front_back(
        blk1, d_keep, d_send, h_other, h_late,
        qkv_weight, hidden0, gh1, ln1_gain, positions, sums, b1_grad, places,
        (second[0],) + outs,
    )
    summed_first = close_pairs(plan, ndp, open_first)
    open_second, _ = next_pairs(plan, ndp, open_second)
    summed_second = close_pairs(plan, ndp, open_second)
    small = total_small(small, ndp)

    rg = width // ndp
    r1 = width // plan.groups
    cols = width // 2

    def finish(value, lead):
        parts = value.reshape(lead, 2, -1, cols)
        mine = lax.dynamic_index_in_dim(parts, blk, 1, keepdims=False)
        got = swap(lax.dynamic_index_in_dim(parts, 1 - blk, 1, keepdims=False))
        return pick(jnp.stack([mine, got], 2), jnp.stack([got, mine], 2))

    fc2_block = rest_of(plan, ndp, summed_first[:1], hidden // ndp)
    fc1_block = rest_of(plan, ndp, summed_first[1].reshape(4, r1, cols), rg)
    att_block = rest_of(plan, ndp, summed_second.reshape(4, r1, cols), rg)
    fc2_grad = finish(fc2_block, 1).reshape(-1, width)
    fc1_own = finish(fc1_block, 4)
    fc1_grad = fc1_own.transpose(1, 2, 0, 3).reshape(rg // 2, hidden)
    att_own = finish(att_block, 4).reshape(4, rg // 2, width)
    qkv_grad = att_own[:3].transpose(1, 0, 2).reshape(rg // 2, 3 * width)
    out_grad = att_own[3]
    vec = lambda k: small[places + k]
    return (
        result[None], grad_x[None], small[:places], vec(0), vec(1), qkv_grad, vec(2), vec(3), out_grad,
        vec(6), vec(4), vec(5), fc1_grad, small[places + 8 :].reshape(-1), fc2_grad, vec(7),
    )


def solution(mesh):
    split = P("dp", "blk", None)
    ids = P("dp", "blk")
    both = P(("dp", "blk"), None)
    none = P()
    return jax.shard_map(
        functools.partial(per_device, mesh.shape["dp"]),
        mesh=mesh,
        in_specs=(split, ids, ids) + (none,) * 14 + (split,),
        out_specs=(
            split, split, none, none, none, both, none, none, both, none, none, none, both, none, both, none,
        ),
        check_vma=False,
    )
```

```python
import functools

import jax
import jax.numpy as jnp
from jax import lax
from jax.experimental import pallas as pl
from jax.experimental.pallas import tpu as pltpu
from jax.sharding import PartitionSpec as P

HD = 64
SEG_MOST = 196
EPS = 1e-06
inv_root_two = 0.7071067811865476
inv_root_two_pi = 0.3989422804014327
BF = jnp.bfloat16
F32 = jnp.float32
MIB = 1 << 20


def dot_nn(a, b):
    return jnp.dot(a, b, preferred_element_type=F32)


def dot_nt(a, b):
    return lax.dot_general(a, b, (((1,), (1,)), ((), ())), preferred_element_type=F32)


def dot_tn(a, b):
    return lax.dot_general(a, b, (((0,), (0,)), ((), ())), preferred_element_type=F32)


def normalise(hidden):
    mean = jnp.mean(hidden, -1, keepdims=True)
    centred = hidden - mean
    inv = lax.rsqrt(jnp.mean(centred * centred, -1, keepdims=True) + EPS)
    return centred * inv, inv


def norm_back(grad, normal, inv, gain):
    scaled = grad * gain
    centre = jnp.mean(scaled, -1, keepdims=True)
    along = jnp.mean(scaled * normal, -1, keepdims=True)
    return inv * (scaled - centre - normal * along)


def line(ref):
    return ref[...].reshape(1, -1)


def column_sum(v):
    return jnp.sum(v, axis=0, keepdims=True)


def params(vmem):
    return pltpu.CompilerParams(vmem_limit_bytes=(60 if vmem > 24 else vmem) * MIB)


def cost(flops, bytes_accessed, trans=0):
    return pl.CostEstimate(
        flops=int(flops) // 100, bytes_accessed=int(bytes_accessed) // 100, transcendentals=int(trans) // 100
    )


def whole(shape):
    return pl.BlockSpec(shape, lambda *_: (0,) * len(shape))


def lanes_of(shape, head):
    return (lax.broadcasted_iota(jnp.int32, shape, 1) % 128 < HD) == (head % 2 == 0)


def embedded(x_ref, pos_ref, table_ref):
    half = x_ref.shape[0]
    places = table_ref.shape[0]
    hot = (lax.broadcasted_iota(jnp.int32, (places, half), 0) == pos_ref[...]).astype(F32).astype(BF)
    return x_ref[...].astype(F32) + dot_tn(hot, table_ref[...])


def crop_lanes(seg_ref):
    half = seg_ref.shape[1]
    hot = (lax.broadcasted_iota(jnp.int32, (8, half), 0) == seg_ref[...]).astype(F32).astype(BF)
    eye = lax.broadcasted_iota(jnp.int32, (8, 128), 0) == lax.broadcasted_iota(jnp.int32, (8, 128), 1)
    return dot_tn(hot, eye.astype(F32).astype(BF)).astype(BF)


def front_kernel(
    block,
    blk_ref, x_ref, xo_ref, seg_ref, sego_ref, pos_ref, poso_ref, cot_ref, table_ref,
    g1_ref, s1_ref, qb_ref, vb_ref, bo_ref, g2_ref, s2_ref, b1_ref, b2_ref,
    wqkv_hbm, wo_hbm, w1_hbm, w2_hbm,
    h0_out, n1_out, n1o_out, q_out, k_out, v_out, att_out, p_out, n2_out,
    gs_out, gk_out, as_out, ak_out, res_out, gh_out, gb_out, ga_out, b1g_ref, sums_ref,
    wqkv_ref, wo_ref, w1_ref, w2_ref, h0_ref, n1_ref, n1o_ref, hoto_ref, q_ref, k_ref, v_ref, bias_ref,
    att_ref, p_ref, h1_ref, n2_ref, gp_ref, act_ref, mixed_ref, gn_ref, res_ref, gh_ref, gb_ref, ga_ref,
    in_sem, out_sem, p_sem, late_sem,
):
    step = pl.program_id(0)
    half, width = x_ref.shape
    keys = k_ref.shape[0]
    halo = keys - half
    hidden = w1_ref.shape[1]
    blk = blk_ref[0]
    start = pl.multiple_of(blk * (half - halo), 16)
    loads = [
        pltpu.make_async_copy(src, dst, in_sem.at[k])
        for k, (src, dst) in enumerate(
            ((wqkv_hbm, wqkv_ref), (wo_hbm, wo_ref), (w1_hbm, w1_ref), (w2_hbm, w2_ref))
        )
    ]
    outs = [
        pltpu.make_async_copy(src, dst, out_sem.at[k])
        for k, (src, dst) in enumerate(
            (
                (h0_ref, h0_out), (n1_ref.at[:half], n1_out), (n1o_ref, n1o_out), (q_ref, q_out), (k_ref, k_out),
                (v_ref, v_out), (att_ref, att_out), (n2_ref, n2_out), (res_ref, res_out), (gh_ref, gh_out),
                (gb_ref, gb_out), (ga_ref, ga_out),
            )
        )
    ]

    def p_copy(i, slot):
        return pltpu.make_async_copy(p_ref.at[slot], p_out.at[pl.ds(4 * i, 4)], p_sem.at[slot])

    @pl.when(step == 0)
    def _():
        for load in loads:
            load.start()
        hidden0 = embedded(x_ref, pos_ref, table_ref)
        h0_ref[...] = hidden0
        normal, _ = normalise(hidden0)
        n1_ref[:half, :] = (normal * line(g1_ref) + line(s1_ref)).astype(BF)
        normal, _ = normalise(embedded(xo_ref, poso_ref, table_ref))
        n1o_ref[...] = (normal * line(g1_ref) + line(s1_ref)).astype(BF)
        n1_ref[half:, :] = n1o_ref[pl.ds(start, halo), :]
        hot = crop_lanes(seg_ref)
        hoto_ref[...] = crop_lanes(sego_ref)
        bias_ref[:, :half] = (dot_nt(hot, hot) - 1.0) * 1e9
        bias_ref[:, half:] = (dot_nt(hot, hoto_ref[pl.ds(start, halo), :]) - 1.0) * 1e9
        loads[0].wait()
        q = dot_nn(n1_ref[:half, :], wqkv_ref[:, :width]) + line(qb_ref)
        q_ref[...] = (q.astype(BF).astype(F32) * 0.125).astype(BF)
        k_ref[...] = dot_nn(n1_ref[...], wqkv_ref[:, width : 2 * width]).astype(BF)
        v_ref[...] = (dot_nn(n1_ref[...], wqkv_ref[:, 2 * width :]) + line(vb_ref)).astype(BF)
        for out in outs[:6]:
            out.start()

    @pl.when(step < 3)
    def _():
        slot = step % 2

        @pl.when(step == 2)
        def _():
            p_copy(0, 0).wait()

        for pair in range(2):
            cols = pl.ds(pl.multiple_of(step * 256 + pair * 128, 128), 128)
            q = q_ref[:, cols]
            both = []
            for head in range(2):
                q_one = jnp.where(lanes_of(q.shape, head), q, jnp.zeros_like(q))
                scores = dot_nt(q_one, k_ref[:, cols]) + bias_ref[...]
                top = jnp.max(scores, -1, keepdims=True)
                weight = jnp.exp(scores - top)
                probs = (weight * (1.0 / jnp.sum(weight, -1, keepdims=True))).astype(BF)
                p_ref[slot, 2 * pair + head] = probs
                both.append(dot_nn(probs, v_ref[:, cols]))
            att_ref[:, cols] = jnp.where(lanes_of(both[0].shape, 0), both[0], both[1]).astype(BF)
        p_copy(step, slot).start()

    @pl.when(step == 3)
    def _():
        outs[6].start()
        loads[1].wait()
        hidden1 = h0_ref[...] + dot_nn(att_ref[...], wo_ref[...]) + line(bo_ref)
        h1_ref[...] = hidden1
        normal, _ = normalise(hidden1)
        n2_ref[...] = (normal * line(g2_ref) + line(s2_ref)).astype(BF)
        outs[7].start()
        loads[2].wait()
        loads[3].wait()
        late = []
        chunk = 768
        part = chunk // 2
        for j in range(hidden // chunk):
            at = slice(j * chunk, (j + 1) * chunk)
            pre = dot_nn(n2_ref[...], w1_ref[:, at]) + b1_ref[at].reshape(1, -1)
            grad_act = dot_nt(cot_ref[...], w2_ref[at, :])
            cdf = 0.5 + 0.5 * lax.erf(pre * inv_root_two)
            act = (pre * cdf).astype(BF)
            slope = cdf + pre * jnp.exp(-0.5 * pre * pre) * inv_root_two_pi
            grad_pre = (grad_act * slope).astype(BF)
            b1g_ref[:, at] = column_sum(grad_pre.astype(F32))
            side, sub = divmod(j * chunk, hidden // 2)
            gp_ref[side, :, sub : sub + chunk] = grad_pre
            mine = slice(j * part, (j + 1) * part)
            for c in range(2):
                act_ref[c, :, mine] = jnp.concatenate(
                    [act[:, t : t + block] for t in range(c * block, chunk, 2 * block)], 1
                )
            mixed = dot_nn(act, w2_ref[at, :])
            grad_norm = dot_nt(grad_pre, w1_ref[:, at])
            mixed_ref[...] = mixed if j == 0 else mixed_ref[...] + mixed
            gn_ref[...] = grad_norm if j == 0 else gn_ref[...] + grad_norm
        for c, dst in enumerate((ak_out, as_out)):
            late.append((act_ref.at[(blk + c) % 2], dst))
        for c, dst in enumerate((gk_out, gs_out)):
            late.append((gp_ref.at[(blk + c) % 2], dst))
        late = [pltpu.make_async_copy(src, dst, late_sem.at[k]) for k, (src, dst) in enumerate(late)]
        for copy in late:
            copy.start()
        res_ref[...] = (h1_ref[...] + mixed_ref[...] + line(b2_ref)).astype(BF)
        outs[8].start()
        normal, inv = normalise(h1_ref[...])
        total = gn_ref[...]
        cot = cot_ref[...].astype(F32)
        sums_ref[0:1, :] = column_sum(total * normal)
        sums_ref[1:2, :] = column_sum(total)
        grad_hidden1 = cot + norm_back(total, normal, inv, line(g2_ref))
        gh_ref[...] = grad_hidden1
        branch = grad_hidden1.astype(BF)
        gb_ref[...] = branch
        outs[9].start()
        outs[10].start()
        sums_ref[2:3, :] = column_sum(branch.astype(F32))
        sums_ref[3:4, :] = column_sum(cot)
        ga_ref[...] = dot_nt(branch, wo_ref[...]).astype(BF)
        outs[11].start()
        p_copy(1, 1).wait()
        p_copy(2, 0).wait()
        for out in outs:
            out.wait()
        for copy in late:
            copy.wait()


def front(plan, halo, blk, x, xo, seg, sego, pos, poso, cot, table, vectors, wqkv, wo, w1, w2):
    half, width = x.shape
    hidden = w1.shape[1]
    keys = half + halo
    heads = width // HD
    anywhere = pl.BlockSpec(memory_space=pl.ANY)
    shapes = [
        ((half, width), F32),
        ((half, width), BF),
        ((half, width), BF),
        ((half, width), BF),
        ((keys, width), BF),
        ((keys, width), BF),
        ((half, width), BF),
        ((heads, half, keys), BF),
        ((half, width), BF),
        ((half, hidden // 2), BF),
        ((half, hidden // 2), BF),
        ((half, hidden // 2), BF),
        ((half, hidden // 2), BF),
        ((half, width), BF),
        ((half, width), F32),
        ((half, width), BF),
        ((half, width), BF),
        ((1, hidden), F32),
        ((4, width), F32),
    ]
    return pl.pallas_call(
        functools.partial(front_kernel, hidden // plan.groups // 2),
        grid_spec=pltpu.PrefetchScalarGridSpec(
            num_scalar_prefetch=1,
            grid=(4,),
            in_specs=[whole(a.shape) for a in (x, xo, seg, sego, pos, poso, cot, table) + vectors] + [anywhere] * 4,
            out_specs=[anywhere] * 17 + [whole((1, hidden)), whole((4, width))],
            scratch_shapes=[
                pltpu.VMEM(wqkv.shape, BF),
                pltpu.VMEM(wo.shape, BF),
                pltpu.VMEM(w1.shape, BF),
                pltpu.VMEM(w2.shape, BF),
                pltpu.VMEM((half, width), F32),
                pltpu.VMEM((keys, width), BF),
                pltpu.VMEM((half, width), BF),
                pltpu.VMEM((half, 128), BF),
                pltpu.VMEM((half, width), BF),
                pltpu.VMEM((keys, width), BF),
                pltpu.VMEM((keys, width), BF),
                pltpu.VMEM((half, keys), F32),
                pltpu.VMEM((half, width), BF),
                pltpu.VMEM((2, 4, half, keys), BF),
                pltpu.VMEM((half, width), F32),
                pltpu.VMEM((half, width), BF),
                pltpu.VMEM((2, half, hidden // 2), BF),
                pltpu.VMEM((2, half, hidden // 2), BF),
                pltpu.VMEM((half, width), F32),
                pltpu.VMEM((half, width), F32),
                pltpu.VMEM((half, width), BF),
                pltpu.VMEM((half, width), F32),
                pltpu.VMEM((half, width), BF),
                pltpu.VMEM((half, width), BF),
                pltpu.SemaphoreType.DMA((4,)),
                pltpu.SemaphoreType.DMA((12,)),
                pltpu.SemaphoreType.DMA((2,)),
                pltpu.SemaphoreType.DMA((4,)),
            ],
        ),
        out_shape=[jax.ShapeDtypeStruct(*s) for s in shapes],
        compiler_params=params(60),
        cost_estimate=cost(
            200 * half * width * (5 * width + 4 * hidden) + 400 * half * keys * width, 800 * width * hidden
        ),
        name="front",
    )(blk, x, xo, seg, sego, pos, poso, cot, table, *vectors, wqkv, wo, w1, w2)


class Plan:
    def __init__(self, ndp):
        self.ndp = ndp
        self.groups = min(16, ndp)
        self.bits = self.groups.bit_length() - 1
        self.rest = ndp // self.groups
        wanted = {"first": (2, 1, 0, 3), "second": (0, 1, 2, 3), "left": (0, 1, 2, 3), "right": (1, 0, 2, 3), "small": (1, 2, 3, 0)}
        self.orders = {k: [b for b in v if b < self.bits] for k, v in wanted.items()}

    def place(self, piece, p):
        code = 0
        for bit in self.orders[piece]:
            code = 2 * code + ((p >> bit) & 1)
        place = self.groups - 1 - code
        return divmod(place, self.groups // 2)


def feed_weights_kernel(
    plan, own_ref, n2_ref, n2o_ref, g_ref, go_ref, act_ref, acto_ref, cot_ref, coto_ref,
    first_send, first_keep, second_send, second_keep, acc1_ref, acc2_ref,
):
    i = pl.program_id(0)
    own = own_ref[0]
    per = plan.groups // 2
    rows1 = n2_ref.shape[1] // plan.groups
    rows2 = act_ref.shape[1] // per
    acc1_ref[...] = dot_tn(n2_ref[...], g_ref[...]) + dot_tn(n2o_ref[...], go_ref[...])
    acc2_ref[...] = dot_tn(act_ref[...], cot_ref[...]) + dot_tn(acto_ref[...], coto_ref[...])
    for step in range(2):

        @pl.when(i == step)
        def _():
            for p in range(plan.groups):
                block = acc1_ref[pl.ds(pl.multiple_of((own ^ p) * rows1, 16), rows1), :]
                kept, at = plan.place("first", p)
                (first_send, first_keep)[kept][at, step * rows1 : (step + 1) * rows1, :] = block.astype(BF)
            for low in range(per):
                block = acc2_ref[pl.ds(pl.multiple_of(((own % per) ^ low) * rows2, 16), rows2), :]
                kept, at = plan.place("second", step * per + low)
                (second_send, second_keep)[kept][at] = block.astype(BF)


def feed_weights(plan, own, n2, n2o, g, go, act, acto, cot, coto):
    half, width = n2.shape
    chunk = g.shape[1] // 2
    part = jax.ShapeDtypeStruct((plan.groups // 2, 2 * (width // plan.groups), chunk), BF)
    place = lambda i, o: (0, (o[0] // (plan.groups // 2)) ^ i)
    step = lambda i, o: (0, i)
    return pl.pallas_call(
        functools.partial(feed_weights_kernel, plan),
        grid_spec=pltpu.PrefetchScalarGridSpec(
            num_scalar_prefetch=1,
            grid=(2,),
            in_specs=[
                whole(n2.shape),
                whole(n2o.shape),
                pl.BlockSpec((half, chunk), step),
                pl.BlockSpec((half, chunk), step),
                pl.BlockSpec((half, chunk), place),
                pl.BlockSpec((half, chunk), place),
                whole(cot.shape),
                whole(coto.shape),
            ],
            out_specs=[whole(part.shape)] * 4,
            scratch_shapes=[pltpu.VMEM((width, chunk), F32), pltpu.VMEM((chunk, width), F32)],
        ),
        out_shape=(part,) * 4,
        compiler_params=params(40),
        cost_estimate=cost(8 * half * width * chunk * 2, 24 * width * chunk),
        name="feed_weights",
    )(own, n2, n2o, g, go, act, acto, cot, coto)


def attend_back_kernel(side_ref, q_ref, k_ref, v_ref, p_ref, ga_ref, *rest):
    d_ref, dh_ref = rest[-2:]
    half = q_ref.shape[0]
    q = q_ref[...]
    grad = ga_ref[...]
    dqs, dks, dvs = [], [], []
    for head in range(2):
        grad_one = jnp.where(lanes_of(grad.shape, head), grad, jnp.zeros_like(grad))
        grad_probs = dot_nt(grad_one, v_ref[...])
        probs = p_ref[head].astype(F32)
        row = jnp.sum(probs * grad_probs, -1, keepdims=True)
        grad_scores = (probs * (grad_probs - row)).astype(BF)
        dqs.append(dot_nn(grad_scores, k_ref[...]))
        dks.append(dot_tn(grad_scores, q))
        dvs.append(dot_tn(p_ref[head], grad))
    first = lanes_of(dqs[0].shape, 0)
    d_ref[0] = (jnp.where(first, dqs[0], dqs[1]) * 0.125).astype(BF)
    first = lanes_of(dks[0].shape, 0)
    dk = jnp.where(first, dks[0], dks[1]).astype(BF)
    dv = jnp.where(first, dvs[0], dvs[1]).astype(BF)
    d_ref[1] = dk[:half]
    d_ref[2] = dv[:half]
    dh_ref[0] = dk[half:]
    dh_ref[1] = dv[half:]


def attend_back(side, q, k, v, probs, ga, *after):
    half, width = q.shape
    keys = k.shape[0]
    halo = keys - half
    steps = width // 256

    def col(i, s):
        return s[0] * steps + i

    return pl.pallas_call(
        attend_back_kernel,
        grid_spec=pltpu.PrefetchScalarGridSpec(
            num_scalar_prefetch=1,
            grid=(steps,),
            in_specs=[
                pl.BlockSpec((half, 128), lambda i, s: (0, col(i, s))),
                pl.BlockSpec((keys, 128), lambda i, s: (0, col(i, s))),
                pl.BlockSpec((keys, 128), lambda i, s: (0, col(i, s))),
                pl.BlockSpec((2, half, keys), lambda i, s: (col(i, s), 0, 0)),
                pl.BlockSpec((half, 128), lambda i, s: (0, col(i, s))),
            ]
            + [pl.BlockSpec(memory_space=pl.ANY)] * len(after),
            out_specs=[
                pl.BlockSpec((3, half, 128), lambda i, s: (0, 0, i)),
                pl.BlockSpec((2, halo, 128), lambda i, s: (0, 0, i)),
            ],
        ),
        out_shape=(
            jax.ShapeDtypeStruct((3, half, width // 2), BF),
            jax.ShapeDtypeStruct((2, halo, width // 2), BF),
        ),
        compiler_params=params(40),
        cost_estimate=cost(16 * half * keys * width, half * keys * width // HD),
        name="attend_back",
    )(side, q, k, v, probs, ga, *after)


def add_rows(ref, which, start, halo, extra):
    part = ref[which, pl.ds(start, halo), :].astype(F32) + extra.astype(F32)
    ref[which, pl.ds(start, halo), :] = part.astype(BF)


def attend_weights_kernel(
    plan, own_ref, blk_ref, n1_ref, n1o_ref, d_ref, dh_ref, do_ref, dho_ref, att_ref, atto_ref,
    gb_ref, gbo_ref, *rest
):
    outs, acc_ref, mine_ref, other_ref = rest[:4], rest[4], rest[5], rest[6]
    half = n1_ref.shape[0]
    halo = dh_ref.shape[1]
    width = att_ref.shape[1]
    own = own_ref[0]
    rows = width // plan.groups
    start = pl.multiple_of((1 - blk_ref[0]) * (half - halo), 16)
    start_other = pl.multiple_of(blk_ref[0] * (half - halo), 16)
    mine_ref[...] = d_ref[...]
    other_ref[...] = do_ref[...]
    for which in range(2):
        add_rows(mine_ref, 1 + which, start, halo, dho_ref[which])
        add_rows(other_ref, 1 + which, start_other, halo, dh_ref[which])
    for panel in range(4):
        if panel < 3:
            acc_ref[...] = dot_tn(n1_ref[...], mine_ref[panel]) + dot_tn(
                n1o_ref[...], other_ref[panel]
            )
        else:
            acc_ref[...] = dot_tn(att_ref[...], gb_ref[...]) + dot_tn(atto_ref[...], gbo_ref[...])
        for p in range(plan.groups):
            source = pl.multiple_of((own ^ p) * rows, 16)
            kept, place = plan.place(("left", "right")[panel // 2], p)
            at = (panel % 2) * (width // 2)
            outs[2 * (panel // 2) + kept][place, :, at : at + width // 2] = acc_ref[pl.ds(source, rows), :].astype(BF)


def attend_weights(plan, own, blk, n1, n1o, d, dh, do, dho, att, atto, gb, gbo):
    half, width = att.shape
    cols = width // 2
    part = jax.ShapeDtypeStruct((plan.groups // 2, width // plan.groups, width), BF)
    return pl.pallas_call(
        functools.partial(attend_weights_kernel, plan),
        grid_spec=pltpu.PrefetchScalarGridSpec(
            num_scalar_prefetch=2,
            grid=(1,),
            in_specs=[
                whole(n1.shape),
                whole(n1o.shape),
                whole(d.shape),
                whole(dh.shape),
                whole(do.shape),
                whole(dho.shape),
                whole(att.shape),
                whole(atto.shape),
                pl.BlockSpec((half, cols), lambda i, o, b: (0, b[0])),
                pl.BlockSpec((half, cols), lambda i, o, b: (0, b[0])),
            ],
            out_specs=[whole(part.shape)] * 4,
            scratch_shapes=[
                pltpu.VMEM((width, cols), F32),
                pltpu.VMEM(d.shape, BF),
                pltpu.VMEM(do.shape, BF),
            ],
        ),
        out_shape=(part,) * 4,
        compiler_params=params(40),
        cost_estimate=cost(8 * half * width * width, 4 * width * width + 24 * half * width),
        name="attend_weights",
    )(own, blk, n1, n1o, d, dh, do, dho, att, atto, gb, gbo)


def front_back_kernel(
    blk_ref, da_ref, db_ref, ha_ref, hb_ref, w_ref, h0_ref, gh_ref, g1_ref, pos_ref, sums_ref, b1_ref,
    *rest,
):
    gx_ref, mine_ref, other_ref, acc_ref, small_ref = rest[-5:]
    half, width = h0_ref.shape
    halo = ha_ref.shape[1]
    cols = width // 2
    places = small_ref.shape[0] - 12
    start = pl.multiple_of((1 - blk_ref[0]) * (half - halo), 16)
    acc_ref[0] = da_ref[...]
    acc_ref[1] = db_ref[...]
    for which in range(2):
        add_rows(acc_ref.at[0], 1 + which, start, halo, ha_ref[which])
        add_rows(acc_ref.at[1], 1 + which, start, halo, hb_ref[which])
    total = jnp.zeros((half, width), F32)
    for which in range(3):
        for side, ref in enumerate((acc_ref.at[0], acc_ref.at[1])):
            actual = blk_ref[0] if side == 0 else 1 - blk_ref[0]
            at = pl.multiple_of(actual * cols, 128)
            panel = ref[which]
            total = total + dot_nt(panel, w_ref[:, pl.ds(pl.multiple_of(which * width + at, 128), cols)])
            if which != 1:
                k = places + (2 if which == 0 else 3)
                small_ref[k : k + 1, pl.ds(at, cols)] = column_sum(panel.astype(F32))
    normal, inv = normalise(h0_ref[...])
    small_ref[places : places + 1, :] = column_sum(total * normal)
    small_ref[places + 1 : places + 2, :] = column_sum(total)
    grad = (gh_ref[...] + norm_back(total, normal, inv, line(g1_ref))).astype(BF)
    gx_ref[...] = grad
    hot = (lax.broadcasted_iota(jnp.int32, (places, half), 0) == pos_ref[...]).astype(F32).astype(BF)
    small_ref[:places, :] = dot_nn(hot, grad)
    small_ref[places + 4 : places + 8, :] = sums_ref[...]
    for k in range(4):
        small_ref[places + 8 + k : places + 9 + k, :] = b1_ref[:, k * width : (k + 1) * width]
    for ref, core in ((mine_ref, blk_ref[0]), (other_ref, 1 - blk_ref[0])):
        ref[...] = small_ref[:, pl.ds(pl.multiple_of(core * cols, 128), cols)].astype(BF)


def front_back(blk, da, db, ha, hb, w, h0, gh, g1, pos, sums, b1, places, after):
    half, width = h0.shape
    return pl.pallas_call(
        front_back_kernel,
        grid_spec=pltpu.PrefetchScalarGridSpec(
            num_scalar_prefetch=1,
            grid=(1,),
            in_specs=[whole(a.shape) for a in (da, db, ha, hb, w, h0, gh, g1, pos, sums, b1)]
            + [pl.BlockSpec(memory_space=pl.ANY)] * len(after),
            out_specs=[whole((half, width))] + [whole((places + 12, width // 2))] * 2,
            scratch_shapes=[pltpu.VMEM((2,) + da.shape, BF), pltpu.VMEM((places + 12, width), F32)],
        ),
        out_shape=(
            jax.ShapeDtypeStruct((half, width), BF),
            jax.ShapeDtypeStruct((places + 12, width // 2), BF),
            jax.ShapeDtypeStruct((places + 12, width // 2), BF),
        ),
        compiler_params=params(40),
        cost_estimate=cost(6 * half * width * width, 6 * width * width + 20 * half * width),
        name="front_back",
    )(blk, da, db, ha, hb, w, h0, gh, g1, pos, sums, b1, *after)


def swap(v):
    return lax.ppermute(v, "blk", [(0, 1), (1, 0)])


def across(v, ndp, flip):
    return lax.ppermute(v, "dp", [(i, i ^ flip) for i in range(ndp)])


def wide(v):
    return v.astype(F32)


def add_kernel(count, *refs):
    total = refs[0][...].astype(F32)
    for ref in refs[1:count]:
        total = total + ref[...].astype(F32)
    refs[-1][...] = total.astype(BF)


def spec_at(block, at):
    return pl.BlockSpec(block, lambda i: (at,) + (0,) * (len(block) - 1))


ANYWHERE = pl.BlockSpec(memory_space=pl.ANY)


def add(arrays, places, block, before):
    return pl.pallas_call(
        functools.partial(add_kernel, len(arrays)),
        grid=(1,),
        in_specs=[spec_at(block, at) for at in places] + [ANYWHERE] * len(before),
        out_specs=spec_at(block, 0),
        out_shape=jax.ShapeDtypeStruct(block, BF),
        compiler_params=params(24),
        cost_estimate=cost(1, 1),
        name="add",
    )(*arrays, *before)


class Piece:
    def __init__(self, plan, name, sent, kept):
        self.plan, self.order, self.phase = plan, plan.orders[name], 0
        self.terms, self.starts, self.at = [kept], [0], 0
        self.left = kept.shape[0]
        self.send(sent, 0)

    def send(self, value, start):
        self.sent = value
        self.terms.append(across(value, self.plan.ndp, self.plan.rest << self.order[self.phase]))
        self.starts.append(start)
        self.phase += 1

    def step(self, *before):
        if self.phase == self.plan.bits:
            return
        h = self.left // 2
        block = (h,) + self.terms[0].shape[1:]
        value = add(self.terms, [(self.at - s) // h for s in self.starts], block, before)
        self.at, self.left = self.at + h, h
        self.send(value, self.at)

    def rest(self):
        return self.terms, [self.at - s for s in self.starts]


class Everywhere:
    def __init__(self, plan, mine, other):
        self.plan, self.phase = plan, 0
        self.flips = [plan.rest << b for b in plan.orders["small"]] + [1 << b for b in range(plan.rest.bit_length() - 1)]
        self.sent, self.got = mine, swap(other)

    def step(self, *before):
        if self.phase > len(self.flips):
            return
        self.sent = add((self.sent, self.got), (0, 0), self.sent.shape, before)
        flips = self.flips + [None]
        flip = flips[self.phase]
        self.got = swap(self.sent) if flip is None else across(self.sent, self.plan.ndp, flip)
        self.phase += 1

    def both(self):
        while self.phase <= len(self.flips):
            self.step()
        return self.sent, self.got


def split_kernel(counts, blk_ref, *refs):
    outs = refs[-2 * len(counts) :]
    done = 0
    for g, count in enumerate(counts):
        total = refs[done][0].astype(F32)
        for ref in refs[done + 1 : done + count]:
            total = total + ref[0].astype(F32)
        done += count
        mine, other = outs[2 * g], outs[2 * g + 1]
        half = mine.shape[1]
        for k in range(mine.shape[0]):
            low = total[2 * k * half : (2 * k + 1) * half]
            high = total[(2 * k + 1) * half : (2 * k + 2) * half]
            first = blk_ref[0] == 0
            mine[k] = jnp.where(first, low, high)
            other[k] = jnp.where(first, high, low)


def split_rows(blk, rows, *pieces):
    arrays, specs, counts, shapes = [], [], [], []
    for piece in pieces:
        terms, places = piece.rest()
        block = (1,) + terms[0].shape[1:]
        arrays += terms
        specs += [pl.BlockSpec(block, functools.partial(lambda at, i, b: (at, 0, 0), at)) for at in places]
        counts.append(len(terms))
        shapes += [jax.ShapeDtypeStruct((block[1] // (2 * rows), rows, block[2]), F32)] * 2
    return pl.pallas_call(
        functools.partial(split_kernel, counts),
        grid_spec=pltpu.PrefetchScalarGridSpec(
            num_scalar_prefetch=1, grid=(1,), in_specs=specs, out_specs=[whole(v.shape) for v in shapes]
        ),
        out_shape=shapes,
        compiler_params=params(24),
        cost_estimate=cost(1, 1),
        name="split_rows",
    )(blk, *arrays)


def total_kernel(*refs):
    total = refs[0][0].astype(F32)
    for ref in refs[1:-1]:
        total = total + ref[0].astype(F32)
    refs[-1][...] = total


def total_of(piece):
    terms, places = piece.rest()
    block = (1,) + terms[0].shape[1:]
    return pl.pallas_call(
        total_kernel,
        grid=(1,),
        in_specs=[spec_at(block, at) for at in places],
        out_specs=whole(block[1:]),
        out_shape=jax.ShapeDtypeStruct(block[1:], F32),
        compiler_params=params(24),
        cost_estimate=cost(1, 1),
        name="total",
    )(*terms)


def join_feed_kernel(blk_ref, mine_ref, got_ref, out_ref):
    count, _, cols = mine_ref.shape
    for ref, core in ((mine_ref, blk_ref[0]), (got_ref, 1 - blk_ref[0])):
        for k in range(count):
            out_ref[:, pl.ds(pl.multiple_of((core * count + k) * cols, 128), cols)] = ref[k]


def join_feed(blk, mine, got):
    count, rows, cols = mine.shape
    shape = (rows, 2 * count * cols)
    return pl.pallas_call(
        join_feed_kernel,
        grid_spec=pltpu.PrefetchScalarGridSpec(
            num_scalar_prefetch=1, grid=(1,), in_specs=[whole(mine.shape)] * 2, out_specs=whole(shape)
        ),
        out_shape=jax.ShapeDtypeStruct(shape, F32),
        compiler_params=params(24),
        cost_estimate=cost(1, 1),
        name="join_feed",
    )(blk, mine, got)


def join_attend_kernel(blk_ref, left_ref, right_ref, left_got_ref, right_got_ref, qkv_ref, out_ref):
    width = left_ref.shape[2]
    cols = width // 2
    for left, right, core in (
        (left_ref, right_ref, blk_ref[0]),
        (left_got_ref, right_got_ref, 1 - blk_ref[0]),
    ):
        at = core * cols
        qkv_ref[:, pl.ds(pl.multiple_of(at, 128), cols)] = left[0, :, :cols]
        qkv_ref[:, pl.ds(pl.multiple_of(width + at, 128), cols)] = left[0, :, cols:]
        qkv_ref[:, pl.ds(pl.multiple_of(2 * width + at, 128), cols)] = right[0, :, :cols]
        out_ref[:, pl.ds(pl.multiple_of(at, 128), cols)] = right[0, :, cols:]


def join_attend(blk, left, right, left_got, right_got):
    _, rows, width = left.shape
    shapes = ((rows, 3 * width), (rows, width))
    return pl.pallas_call(
        join_attend_kernel,
        grid_spec=pltpu.PrefetchScalarGridSpec(
            num_scalar_prefetch=1,
            grid=(1,),
            in_specs=[whole(left.shape)] * 4,
            out_specs=[whole(v) for v in shapes],
        ),
        out_shape=[jax.ShapeDtypeStruct(v, F32) for v in shapes],
        compiler_params=params(24),
        cost_estimate=cost(1, 1),
        name="join_attend",
    )(blk, left, right, left_got, right_got)


def join_small_kernel(blk_ref, mine_ref, got_ref, *outs):
    joined_ref = outs[-1]
    cols = mine_ref.shape[1]
    width = 2 * cols
    places = outs[0].shape[0]
    for ref, core in ((mine_ref, blk_ref[0]), (got_ref, 1 - blk_ref[0])):
        joined_ref[:, pl.ds(pl.multiple_of(core * cols, 128), cols)] = ref[...].astype(F32)
    outs[0][...] = joined_ref[:places, :]
    for k, out in enumerate(outs[1:9]):
        out[...] = joined_ref[places + k, :]
    for k in range(outs[9].shape[0] // width):
        outs[9][k * width : (k + 1) * width] = joined_ref[places + 8 + k, :]


def join_small(blk, mine, got, places, hidden):
    rows, cols = mine.shape
    width = 2 * cols
    shapes = [(places, width)] + [(width,)] * 8 + [(hidden,)]
    return pl.pallas_call(
        join_small_kernel,
        grid_spec=pltpu.PrefetchScalarGridSpec(
            num_scalar_prefetch=1,
            grid=(1,),
            in_specs=[whole(mine.shape)] * 2,
            out_specs=[whole(v) for v in shapes],
            scratch_shapes=[pltpu.VMEM((rows, width), F32)],
        ),
        out_shape=[jax.ShapeDtypeStruct(v, F32) for v in shapes],
        compiler_params=params(24),
        cost_estimate=cost(1, 1),
        name="join_small",
    )(blk, mine, got)


def behind(values, *others):
    return lax.optimization_barrier((values, others))[0]


def rest_of(plan, value, blk):
    groups = [[g * plan.rest + i for i in range(plan.rest)] for g in range(plan.groups)]
    value = lax.psum(value, "dp", axis_index_groups=groups)
    rows = value.shape[0] // (2 * plan.rest)
    return lax.dynamic_slice_in_dim(value, ((lax.axis_index("dp") % plan.rest) * 2 + blk) * rows, rows, axis=0)


def per_device(
    ndp, inputs, segments, positions, pos_table, ln1_gain, ln1_shift, qkv_weight, query_bias,
    value_bias, out_weight, out_bias, ln2_gain, ln2_shift, fc1_weight, fc1_bias, fc2_weight,
    fc2_bias, cotangent,
):
    plan = Plan(ndp)
    x, cot = inputs[0], cotangent[0]
    half, width = x.shape
    hidden = fc1_weight.shape[1]
    places = pos_table.shape[0]
    halo = next(h for h in range(SEG_MOST - 1, half + 1) if (half + h) % 128 == 0 and (half - h) % 16 == 0)
    blk = lax.axis_index("blk")
    dp = lax.axis_index("dp")
    blk1 = blk.astype(jnp.int32).reshape(1)
    own1 = (dp // plan.rest).astype(jnp.int32).reshape(1)

    x_other, seg_other, pos_other = swap(x), swap(segments), swap(positions)
    cot_other = swap(cot)
    vectors = (ln1_gain, ln1_shift, query_bias, value_bias, out_bias, ln2_gain, ln2_shift, fc1_bias, fc2_bias)
    (
        hidden0, n1, n1_other, q, k, v, att, probs, n2, grad_send, grad_keep, act_send, act_keep, result, gh1, gb, ga,
        b1_grad, sums,
    ) = front(
        plan, halo, blk1, x, x_other, segments, seg_other, positions, pos_other, cot, pos_table, vectors,
        qkv_weight, out_weight, fc1_weight, fc2_weight,
    )
    grad_other, act_other, n2_other = swap(grad_send), swap(act_send), swap(behind(n2, cot_other))
    d_send, h_send = attend_back(1 - blk1, q, k, v, probs, ga)
    parts = feed_weights(
        plan, own1, n2, n2_other, grad_keep, grad_other, behind(act_keep, d_send), act_other, cot, cot_other
    )
    first, second = Piece(plan, "first", *parts[:2]), Piece(plan, "second", *parts[2:])
    att_other, gb_other, d_other, h_other = swap(att), swap(gb), swap(d_send), swap(h_send)
    d_keep, h_keep = attend_back(blk1, q, k, v, probs, ga, parts[0])
    h_late = swap(h_keep)
    parts = attend_weights(
        plan, own1, blk1, n1, n1_other, d_keep, h_keep, d_other, h_other, att, att_other, gb, gb_other
    )
    left, right = Piece(plan, "left", *parts[:2]), Piece(plan, "right", *parts[2:])
    grad_x, mine, other = front_back(
        blk1, d_keep, d_send, h_other, h_late,
        qkv_weight, hidden0, gh1, ln1_gain, positions, sums, b1_grad, places, (parts[0],),
    )
    small = Everywhere(plan, mine, other)
    before = grad_x
    for piece in (
        small, first, right, small, second, left, small, first, right, small, second, left, first, right, second, left
    ):
        piece.step(before)
        before = piece.sent
    rows = width // plan.groups // 2
    if plan.rest == 1:
        fc2_grad = total_of(second)
        first_mine, first_sent = split_rows(blk1, rows, first)
        first_got = swap(first_sent)
        left_mine, left_sent, right_mine, right_sent = split_rows(blk1, rows, left, right)
        left_got, right_got = swap(left_sent), swap(right_sent)
        fc1_grad = join_feed(blk1, first_mine, first_got)
        qkv_grad, out_grad = join_attend(blk1, left_mine, right_mine, left_got, right_got)
    else:
        both = lax.all_gather(total_of(second), "blk", axis=0, tiled=True)
        fc2_grad = rest_of(plan, both, blk)
        value = total_of(first).reshape(2, 2 * rows, -1)
        columns = [lax.all_gather(v, "blk", axis=1, tiled=True) for v in (value[0], value[1])]
        columns = jnp.concatenate(columns, 1).reshape(2 * rows, 2, 2, -1).transpose(0, 2, 1, 3)
        fc1_grad = rest_of(plan, columns.reshape(2 * rows, -1), blk)
        value = jnp.concatenate([total_of(left), total_of(right)], 1).reshape(2 * rows, 4, -1)
        value = lax.all_gather(value, "blk", axis=2, tiled=True)
        value = rest_of(plan, value.reshape(2 * rows, -1), blk)
        qkv_grad, out_grad = value[:, : 3 * width], value[:, 3 * width :]
    table, *vec, b1_all = join_small(blk1, *small.both(), places, hidden)
    return (
        result[None], grad_x[None], table, vec[0], vec[1], qkv_grad, vec[2], vec[3], out_grad,
        vec[6], vec[4], vec[5], fc1_grad, b1_all, fc2_grad, vec[7],
    )


def solution(mesh):
    split = P("dp", "blk", None)
    ids = P("dp", "blk")
    both = P(("dp", "blk"), None)
    none = P()
    return jax.shard_map(
        functools.partial(per_device, mesh.shape["dp"]),
        mesh=mesh,
        in_specs=(split, ids, ids) + (none,) * 14 + (split,),
        out_specs=(
            split, split, none, none, none, both, none, none, both, none, none, none, both, none, both, none,
        ),
        check_vma=False,
    )
```

```python
import functools

import jax
import jax.numpy as jnp
from jax import lax
from jax.experimental import pallas as pl
from jax.experimental.pallas import tpu as pltpu
from jax.sharding import PartitionSpec as P

HD = 64
SEG_MOST = 196
EPS = 1e-06
inv_root_two = 0.7071067811865476
inv_root_two_pi = 0.3989422804014327
BF = jnp.bfloat16
F32 = jnp.float32
MIB = 1 << 20


def dot_nn(a, b):
    return jnp.dot(a, b, preferred_element_type=F32)


def dot_nt(a, b):
    return lax.dot_general(a, b, (((1,), (1,)), ((), ())), preferred_element_type=F32)


def dot_tn(a, b):
    return lax.dot_general(a, b, (((0,), (0,)), ((), ())), preferred_element_type=F32)


def normalise(hidden):
    mean = jnp.mean(hidden, -1, keepdims=True)
    centred = hidden - mean
    inv = lax.rsqrt(jnp.mean(centred * centred, -1, keepdims=True) + EPS)
    return centred * inv, inv


def norm_back(grad, normal, inv, gain):
    scaled = grad * gain
    centre = jnp.mean(scaled, -1, keepdims=True)
    along = jnp.mean(scaled * normal, -1, keepdims=True)
    return inv * (scaled - centre - normal * along)


def line(ref):
    return ref[...].reshape(1, -1)


def column_sum(v):
    return jnp.sum(v, axis=0, keepdims=True)


def params(vmem):
    return pltpu.CompilerParams(vmem_limit_bytes=(60 if vmem > 24 else vmem) * MIB)


def cost(flops, bytes_accessed, trans=0):
    return pl.CostEstimate(
        flops=int(flops), bytes_accessed=int(bytes_accessed), transcendentals=int(trans)
    )


def whole(shape):
    return pl.BlockSpec(shape, lambda *_: (0,) * len(shape))


ANYWHERE = pl.BlockSpec(memory_space=pl.ANY)


def copies(pairs, sem):
    return [pltpu.make_async_copy(src, dst, sem.at[k]) for k, (src, dst) in enumerate(pairs)]


def started(pairs, sem):
    made = copies(pairs, sem)
    for copy in made:
        copy.start()
    return made


def done(made):
    for copy in made:
        copy.wait()


def lanes_of(shape, head):
    return (lax.broadcasted_iota(jnp.int32, shape, 1) % 128 < HD) == (head % 2 == 0)


def embedded(x_ref, pos_ref, table_ref):
    half = x_ref.shape[0]
    places = table_ref.shape[0]
    hot = (lax.broadcasted_iota(jnp.int32, (places, half), 0) == pos_ref[...]).astype(F32).astype(BF)
    return x_ref[...].astype(F32) + dot_tn(hot, table_ref[...])


def crop_lanes(seg_ref):
    half = seg_ref.shape[1]
    hot = (lax.broadcasted_iota(jnp.int32, (8, half), 0) == seg_ref[...]).astype(F32).astype(BF)
    eye = lax.broadcasted_iota(jnp.int32, (8, 128), 0) == lax.broadcasted_iota(jnp.int32, (8, 128), 1)
    return dot_tn(hot, eye.astype(F32).astype(BF)).astype(BF)


def front_kernel(block, blk_ref, *refs):
    sources, refs = refs[:21], refs[21:]
    (
        h0_out, n1_out, n1o_out, q_out, k_out, v_out, att_out, p_out, n2_out,
        gs_out, gk_out, as_out, ak_out, res_out, gn_out, h1_out, b1g_ref,
    ) = refs[:17]
    targets, refs = refs[17:38], refs[38:]
    (
        x_ref, xo_ref, seg_ref, sego_ref, pos_ref, poso_ref, cot_ref, table_ref,
        g1_ref, s1_ref, qb_ref, vb_ref, bo_ref, g2_ref, s2_ref, b1_ref, b2_ref, wqkv_ref, wo_ref, w1_ref, w2_ref,
    ) = targets
    (
        h0_ref, own_ref, n1_ref, n1o_ref, hoto_ref, q_ref, k_ref, v_ref, bias_ref,
        att_ref, p_ref, h1_ref, n2_ref, gp_ref, act_ref, mixed_ref, gn_ref, res_ref,
        in_sem, out_sem, late_sem,
    ) = refs
    half, width = x_ref.shape
    keys = k_ref.shape[0]
    halo = keys - half
    hidden = w1_ref.shape[1]
    blk = blk_ref[0]
    start = pl.multiple_of(blk * (half - halo), 16)
    loads = [pltpu.make_async_copy(src, dst, in_sem.at[k]) for k, (src, dst) in enumerate(zip(sources, targets))]
    outs = [
        pltpu.make_async_copy(src, dst, out_sem.at[k])
        for k, (src, dst) in enumerate(
            (
                (h0_ref, h0_out), (own_ref, n1_out), (n1o_ref, n1o_out), (q_ref, q_out), (k_ref, k_out),
                (v_ref, v_out), (att_ref, att_out), (n2_ref, n2_out), (res_ref, res_out), (gn_ref, gn_out),
                (h1_ref, h1_out), (p_ref, p_out),
            )
        )
    ]
    soon = (0, 4, 7, 1, 5, 8, 9, 17, 2, 3, 10, 11)
    then = (18, 19, 20, 6, 12, 13, 14, 15, 16)
    for k in soon:
        loads[k].start()
    for k in soon[:7]:
        loads[k].wait()
    hidden0 = embedded(x_ref, pos_ref, table_ref)
    h0_ref[...] = hidden0
    normal, _ = normalise(hidden0)
    own_ref[...] = (normal * line(g1_ref) + line(s1_ref)).astype(BF)
    n1_ref[:half, :] = own_ref[...]
    normal, _ = normalise(embedded(xo_ref, poso_ref, table_ref))
    n1o_ref[...] = (normal * line(g1_ref) + line(s1_ref)).astype(BF)
    n1_ref[half:, :] = n1o_ref[pl.ds(start, halo), :]
    for k in soon[7:]:
        loads[k].wait()
    for k in then:
        loads[k].start()
    hot = crop_lanes(seg_ref)
    hoto_ref[...] = crop_lanes(sego_ref)
    bias_ref[:, :half] = (dot_nt(hot, hot) - 1.0) * 1e9
    bias_ref[:, half:] = (dot_nt(hot, hoto_ref[pl.ds(start, halo), :]) - 1.0) * 1e9
    q = dot_nn(own_ref[...], wqkv_ref[:, :width]) + line(qb_ref)
    q_ref[...] = (q.astype(BF).astype(F32) * 0.125).astype(BF)
    k_ref[...] = dot_nn(n1_ref[...], wqkv_ref[:, width : 2 * width]).astype(BF)
    v_ref[...] = (dot_nn(n1_ref[...], wqkv_ref[:, 2 * width :]) + line(vb_ref)).astype(BF)
    for out in outs[:6]:
        out.start()
    for pair in range(width // 128):
        cols = slice(pair * 128, pair * 128 + 128)
        q = q_ref[:, cols]
        both = []
        for head in range(2):
            q_one = jnp.where(lanes_of(q.shape, head), q, jnp.zeros_like(q))
            scores = dot_nt(q_one, k_ref[:, cols]) + bias_ref[...]
            top = jnp.max(scores, -1, keepdims=True)
            weight = jnp.exp(scores - top)
            probs = (weight * (1.0 / jnp.sum(weight, -1, keepdims=True))).astype(BF)
            p_ref[2 * pair + head] = probs
            both.append(dot_nn(probs, v_ref[:, cols]))
        att_ref[:, cols] = jnp.where(lanes_of(both[0].shape, 0), both[0], both[1]).astype(BF)
    outs[6].start()
    outs[11].start()
    for k in then:
        loads[k].wait()
    hidden1 = h0_ref[...] + dot_nn(att_ref[...], wo_ref[...]) + line(bo_ref)
    h1_ref[...] = hidden1
    normal, _ = normalise(hidden1)
    n2_ref[...] = (normal * line(g2_ref) + line(s2_ref)).astype(BF)
    outs[7].start()
    outs[10].start()
    late = []
    chunk = 768
    part = chunk // 2
    for j in range(hidden // chunk):
        at = slice(j * chunk, (j + 1) * chunk)
        pre = dot_nn(n2_ref[...], w1_ref[:, at]) + b1_ref[at].reshape(1, -1)
        grad_act = dot_nt(cot_ref[...], w2_ref[at, :])
        cdf = 0.5 + 0.5 * lax.erf(pre * inv_root_two)
        act = (pre * cdf).astype(BF)
        slope = cdf + pre * jnp.exp(-0.5 * pre * pre) * inv_root_two_pi
        grad_pre = (grad_act * slope).astype(BF)
        b1g_ref[:, at] = column_sum(grad_pre.astype(F32))
        side, sub = divmod(j * chunk, hidden // 2)
        gp_ref[side, :, sub : sub + chunk] = grad_pre
        mine = slice(j * part, (j + 1) * part)
        for c in range(2):
            act_ref[c, :, mine] = jnp.concatenate(
                [act[:, t : t + block] for t in range(c * block, chunk, 2 * block)], 1
            )
        mixed = dot_nn(act, w2_ref[at, :])
        grad_norm = dot_nt(grad_pre, w1_ref[:, at])
        mixed_ref[...] = h1_ref[...] + line(b2_ref) + mixed if j == 0 else mixed_ref[...] + mixed
        gn_ref[...] = grad_norm if j == 0 else gn_ref[...] + grad_norm
    res_ref[...] = mixed_ref[...].astype(BF)
    for c, dst in enumerate((ak_out, as_out)):
        late.append((act_ref.at[(blk + c) % 2], dst))
    for c, dst in enumerate((gk_out, gs_out)):
        late.append((gp_ref.at[(blk + c) % 2], dst))
    late = [pltpu.make_async_copy(src, dst, late_sem.at[k]) for k, (src, dst) in enumerate(late)]
    for copy in late:
        copy.start()
    outs[8].start()
    outs[9].start()
    for out in outs:
        out.wait()
    for copy in late:
        copy.wait()


def front(plan, halo, blk, x, xo, seg, sego, pos, poso, cot, table, vectors, wqkv, wo, w1, w2):
    half, width = x.shape
    hidden = w1.shape[1]
    keys = half + halo
    heads = width // HD
    anywhere = pl.BlockSpec(memory_space=pl.ANY)
    operands = (x, xo, seg, sego, pos, poso, cot, table, *vectors, wqkv, wo, w1, w2)
    shapes = [
        ((half, width), F32),
        ((half, width), BF),
        ((half, width), BF),
        ((half, width), BF),
        ((keys, width), BF),
        ((keys, width), BF),
        ((half, width), BF),
        ((heads, half, keys), BF),
        ((half, width), BF),
        ((half, hidden // 2), BF),
        ((half, hidden // 2), BF),
        ((half, hidden // 2), BF),
        ((half, hidden // 2), BF),
        ((half, width), BF),
        ((half, width), F32),
        ((half, width), F32),
        ((1, hidden), F32),
    ]
    return pl.pallas_call(
        functools.partial(front_kernel, hidden // plan.groups // 2),
        grid_spec=pltpu.PrefetchScalarGridSpec(
            num_scalar_prefetch=1,
            grid=(1,),
            in_specs=[anywhere] * len(operands),
            out_specs=[anywhere] * 16 + [whole((1, hidden))],
            scratch_shapes=[pltpu.VMEM(v.shape, v.dtype) for v in operands]
            + [
                pltpu.VMEM((half, width), F32),
                pltpu.VMEM((half, width), BF),
                pltpu.VMEM((keys, width), BF),
                pltpu.VMEM((half, width), BF),
                pltpu.VMEM((half, 128), BF),
                pltpu.VMEM((half, width), BF),
                pltpu.VMEM((keys, width), BF),
                pltpu.VMEM((keys, width), BF),
                pltpu.VMEM((half, keys), F32),
                pltpu.VMEM((half, width), BF),
                pltpu.VMEM((heads, half, keys), BF),
                pltpu.VMEM((half, width), F32),
                pltpu.VMEM((half, width), BF),
                pltpu.VMEM((2, half, hidden // 2), BF),
                pltpu.VMEM((2, half, hidden // 2), BF),
                pltpu.VMEM((half, width), F32),
                pltpu.VMEM((half, width), F32),
                pltpu.VMEM((half, width), BF),
                pltpu.SemaphoreType.DMA((len(operands),)),
                pltpu.SemaphoreType.DMA((12,)),
                pltpu.SemaphoreType.DMA((4,)),
            ],
        ),
        out_shape=[jax.ShapeDtypeStruct(*s) for s in shapes],
        compiler_params=params(60),
        cost_estimate=cost(
            2 * half * width * (5 * width + 4 * hidden) + 4 * half * keys * width, 8 * width * hidden
        ),
        name="front",
    )(blk, *operands)


def mid_kernel(gn_hbm, h1_hbm, cot_hbm, wo_hbm, g2_hbm, gh_ref, gb_ref, ga_ref, sums_ref, *refs):
    gn_ref, h1_ref, cot_ref, wo_ref, g2_ref, sem = refs
    done(started(zip((gn_hbm, h1_hbm, cot_hbm, g2_hbm, wo_hbm), (gn_ref, h1_ref, cot_ref, g2_ref, wo_ref)), sem))
    normal, inv = normalise(h1_ref[...])
    total = gn_ref[...]
    cot = cot_ref[...].astype(F32)
    grad_hidden1 = cot + norm_back(total, normal, inv, line(g2_ref))
    gh_ref[...] = grad_hidden1
    branch = grad_hidden1.astype(BF)
    gb_ref[...] = branch
    ga_ref[...] = dot_nt(branch, wo_ref[...]).astype(BF)
    sums_ref[0:1, :] = column_sum(total * normal)
    sums_ref[1:2, :] = column_sum(total)
    sums_ref[2:3, :] = column_sum(branch.astype(F32))
    sums_ref[3:4, :] = column_sum(cot)


def mid(gn, h1, cot, wo, g2):
    half, width = h1.shape
    operands = (gn, h1, cot, wo, g2)
    shapes = [((half, width), F32), ((half, width), BF), ((half, width), BF), ((4, width), F32)]
    return pl.pallas_call(
        mid_kernel,
        grid=(1,),
        in_specs=[ANYWHERE] * 5,
        out_specs=[whole(v[0]) for v in shapes],
        out_shape=[jax.ShapeDtypeStruct(*v) for v in shapes],
        scratch_shapes=[pltpu.VMEM(v.shape, v.dtype) for v in operands] + [pltpu.SemaphoreType.DMA((5,))],
        compiler_params=params(40),
        cost_estimate=cost(1, 1),
        name="mid",
    )(*operands)


class Plan:
    def __init__(self, ndp):
        self.ndp = ndp
        self.groups = min(16, ndp)
        self.bits = self.groups.bit_length() - 1
        self.rest = ndp // self.groups
        wanted = {"feed": ((0, 1, 2, 3), (1, 2, 0, 3), (2, 0, 1, 3)), "attend": ((0, 1, 2, 3), (1, 2, 0, 3), (2, 0, 1, 3))}
        self.orders = {k: [[b for b in o if b < self.bits] for o in v] for k, v in wanted.items()}
        self.small = [b for b in (3, 2, 1, 0) if b < self.bits]

    def place(self, name, piece, p):
        code = 0
        for bit in self.orders[name][piece]:
            code = 2 * code + ((p >> bit) & 1)
        return divmod(self.groups - 1 - code, self.groups // 2)


def feed_weights_kernel(plan, own_ref, *refs):
    sources, refs = refs[:12], refs[-24:]
    outs, targets, stages = refs[:6], refs[6:18], refs[18:20]
    acc_ref, low_ref, in_sem, out_sem = refs[20:]
    n2_ref, n2o_ref, g_ref, go_ref, act_ref, acto_ref, cot_ref, coto_ref, att_ref, atto_ref, gb_ref, gbo_ref = targets
    own = own_ref[0]
    width = n2_ref.shape[1]
    cols = width // 2
    groups, per = plan.groups, plan.groups // 2
    chunk = g_ref.shape[1] // 2
    rows = width // groups
    unit = rows // 2
    at = pl.ds(pl.multiple_of(own_ref[1] * cols, 128), cols)
    pairs = list(zip(sources[:10], targets)) + [(sources[10].at[:, at], gb_ref), (sources[11].at[:, at], gbo_ref)]
    loads = started(pairs, in_sem)

    def emit(number, p, value):
        piece, slot = divmod(number, 3)
        kept, place = plan.place("feed", piece, p)
        stages[kept][piece, place, slot] = value.astype(BF)

    done(loads[:4])
    for step in range(2):
        lanes = slice(step * chunk, (step + 1) * chunk)
        acc_ref[step] = dot_tn(n2_ref[...], g_ref[:, lanes]) + dot_tn(n2o_ref[...], go_ref[:, lanes])
        for p in range(groups):
            for k in range(2):
                source = pl.multiple_of((own ^ p) * rows + k * unit, 8)
                emit(5 + 2 * step + k, p, acc_ref[step, pl.ds(source, unit), :])
    done(loads[4:])
    low_ref[...] = dot_tn(att_ref[...], gb_ref[...]) + dot_tn(atto_ref[...], gbo_ref[...])
    for p in range(groups):
        source = pl.multiple_of((own ^ p) * rows, 16)
        block = low_ref[pl.ds(source, rows), :]
        emit(4, p, jnp.concatenate([block[:unit], block[unit:]], 1))
    sent = copies([(stages[kept].at[piece], outs[2 * piece + kept]) for piece in range(3) for kept in range(2)], out_sem)
    for copy in sent[4:]:
        copy.start()
    for step in range(2):
        lanes = pl.ds(pl.multiple_of(((own // per) ^ step) * chunk, 128), chunk)
        acc_ref[2 + step] = dot_tn(act_ref[:, lanes], cot_ref[...]) + dot_tn(acto_ref[:, lanes], coto_ref[...])
        for low in range(per):
            for k in range(4):
                source = pl.multiple_of(((own % per) ^ low) * (chunk // per) + k * unit, 8)
                emit(k, step * per + low, acc_ref[2 + step, pl.ds(source, unit), :])
    for copy in sent[:4]:
        copy.start()
    done(sent)


def feed_weights(plan, own, *operands, after):
    half, width = operands[0].shape
    chunk, cols = operands[2].shape[1] // 2, width // 2
    part = jax.ShapeDtypeStruct((plan.groups // 2, 3, width // plan.groups // 2, width), BF)
    shapes = [v.shape for v in operands[:10]] + [(half, cols)] * 2

    return pl.pallas_call(
        functools.partial(feed_weights_kernel, plan),
        grid_spec=pltpu.PrefetchScalarGridSpec(
            num_scalar_prefetch=1,
            grid=(1,),
            in_specs=[ANYWHERE] * (12 + len(after)),
            out_specs=[ANYWHERE] * 6,
            scratch_shapes=[pltpu.VMEM(v, BF) for v in shapes]
            + [pltpu.VMEM((3,) + part.shape, BF)] * 2
            + [pltpu.VMEM((4, width, chunk), F32), pltpu.VMEM((width, cols), F32)]
            + [pltpu.SemaphoreType.DMA((12,)), pltpu.SemaphoreType.DMA((6,))],
        ),
        out_shape=(part,) * 6,
        compiler_params=params(40),
        cost_estimate=cost(1, 1),
        name="feed_weights",
    )(own, *operands, *after)


def attend_back_kernel(blk_ref, q_hbm, k_hbm, v_hbm, ga_hbm, p_hbm, *refs):
    outs, refs = refs[:6], refs[6:]
    q_ref, k_ref, v_ref, ga_ref, p_ref, d_ref, h_ref, sem, p_sem, out_sem = refs
    half, width = q_ref.shape
    cols = width // 2
    loads = started(
        [(q_hbm, q_ref), (k_hbm, k_ref), (v_hbm, v_ref), (ga_hbm, ga_ref)], sem
    )
    heads = p_ref.shape[0]
    per = 4
    probs_in = started([(p_hbm.at[k : k + per], p_ref.at[k : k + per]) for k in range(0, heads, per)], p_sem)
    done(loads + probs_in)
    for pair in range(heads // 2):
        lanes = slice(pair * 128, pair * 128 + 128)
        q, k, grad = q_ref[:, lanes], k_ref[:, lanes], ga_ref[:, lanes]
        dqs, dks, dvs = [], [], []
        for head in range(2):
            grad_one = jnp.where(lanes_of(grad.shape, head), grad, jnp.zeros_like(grad))
            grad_probs = dot_nt(grad_one, v_ref[:, lanes])
            low = p_ref[2 * pair + head]
            probs = low.astype(F32)
            row = jnp.sum(probs * grad_probs, -1, keepdims=True)
            grad_scores = (probs * (grad_probs - row)).astype(BF)
            dqs.append(dot_nn(grad_scores, k))
            dks.append(dot_tn(q, grad_scores))
            dvs.append(dot_tn(grad, low))
        side, at = divmod(pair * 128, cols)
        at = slice(at, at + 128)
        d_ref[side, 0, :, at] = (jnp.where(lanes_of(dqs[0].shape, 0), dqs[0], dqs[1]) * 0.125).astype(BF)
        first = lax.broadcasted_iota(jnp.int32, dks[0].shape, 0) < HD
        dk = jnp.where(first, dks[0], dks[1]).T.astype(BF)
        dv = jnp.where(first, dvs[0], dvs[1]).T.astype(BF)
        d_ref[side, 1, :, at] = dk[:half]
        d_ref[side, 2, :, at] = dv[:half]
        h_ref[side, 0, :, at] = dk[half:]
        h_ref[side, 1, :, at] = dv[half:]
    core = blk_ref[0]
    done(
        started(
            [
                (h_ref.at[1 - core], outs[0]),
                (h_ref.at[core], outs[1]),
                (d_ref.at[core], outs[2]),
                (d_ref.at[1 - core, 0], outs[3]),
                (d_ref.at[1 - core, 1], outs[4]),
                (d_ref.at[1 - core, 2], outs[5]),
            ],
            out_sem,
        )
    )


def attend_back(blk, q, k, v, probs, ga, *after):
    half, width = q.shape
    keys = k.shape[0]
    halo = keys - half
    cols = width // 2
    shapes = ((2, halo, cols),) * 2 + ((3, half, cols),) + ((half, cols),) * 3

    def body(blk_ref, *refs):
        ins, refs = refs[:5], refs[5 + len(after) :]
        attend_back_kernel(blk_ref, *ins, *refs)

    return pl.pallas_call(
        body,
        grid_spec=pltpu.PrefetchScalarGridSpec(
            num_scalar_prefetch=1,
            grid=(1,),
            in_specs=[ANYWHERE] * (5 + len(after)),
            out_specs=[ANYWHERE] * 6,
            scratch_shapes=[
                pltpu.VMEM((half, width), BF),
                pltpu.VMEM((keys, width), BF),
                pltpu.VMEM((keys, width), BF),
                pltpu.VMEM((half, width), BF),
                pltpu.VMEM(probs.shape, BF),
                pltpu.VMEM((2, 3, half, cols), BF),
                pltpu.VMEM((2, 2, halo, cols), BF),
                pltpu.SemaphoreType.DMA((4,)),
                pltpu.SemaphoreType.DMA((probs.shape[0] // 4,)),
                pltpu.SemaphoreType.DMA((6,)),
            ],
        ),
        out_shape=[jax.ShapeDtypeStruct(v, BF) for v in shapes],
        compiler_params=params(40),
        cost_estimate=cost(1, 1),
        name="attend_back",
    )(blk, q, k, v, ga, probs, *after)


def add_rows(ref, start, at, cols, extra):
    rows = pl.ds(start, extra.shape[0])
    part = ref[rows, pl.ds(at, cols)].astype(F32) + extra.astype(F32)
    ref[rows, pl.ds(at, cols)] = part.astype(BF)


def tail_kernel(plan, places, own_ref, *refs):
    sources, refs = refs[:19], refs[-30:]
    outs, gx_ref, small_mine, small_other = refs[:6], refs[6], refs[7], refs[8]
    (
        n1_ref, n1o_ref, hk_ref, ho_ref, hl_ref, mine_ref, other_ref, gj_ref, w_ref, h0_ref, gh_ref, g1_ref, pos_ref,
        sums_ref, b1_ref, acc_ref, send_ref, keep_ref, small_ref, sem, out_sem,
    ) = refs[9:]
    half, width = n1_ref.shape
    halo = hk_ref.shape[1]
    cols = width // 2
    own, blk = own_ref[0], own_ref[1]
    rows = width // plan.groups
    start = pl.multiple_of((1 - blk) * (half - halo), 16)
    start_other = pl.multiple_of(blk * (half - halo), 16)
    lanes = [[pl.multiple_of(which * width + core * cols, 128) for core in (blk, 1 - blk)] for which in range(3)]
    n1, n1o, d, hk, ho, hl = sources[:6]
    pairs = [(d.at[k], mine_ref.at[:, k * cols : (k + 1) * cols]) for k in range(3)]
    pairs += [(sources[6 + k], other_ref.at[:, k * cols : (k + 1) * cols]) for k in range(3)]
    pairs += [(n1, n1_ref), (n1o, n1o_ref), (hk, hk_ref), (ho, ho_ref)]
    pairs += [(d.at[k], gj_ref.at[:, pl.ds(lanes[k][0], cols)]) for k in range(3)]
    pairs += [(sources[9 + k], gj_ref.at[:, pl.ds(lanes[k][1], cols)]) for k in range(3)]
    pairs += [(hl, hl_ref)] + list(zip(sources[12:], (w_ref, h0_ref, gh_ref, g1_ref, pos_ref, sums_ref, b1_ref)))
    loads = started(pairs, sem)
    done(loads[:10])
    for which in range(2):
        lane = (1 + which) * cols
        add_rows(mine_ref, start, lane, cols, ho_ref[which])
        add_rows(other_ref, start_other, lane, cols, hk_ref[which])
    part = rows // 3
    stages = (send_ref, keep_ref)
    for at in (slice(0, width), slice(width, width + cols)):
        acc_ref[:, at] = dot_tn(n1_ref[...], mine_ref[:, at]) + dot_tn(n1o_ref[...], other_ref[:, at])
        for p in range(plan.groups):
            for piece in range(3):
                source = pl.multiple_of((own ^ p) * rows + piece * part, 8)
                kept, place = plan.place("attend", piece, p)
                stages[kept][piece, place, :, at] = acc_ref[pl.ds(source, part), at].astype(BF)
    sent = copies([(stages[kept].at[piece], outs[2 * piece + kept]) for piece in range(3) for kept in range(2)], out_sem)
    for copy in sent:
        copy.start()
    done(loads[10:])
    for which in range(2):
        add_rows(gj_ref, start, lanes[1 + which][0], cols, ho_ref[which])
        add_rows(gj_ref, start, lanes[1 + which][1], cols, hl_ref[which])
    total = dot_nt(gj_ref[...], w_ref[...])
    small_ref[places + 2 : places + 3, :] = column_sum(gj_ref[:, :width].astype(F32))
    small_ref[places + 3 : places + 4, :] = column_sum(gj_ref[:, 2 * width :].astype(F32))
    normal, inv = normalise(h0_ref[...])
    small_ref[places : places + 1, :] = column_sum(total * normal)
    small_ref[places + 1 : places + 2, :] = column_sum(total)
    grad = (gh_ref[...] + norm_back(total, normal, inv, line(g1_ref))).astype(BF)
    gx_ref[...] = grad
    hot = (lax.broadcasted_iota(jnp.int32, (places, half), 0) == pos_ref[...]).astype(F32).astype(BF)
    small_ref[:places, :] = dot_nn(hot, grad)
    small_ref[places + 4 : places + 8, :] = sums_ref[...]
    for k in range(4):
        small_ref[places + 8 + k : places + 9 + k, :] = b1_ref[:, k * width : (k + 1) * width]
    for ref, core in ((small_mine, blk), (small_other, 1 - blk)):
        ref[0] = small_ref[:, pl.ds(pl.multiple_of(core * cols, 128), cols)].astype(BF)
    done(sent)


def tail(plan, own, n1, n1o, d, hk, ho, hl, do, ds, w, h0, gh, g1, pos, sums, b1, places, after):
    half, width = h0.shape
    cols = width // 2
    part = jax.ShapeDtypeStruct((plan.groups // 2, width // plan.groups // 3, 3 * cols), BF)
    rest = (w, h0, gh, g1, pos, sums, b1)
    operands = (n1, n1o, d, hk, ho, hl) + tuple(do) + tuple(ds) + rest
    extra = (1, places + 12, cols)

    return pl.pallas_call(
        functools.partial(tail_kernel, plan, places),
        grid_spec=pltpu.PrefetchScalarGridSpec(
            num_scalar_prefetch=1,
            grid=(1,),
            in_specs=[ANYWHERE] * (19 + len(after)),
            out_specs=[ANYWHERE] * 6 + [whole((half, width)), whole(extra), whole(extra)],
            scratch_shapes=[pltpu.VMEM((half, width), BF)] * 2
            + [pltpu.VMEM(hk.shape, BF)] * 3
            + [pltpu.VMEM((half, 3 * cols), BF)] * 2
            + [pltpu.VMEM((half, 3 * width), BF)]
            + [pltpu.VMEM(v.shape, v.dtype) for v in rest]
            + [pltpu.VMEM((width, 3 * cols), F32)]
            + [pltpu.VMEM((3,) + part.shape, BF)] * 2
            + [pltpu.VMEM((places + 12, width), F32)]
            + [pltpu.SemaphoreType.DMA((24,)), pltpu.SemaphoreType.DMA((6,))],
        ),
        out_shape=(part,) * 6
        + (
            jax.ShapeDtypeStruct((half, width), BF),
            jax.ShapeDtypeStruct(extra, BF),
            jax.ShapeDtypeStruct(extra, BF),
        ),
        compiler_params=params(40),
        cost_estimate=cost(1, 1),
        name="tail",
    )(own, *operands, *after)


def swap(v):
    return lax.ppermute(v, "blk", [(0, 1), (1, 0)])


def across(v, ndp, flip):
    return lax.ppermute(v, "dp", [(i, i ^ flip) for i in range(ndp)])


def wide(v):
    return v.astype(F32)


def combine_kernel(plans, *refs):
    outs = refs[-len(plans) :]
    for out, plan in zip(outs, plans):
        at = 0
        for count, terms in plan:
            total = None
            for k, start in terms:
                value = refs[k][start : start + count].astype(F32)
                total = value if total is None else total + value
            out[at : at + count] = total.astype(out.dtype)
            at += count


def combine(arrays, plans, types, before=()):
    block = arrays[0].shape[1:]
    shapes = [(sum(count for count, _ in plan),) + block for plan in plans]

    def body(*refs):
        combine_kernel(plans, *refs[: len(arrays)], *refs[len(arrays) + len(before) :])

    return pl.pallas_call(
        body,
        grid=(1,),
        in_specs=[whole(v.shape) for v in arrays] + [ANYWHERE] * len(before),
        out_specs=[whole(v) for v in shapes],
        out_shape=[jax.ShapeDtypeStruct(v, t) for v, t in zip(shapes, types)],
        compiler_params=params(24),
        cost_estimate=cost(1, 1),
        name="combine",
    )(*arrays, *before)


class Trio:
    def __init__(self, plan, name, parts):
        self.plan, self.orders, self.phase = plan, plan.orders[name], 0
        self.terms = [[(parts[2 * k + 1], 0, 0)] for k in range(3)]
        self.at, self.left = 0, plan.groups // 2
        self.sent = parts[0]
        for k in range(3):
            self.terms[k].append((self.across(parts[2 * k], self.orders[k][0]), 0, 0))
        self.phase = 1

    def across(self, value, bit):
        return across(value, self.plan.ndp, self.plan.rest << bit)

    def collect(self):
        arrays, where = [], []
        for k in range(3):
            where.append([])
            for array, place, start in self.terms[k]:
                if not any(array is v for v in arrays):
                    arrays.append(array)
                index = [array is v for v in arrays].index(True)
                where[k].append((index, start + self.at - place))
        return arrays, where

    def step(self, *before):
        if self.phase >= self.plan.bits:
            return
        h = self.left // 2
        arrays, where = self.collect()
        bits = [order[self.phase] for order in self.orders]
        joined = len(set(bits)) == 1
        plans = [[(h, w)] for w in where]
        values = combine(arrays, [sum(plans, [])] if joined else plans, [BF] * 3, before)
        self.at, self.left = self.at + h, h
        self.sent = values[0]
        if joined:
            got = [self.across(values[0], bits[0])] * 3
        else:
            got = [self.across(v, bit) for v, bit in zip(values, bits)]
        for k in range(3):
            self.terms[k].append((got[k], self.at, k * h if joined else 0))
        self.phase += 1

    def totals(self, *before):
        arrays, where = self.collect()
        return combine(arrays, [[(1, w) for w in where]], [F32], before)[0]


class Everywhere:
    def __init__(self, plan, mine, other):
        self.plan, self.phase = plan, 0
        self.flips = [plan.rest << b for b in plan.small] + [1 << b for b in range(plan.rest.bit_length() - 1)] + [None]
        self.sent, self.got = mine, swap(other)

    def step(self, *before):
        if self.phase >= len(self.flips):
            return
        (self.sent,) = combine([self.sent, self.got], [[(1, [(0, 0), (1, 0)])]], [BF], before)
        flip = self.flips[self.phase]
        self.got = swap(self.sent) if flip is None else across(self.sent, self.plan.ndp, flip)
        self.phase += 1

    def both(self):
        while self.phase < len(self.flips):
            self.step()
        return self.sent, self.got


def split_feed_kernel(blk_ref, value_ref, fc2_ref, mine, other):
    unit = value_ref.shape[2]
    units = [value_ref[k // 3, k % 3] for k in range(9)]
    cols = units[0].shape[1] // 2
    for k in range(4):
        fc2_ref[k * unit : (k + 1) * unit, :] = units[k]
    low_core = blk_ref[0] == 0
    for k in range(2):
        low, high = units[5 + 2 * k], units[6 + 2 * k]
        mine[k] = jnp.where(low_core, low, high)
        other[k] = jnp.where(low_core, high, low)
    low, high = units[4][:, :cols], units[4][:, cols:]
    mine[2, :, :cols] = jnp.where(low_core, low, high)
    other[2, :, :cols] = jnp.where(low_core, high, low)
    mine[2, :, cols:] = jnp.zeros_like(low)
    other[2, :, cols:] = jnp.zeros_like(low)


def split_feed(blk, value):
    _, _, unit, width = value.shape
    shapes = [(4 * unit, width), (3, unit, width), (3, unit, width)]
    return pl.pallas_call(
        split_feed_kernel,
        grid_spec=pltpu.PrefetchScalarGridSpec(
            num_scalar_prefetch=1, grid=(1,), in_specs=[whole(value.shape)], out_specs=[whole(v) for v in shapes]
        ),
        out_shape=[jax.ShapeDtypeStruct(v, F32) for v in shapes],
        compiler_params=params(24),
        cost_estimate=cost(1, 1),
        name="split_feed",
    )(blk, value)


def join_feed_kernel(blk_ref, mine_ref, got_ref, fc1_ref, out_ref):
    width = mine_ref.shape[2]
    cols = width // 2
    for ref, core in ((mine_ref, blk_ref[0]), (got_ref, 1 - blk_ref[0])):
        for k in range(2):
            fc1_ref[:, pl.ds(pl.multiple_of((core * 2 + k) * width, 128), width)] = ref[k]
        out_ref[:, pl.ds(pl.multiple_of(core * cols, 128), cols)] = ref[2, :, :cols]


def join_feed(blk, mine, got):
    _, rows, width = mine.shape
    shapes = [(rows, 4 * width), (rows, width)]
    return pl.pallas_call(
        join_feed_kernel,
        grid_spec=pltpu.PrefetchScalarGridSpec(
            num_scalar_prefetch=1,
            grid=(1,),
            in_specs=[whole(mine.shape)] * 2,
            out_specs=[whole(v) for v in shapes],
        ),
        out_shape=[jax.ShapeDtypeStruct(v, F32) for v in shapes],
        compiler_params=params(24),
        cost_estimate=cost(1, 1),
        name="join_feed",
    )(blk, mine, got)


def join_attend_kernel(blk_ref, mine_ref, got_ref, qkv_ref):
    cols = mine_ref.shape[1] // 3
    for ref, core in ((mine_ref, blk_ref[0]), (got_ref, 1 - blk_ref[0])):
        for k in range(3):
            at = pl.ds(pl.multiple_of((2 * k + core) * cols, 128), cols)
            qkv_ref[:, at] = ref[:, k * cols : (k + 1) * cols]


def join_attend(blk, mine, got):
    shape = (mine.shape[0], 2 * mine.shape[1])
    return pl.pallas_call(
        join_attend_kernel,
        grid_spec=pltpu.PrefetchScalarGridSpec(
            num_scalar_prefetch=1, grid=(1,), in_specs=[whole(mine.shape)] * 2, out_specs=whole(shape)
        ),
        out_shape=jax.ShapeDtypeStruct(shape, F32),
        compiler_params=params(24),
        cost_estimate=cost(1, 1),
        name="join_attend",
    )(blk, mine, got)


def split_attend_kernel(counts, blk_ref, *refs):
    mine, other, whole_ref = refs[-3:]
    part = whole_ref.shape[0] // 3
    arrays, where = counts
    for piece in range(3):
        total = None
        for index, at in where[piece]:
            value = refs[index][at].astype(F32)
            total = value if total is None else total + value
        whole_ref[piece * part : (piece + 1) * part, :] = total
    half = mine.shape[0]
    low, high = whole_ref[:half, :], whole_ref[half:, :]
    low_core = blk_ref[0] == 0
    mine[...] = jnp.where(low_core, low, high)
    other[...] = jnp.where(low_core, high, low)


def split_attend(blk, trio):
    arrays, where = trio.collect()
    _, part, cols = arrays[0].shape
    shape = (3 * part // 2, cols)
    return pl.pallas_call(
        functools.partial(split_attend_kernel, (len(arrays), where)),
        grid_spec=pltpu.PrefetchScalarGridSpec(
            num_scalar_prefetch=1,
            grid=(1,),
            in_specs=[whole(v.shape) for v in arrays],
            out_specs=[whole(shape)] * 2,
            scratch_shapes=[pltpu.VMEM((3 * part, cols), F32)],
        ),
        out_shape=[jax.ShapeDtypeStruct(shape, F32)] * 2,
        compiler_params=params(24),
        cost_estimate=cost(1, 1),
        name="split_attend",
    )(blk, *arrays)


def join_small_kernel(blk_ref, mine_ref, got_ref, *outs):
    joined_ref = outs[-1]
    cols = mine_ref.shape[2]
    width = 2 * cols
    places = outs[0].shape[0]
    for ref, core in ((mine_ref, blk_ref[0]), (got_ref, 1 - blk_ref[0])):
        joined_ref[:, pl.ds(pl.multiple_of(core * cols, 128), cols)] = ref[0].astype(F32)
    outs[0][...] = joined_ref[:places, :]
    for k, out in enumerate(outs[1:9]):
        out[...] = joined_ref[places + k, :]
    for k in range(outs[9].shape[0] // width):
        outs[9][k * width : (k + 1) * width] = joined_ref[places + 8 + k, :]


def join_small(blk, mine, got, places, hidden):
    _, rows, cols = mine.shape
    width = 2 * cols
    shapes = [(places, width)] + [(width,)] * 8 + [(hidden,)]
    return pl.pallas_call(
        join_small_kernel,
        grid_spec=pltpu.PrefetchScalarGridSpec(
            num_scalar_prefetch=1,
            grid=(1,),
            in_specs=[whole(mine.shape)] * 2,
            out_specs=[whole(v) for v in shapes],
            scratch_shapes=[pltpu.VMEM((rows, width), F32)],
        ),
        out_shape=[jax.ShapeDtypeStruct(v, F32) for v in shapes],
        compiler_params=params(24),
        cost_estimate=cost(1, 1),
        name="join_small",
    )(blk, mine, got)


def behind(values, *others):
    return lax.optimization_barrier((values, others))[0]


def rest_of(plan, value, blk):
    groups = [[g * plan.rest + i for i in range(plan.rest)] for g in range(plan.groups)]
    value = lax.psum(value, "dp", axis_index_groups=groups)
    rows = value.shape[0] // (2 * plan.rest)
    return lax.dynamic_slice_in_dim(value, ((lax.axis_index("dp") % plan.rest) * 2 + blk) * rows, rows, axis=0)


def per_device(
    ndp, inputs, segments, positions, pos_table, ln1_gain, ln1_shift, qkv_weight, query_bias,
    value_bias, out_weight, out_bias, ln2_gain, ln2_shift, fc1_weight, fc1_bias, fc2_weight,
    fc2_bias, cotangent,
):
    plan = Plan(ndp)
    x, cot = inputs[0], cotangent[0]
    half, width = x.shape
    hidden = fc1_weight.shape[1]
    places = pos_table.shape[0]
    halo = next(h for h in range(SEG_MOST - 1, half + 1) if (half + h) % 128 == 0 and (half - h) % 16 == 0)
    blk = lax.axis_index("blk")
    dp = lax.axis_index("dp")
    blk1 = blk.astype(jnp.int32).reshape(1)
    own1 = (dp // plan.rest).astype(jnp.int32).reshape(1)

    x_other, seg_other, pos_other = swap(x), swap(segments), swap(positions)
    cot_other = swap(cot)
    vectors = (ln1_gain, ln1_shift, query_bias, value_bias, out_bias, ln2_gain, ln2_shift, fc1_bias, fc2_bias)
    (
        hidden0, n1, n1_other, q, k, v, att, probs, n2, grad_send, grad_keep, act_send, act_keep, result, gn2, hidden1,
        b1_grad,
    ) = front(
        plan, halo, blk1, x, x_other, segments, seg_other, positions, pos_other, cot, pos_table, vectors,
        qkv_weight, out_weight, fc1_weight, fc2_weight,
    )
    grad_other, act_other, n2_other = swap(grad_send), swap(act_send), swap(behind(n2, cot_other))
    gh1, gb, ga, sums = mid(gn2, hidden1, cot, out_weight, ln2_gain)
    att_other, gb_other = swap(att), swap(gb)
    own2 = jnp.stack([own1[0], blk1[0]])
    parts = feed_weights(
        plan, own2, n2, n2_other, grad_keep, grad_other, act_keep, act_other, cot, cot_other, att, att_other, gb, gb_other,
        after=(ga,),
    )
    feed_sums = Trio(plan, "feed", parts)
    h_send, h_keep, d_keep, *d_send = attend_back(blk1, q, k, v, probs, ga, parts[0])
    h_other, h_late = swap(h_send), swap(h_keep)
    d_other = [swap(v) for v in d_send]
    feed_sums.step(d_keep)
    *parts, grad_x, mine, other = tail(
        plan, own2, n1, n1_other, d_keep, h_keep, h_other, h_late, d_other, d_send,
        qkv_weight, hidden0, gh1, ln1_gain, positions, sums, b1_grad, places, (feed_sums.sent,),
    )
    attend_sums = Trio(plan, "attend", parts)
    small = Everywhere(plan, mine, other)
    before = grad_x
    for item in (small, feed_sums, attend_sums, small, feed_sums, attend_sums, small, attend_sums, small, small):
        item.step(before)
        before = item.sent
    unit = width // plan.groups // 2
    value = feed_sums.totals()
    attend_mine, attend_sent = split_attend(blk1, attend_sums)
    if plan.rest == 1:
        fc2_grad, feed_mine, feed_sent = split_feed(blk1, value)
        feed_got = swap(feed_sent)
        qkv_grad = join_attend(blk1, attend_mine, swap(attend_sent))
        fc1_grad, out_grad = join_feed(blk1, feed_mine, feed_got)
    else:
        units = value.reshape(9, unit, width)
        fc2_grad = rest_of(plan, lax.all_gather(units[:4].reshape(-1, width), "blk", axis=0, tiled=True), blk)
        rows = jnp.concatenate([units[5:7].reshape(-1, width), units[7:].reshape(-1, width)], 1)
        fc1_grad = rest_of(plan, lax.all_gather(rows, "blk", axis=1, tiled=True), blk)
        rows = jnp.concatenate([units[4][:, : width // 2], units[4][:, width // 2 :]], 0)
        out_grad = rest_of(plan, lax.all_gather(rows, "blk", axis=1, tiled=True), blk)
        rows = jnp.where(blk == 0, jnp.stack([attend_mine, attend_sent]), jnp.stack([attend_sent, attend_mine]))
        rows = rows.reshape(2 * unit, 3, width // 2)
        qkv_grad = rest_of(plan, lax.all_gather(rows, "blk", axis=2, tiled=True).reshape(2 * unit, -1), blk)
    table, *vec, b1_all = join_small(blk1, *small.both(), places, hidden)
    return (
        result[None], grad_x[None], table, vec[0], vec[1], qkv_grad, vec[2], vec[3], out_grad,
        vec[6], vec[4], vec[5], fc1_grad, b1_all, fc2_grad, vec[7],
    )


def solution(mesh):
    split = P("dp", "blk", None)
    ids = P("dp", "blk")
    both = P(("dp", "blk"), None)
    none = P()
    return jax.shard_map(
        functools.partial(per_device, mesh.shape["dp"]),
        mesh=mesh,
        in_specs=(split, ids, ids) + (none,) * 14 + (split,),
        out_specs=(
            split, split, none, none, none, both, none, none, both, none, none, none, both, none, both, none,
        ),
        check_vma=False,
    )
```

```python
import functools

import jax
import jax.numpy as jnp
from jax import lax
from jax.experimental import pallas as pl
from jax.experimental.pallas import tpu as pltpu
from jax.sharding import PartitionSpec as P

HD = 64
SEG_MOST = 196
EPS = 1e-06
inv_root_two = 0.7071067811865476
inv_root_two_pi = 0.3989422804014327
BF = jnp.bfloat16
F32 = jnp.float32
MIB = 1 << 20


def dot_nn(a, b):
    return jnp.dot(a, b, preferred_element_type=F32)


def dot_nt(a, b):
    return lax.dot_general(a, b, (((1,), (1,)), ((), ())), preferred_element_type=F32)


def dot_tn(a, b):
    return lax.dot_general(a, b, (((0,), (0,)), ((), ())), preferred_element_type=F32)


def normalise(hidden):
    mean = jnp.mean(hidden, -1, keepdims=True)
    centred = hidden - mean
    inv = lax.rsqrt(jnp.mean(centred * centred, -1, keepdims=True) + EPS)
    return centred * inv, inv


def norm_back(grad, normal, inv, gain):
    scaled = grad * gain
    centre = jnp.mean(scaled, -1, keepdims=True)
    along = jnp.mean(scaled * normal, -1, keepdims=True)
    return inv * (scaled - centre - normal * along)


def line(ref):
    return ref[...].reshape(1, -1)


def column_sum(v):
    return jnp.sum(v, axis=0, keepdims=True)


def params(vmem):
    return pltpu.CompilerParams(vmem_limit_bytes=vmem * MIB)


def cost(flops, bytes_accessed, trans=0):
    return pl.CostEstimate(
        flops=int(flops), bytes_accessed=int(bytes_accessed), transcendentals=int(trans)
    )


def whole(shape):
    return pl.BlockSpec(shape, lambda *_: (0,) * len(shape))


ANYWHERE = pl.BlockSpec(memory_space=pl.ANY)


def copies(pairs, sem):
    return [pltpu.make_async_copy(src, dst, sem.at[k]) for k, (src, dst) in enumerate(pairs)]


def started(pairs, sem):
    made = copies(pairs, sem)
    for copy in made:
        copy.start()
    return made


def done(made):
    for copy in made:
        copy.wait()


def lanes_of(shape, head):
    return (lax.broadcasted_iota(jnp.int32, shape, 1) % 128 < HD) == (head % 2 == 0)


def embedded(x_ref, pos_ref, table_ref):
    half = x_ref.shape[0]
    places = table_ref.shape[0]
    hot = (lax.broadcasted_iota(jnp.int32, (places, half), 0) == pos_ref[...]).astype(F32).astype(BF)
    return x_ref[...].astype(F32) + dot_tn(hot, table_ref[...])


def crop_lanes(seg_ref):
    half = seg_ref.shape[1]
    hot = (lax.broadcasted_iota(jnp.int32, (8, half), 0) == seg_ref[...]).astype(F32).astype(BF)
    eye = lax.broadcasted_iota(jnp.int32, (8, 128), 0) == lax.broadcasted_iota(jnp.int32, (8, 128), 1)
    return dot_tn(hot, eye.astype(F32).astype(BF)).astype(BF)


def front_kernel(block, blk_ref, *refs):
    sources, refs = refs[:21], refs[21:]
    (
        h0_out, n1_out, n1o_out, q_out, k_out, v_out, att_out, p_out, n2_out,
        gs_out, gk_out, as_out, ak_out, res_out, gn_out, h1_out, b1g_ref,
    ) = refs[:17]
    targets, refs = refs[17:38], refs[38:]
    (
        x_ref, xo_ref, seg_ref, sego_ref, pos_ref, poso_ref, cot_ref, table_ref,
        g1_ref, s1_ref, qb_ref, vb_ref, bo_ref, g2_ref, s2_ref, b1_ref, b2_ref, wqkv_ref, wo_ref, w1_ref, w2_ref,
    ) = targets
    (
        h0_ref, own_ref, n1_ref, n1o_ref, hoto_ref, q_ref, k_ref, v_ref, bias_ref,
        att_ref, p_ref, h1_ref, n2_ref, gp_ref, act_ref, mixed_ref, gn_ref, res_ref, bias_line_ref,
        in_sem, out_sem, late_sem,
    ) = refs
    half, width = x_ref.shape
    keys = k_ref.shape[0]
    halo = keys - half
    hidden = w1_ref.shape[1]
    blk = blk_ref[0]
    start = pl.multiple_of(blk * (half - halo), 16)
    loads = [pltpu.make_async_copy(src, dst, in_sem.at[k]) for k, (src, dst) in enumerate(zip(sources, targets))]
    outs = [
        pltpu.make_async_copy(src, dst, out_sem.at[k])
        for k, (src, dst) in enumerate(
            (
                (h0_ref, h0_out), (own_ref, n1_out), (n1o_ref, n1o_out), (q_ref, q_out), (k_ref, k_out),
                (v_ref, v_out), (att_ref, att_out), (n2_ref, n2_out), (res_ref, res_out), (gn_ref, gn_out),
                (h1_ref, h1_out), (p_ref, p_out),
            )
        )
    ]
    soon = (0, 4, 7, 1, 5, 8, 9, 17, 2, 3, 10, 11)
    then = (18, 19, 20, 6, 12, 13, 14, 15, 16)
    for k in soon:
        loads[k].start()
    for k in soon[:7]:
        loads[k].wait()
    hidden0 = embedded(x_ref, pos_ref, table_ref)
    h0_ref[...] = hidden0
    normal, _ = normalise(hidden0)
    own_ref[...] = (normal * line(g1_ref) + line(s1_ref)).astype(BF)
    n1_ref[:half, :] = own_ref[...]
    normal, _ = normalise(embedded(xo_ref, poso_ref, table_ref))
    n1o_ref[...] = (normal * line(g1_ref) + line(s1_ref)).astype(BF)
    n1_ref[half:, :] = n1o_ref[pl.ds(start, halo), :]
    for k in soon[7:]:
        loads[k].wait()
    for k in then:
        loads[k].start()
    hot = crop_lanes(seg_ref)
    hoto_ref[...] = crop_lanes(sego_ref)
    bias_ref[:, :half] = (dot_nt(hot, hot) - 1.0) * 1e9
    bias_ref[:, half:] = (dot_nt(hot, hoto_ref[pl.ds(start, halo), :]) - 1.0) * 1e9
    q = dot_nn(own_ref[...], wqkv_ref[:, :width]) + line(qb_ref)
    q_ref[...] = (q.astype(BF).astype(F32) * 0.125).astype(BF)
    k_ref[...] = dot_nn(n1_ref[...], wqkv_ref[:, width : 2 * width]).astype(BF)
    v_ref[...] = (dot_nn(n1_ref[...], wqkv_ref[:, 2 * width :]) + line(vb_ref)).astype(BF)
    for out in outs[:6]:
        out.start()
    rounds = 2
    pairs = width // 128 // rounds

    def heads(i, carry):
        for pair in range(pairs):
            cols = pl.ds(pl.multiple_of((i * pairs + pair) * 128, 128), 128)
            q = q_ref[:, cols]
            both = []
            for head in range(2):
                q_one = jnp.where(lanes_of(q.shape, head), q, jnp.zeros_like(q))
                scores = dot_nt(q_one, k_ref[:, cols]) + bias_ref[...]
                top = jnp.max(scores, -1, keepdims=True)
                weight = jnp.exp(scores - top)
                probs = (weight * (1.0 / jnp.sum(weight, -1, keepdims=True))).astype(BF)
                p_ref[2 * (i * pairs + pair) + head] = probs
                both.append(dot_nn(probs, v_ref[:, cols]))
            att_ref[:, cols] = jnp.where(lanes_of(both[0].shape, 0), both[0], both[1]).astype(BF)
        return carry

    lax.fori_loop(0, rounds, heads, 0)
    outs[6].start()
    outs[11].start()
    for k in then:
        loads[k].wait()
    hidden1 = h0_ref[...] + dot_nn(att_ref[...], wo_ref[...]) + line(bo_ref)
    h1_ref[...] = hidden1
    normal, _ = normalise(hidden1)
    n2_ref[...] = (normal * line(g2_ref) + line(s2_ref)).astype(BF)
    outs[7].start()
    outs[10].start()
    late = []
    chunk = 768
    part = chunk // 2
    mixed_ref[...] = hidden1 + line(b2_ref)
    gn_ref[...] = jnp.zeros_like(gn_ref)
    bias_line_ref[...] = line(b1_ref)

    def chunks(i, carry):
        for j in range(hidden // chunk // 2):
            first = i * (hidden // 2) + j * chunk
            at = pl.ds(pl.multiple_of(first, 128), chunk)
            pre = dot_nn(n2_ref[...], w1_ref[:, at]) + bias_line_ref[:, at]
            grad_act = dot_nt(cot_ref[...], w2_ref[at, :])
            cdf = 0.5 + 0.5 * lax.erf(pre * inv_root_two)
            act = (pre * cdf).astype(BF)
            slope = cdf + pre * jnp.exp(-0.5 * pre * pre) * inv_root_two_pi
            grad_pre = (grad_act * slope).astype(BF)
            b1g_ref[:, at] = column_sum(grad_pre.astype(F32))
            gp_ref[i, :, j * chunk : (j + 1) * chunk] = grad_pre
            mine = pl.ds(pl.multiple_of(i * (hidden // 4) + j * part, 128), part)
            for c in range(2):
                act_ref[c, :, mine] = jnp.concatenate(
                    [act[:, t : t + block] for t in range(c * block, chunk, 2 * block)], 1
                )
            mixed_ref[...] += dot_nn(act, w2_ref[at, :])
            gn_ref[...] += dot_nt(grad_pre, w1_ref[:, at])
        return carry

    lax.fori_loop(0, 2, chunks, 0)
    res_ref[...] = mixed_ref[...].astype(BF)
    for c, dst in enumerate((ak_out, as_out)):
        late.append((act_ref.at[(blk + c) % 2], dst))
    for c, dst in enumerate((gk_out, gs_out)):
        late.append((gp_ref.at[(blk + c) % 2], dst))
    late = [pltpu.make_async_copy(src, dst, late_sem.at[k]) for k, (src, dst) in enumerate(late)]
    for copy in late:
        copy.start()
    outs[8].start()
    outs[9].start()
    for out in outs:
        out.wait()
    for copy in late:
        copy.wait()


def front(plan, halo, blk, x, xo, seg, sego, pos, poso, cot, table, vectors, wqkv, wo, w1, w2):
    half, width = x.shape
    hidden = w1.shape[1]
    keys = half + halo
    heads = width // HD
    anywhere = pl.BlockSpec(memory_space=pl.ANY)
    operands = (x, xo, seg, sego, pos, poso, cot, table, *vectors, wqkv, wo, w1, w2)
    shapes = [
        ((half, width), F32),
        ((half, width), BF),
        ((half, width), BF),
        ((half, width), BF),
        ((keys, width), BF),
        ((keys, width), BF),
        ((half, width), BF),
        ((heads, half, keys), BF),
        ((half, width), BF),
        ((half, hidden // 2), BF),
        ((half, hidden // 2), BF),
        ((half, hidden // 2), BF),
        ((half, hidden // 2), BF),
        ((half, width), BF),
        ((half, width), F32),
        ((half, width), F32),
        ((1, hidden), F32),
    ]
    return pl.pallas_call(
        functools.partial(front_kernel, hidden // plan.groups // 2),
        grid_spec=pltpu.PrefetchScalarGridSpec(
            num_scalar_prefetch=1,
            grid=(1,),
            in_specs=[anywhere] * len(operands),
            out_specs=[anywhere] * 16 + [whole((1, hidden))],
            scratch_shapes=[pltpu.VMEM(v.shape, v.dtype) for v in operands]
            + [
                pltpu.VMEM((half, width), F32),
                pltpu.VMEM((half, width), BF),
                pltpu.VMEM((keys, width), BF),
                pltpu.VMEM((half, width), BF),
                pltpu.VMEM((half, 128), BF),
                pltpu.VMEM((half, width), BF),
                pltpu.VMEM((keys, width), BF),
                pltpu.VMEM((keys, width), BF),
                pltpu.VMEM((half, keys), F32),
                pltpu.VMEM((half, width), BF),
                pltpu.VMEM((heads, half, keys), BF),
                pltpu.VMEM((half, width), F32),
                pltpu.VMEM((half, width), BF),
                pltpu.VMEM((2, half, hidden // 2), BF),
                pltpu.VMEM((2, half, hidden // 2), BF),
                pltpu.VMEM((half, width), F32),
                pltpu.VMEM((half, width), F32),
                pltpu.VMEM((half, width), BF),
                pltpu.VMEM((1, hidden), F32),
                pltpu.SemaphoreType.DMA((len(operands),)),
                pltpu.SemaphoreType.DMA((12,)),
                pltpu.SemaphoreType.DMA((4,)),
            ],
        ),
        out_shape=[jax.ShapeDtypeStruct(*s) for s in shapes],
        compiler_params=params(60),
        cost_estimate=cost(
            2 * half * width * (5 * width + 4 * hidden) + 4 * half * keys * width, 8 * width * hidden
        ),
        name="front",
    )(blk, *operands)


def mid_kernel(gn_hbm, h1_hbm, cot_hbm, wo_hbm, g2_hbm, gh_ref, gb_ref, ga_ref, sums_ref, *refs):
    gn_ref, h1_ref, cot_ref, wo_ref, g2_ref, sem = refs
    done(started(zip((gn_hbm, h1_hbm, cot_hbm, g2_hbm, wo_hbm), (gn_ref, h1_ref, cot_ref, g2_ref, wo_ref)), sem))
    normal, inv = normalise(h1_ref[...])
    total = gn_ref[...]
    cot = cot_ref[...].astype(F32)
    grad_hidden1 = cot + norm_back(total, normal, inv, line(g2_ref))
    gh_ref[...] = grad_hidden1
    branch = grad_hidden1.astype(BF)
    gb_ref[...] = branch
    ga_ref[...] = dot_nt(branch, wo_ref[...]).astype(BF)
    sums_ref[0:1, :] = column_sum(total * normal)
    sums_ref[1:2, :] = column_sum(total)
    sums_ref[2:3, :] = column_sum(branch.astype(F32))
    sums_ref[3:4, :] = column_sum(cot)


def mid(gn, h1, cot, wo, g2):
    half, width = h1.shape
    operands = (gn, h1, cot, wo, g2)
    shapes = [((half, width), F32), ((half, width), BF), ((half, width), BF), ((4, width), F32)]
    return pl.pallas_call(
        mid_kernel,
        grid=(1,),
        in_specs=[ANYWHERE] * 5,
        out_specs=[whole(v[0]) for v in shapes],
        out_shape=[jax.ShapeDtypeStruct(*v) for v in shapes],
        scratch_shapes=[pltpu.VMEM(v.shape, v.dtype) for v in operands] + [pltpu.SemaphoreType.DMA((5,))],
        compiler_params=params(60),
        cost_estimate=cost(1, 1),
        name="mid",
    )(*operands)


class Plan:
    def __init__(self, ndp):
        self.ndp = ndp
        self.groups = min(16, ndp)
        self.bits = self.groups.bit_length() - 1
        self.rest = ndp // self.groups
        wanted = {"feed": ((0, 1, 2, 3), (1, 2, 0, 3), (2, 0, 1, 3)), "attend": ((0, 1, 2, 3), (1, 0, 2, 3))}
        self.orders = {k: [[b for b in o if b < self.bits] for o in v] for k, v in wanted.items()}
        self.small = [b for b in (3, 2, 1, 0) if b < self.bits]

    def place(self, name, piece, p):
        code = 0
        for bit in self.orders[name][piece]:
            code = 2 * code + ((p >> bit) & 1)
        return divmod(self.groups - 1 - code, self.groups // 2)


def feed_weights_kernel(plan, own_ref, blk_ref, *refs):
    sources, refs = refs[:12], refs[-24:]
    outs, targets, stages = refs[:6], refs[6:18], refs[18:20]
    acc_ref, low_ref, in_sem, out_sem = refs[20:]
    n2_ref, n2o_ref, g_ref, go_ref, act_ref, acto_ref, cot_ref, coto_ref, att_ref, atto_ref, gb_ref, gbo_ref = targets
    own = own_ref[0]
    width = n2_ref.shape[1]
    cols = width // 2
    groups, per = plan.groups, plan.groups // 2
    chunk = g_ref.shape[1] // 2
    rows = width // groups
    unit = rows // 2
    at = pl.ds(pl.multiple_of(blk_ref[0] * cols, 128), cols)
    pairs = list(zip(sources[:10], targets)) + [(sources[10].at[:, at], gb_ref), (sources[11].at[:, at], gbo_ref)]
    loads = started(pairs, in_sem)

    def emit(number, p, value):
        piece, slot = divmod(number, 3)
        kept, place = plan.place("feed", piece, p)
        stages[kept][piece, place, slot] = value.astype(BF)

    done(loads[:4])
    for step in range(2):
        lanes = slice(step * chunk, (step + 1) * chunk)
        acc_ref[step] = dot_tn(n2_ref[...], g_ref[:, lanes]) + dot_tn(n2o_ref[...], go_ref[:, lanes])
        for p in range(groups):
            for k in range(2):
                source = pl.multiple_of((own ^ p) * rows + k * unit, 8)
                emit(5 + 2 * step + k, p, acc_ref[step, pl.ds(source, unit), :])
    done(loads[4:])
    low_ref[...] = dot_tn(att_ref[...], gb_ref[...]) + dot_tn(atto_ref[...], gbo_ref[...])
    for p in range(groups):
        source = pl.multiple_of((own ^ p) * rows, 16)
        block = low_ref[pl.ds(source, rows), :]
        emit(4, p, jnp.concatenate([block[:unit], block[unit:]], 1))
    sent = copies([(stages[kept].at[piece], outs[2 * piece + kept]) for piece in range(3) for kept in range(2)], out_sem)
    for copy in sent[4:]:
        copy.start()
    for step in range(2):
        lanes = pl.ds(pl.multiple_of(((own // per) ^ step) * chunk, 128), chunk)
        acc_ref[2 + step] = dot_tn(act_ref[:, lanes], cot_ref[...]) + dot_tn(acto_ref[:, lanes], coto_ref[...])
        for low in range(per):
            for k in range(4):
                source = pl.multiple_of(((own % per) ^ low) * (chunk // per) + k * unit, 8)
                emit(k, step * per + low, acc_ref[2 + step, pl.ds(source, unit), :])
    for copy in sent[:4]:
        copy.start()
    done(sent)


def feed_weights(plan, own, blk, *operands):
    half, width = operands[0].shape
    chunk, cols = operands[2].shape[1] // 2, width // 2
    part = jax.ShapeDtypeStruct((plan.groups // 2, 3, width // plan.groups // 2, width), BF)
    shapes = [v.shape for v in operands[:10]] + [(half, cols)] * 2

    return pl.pallas_call(
        functools.partial(feed_weights_kernel, plan),
        grid_spec=pltpu.PrefetchScalarGridSpec(
            num_scalar_prefetch=2,
            grid=(1,),
            in_specs=[ANYWHERE] * 12,
            out_specs=[ANYWHERE] * 6,
            scratch_shapes=[pltpu.VMEM(v, BF) for v in shapes]
            + [pltpu.VMEM((3,) + part.shape, BF)] * 2
            + [pltpu.VMEM((4, width, chunk), F32), pltpu.VMEM((width, cols), F32)]
            + [pltpu.SemaphoreType.DMA((12,)), pltpu.SemaphoreType.DMA((6,))],
        ),
        out_shape=(part,) * 6,
        compiler_params=params(60),
        cost_estimate=cost(1, 1),
        name="feed_weights",
    )(own, blk, *operands)


def attend_back_kernel(blk_ref, q_hbm, k_hbm, v_hbm, ga_hbm, p_hbm, *refs):
    outs, refs = refs[:6], refs[6:]
    q_ref, k_ref, v_ref, ga_ref, p_ref, d_ref, h_ref, sem, p_sem, out_sem = refs
    half, width = q_ref.shape
    cols = width // 2
    loads = started(
        [(q_hbm, q_ref), (k_hbm, k_ref), (v_hbm, v_ref), (ga_hbm, ga_ref)], sem
    )
    heads = p_ref.shape[0]
    per = 4
    probs_in = started([(p_hbm.at[k : k + per], p_ref.at[k : k + per]) for k in range(0, heads, per)], p_sem)
    done(loads + probs_in)
    pairs = heads // 4

    def one_side(side, carry):
        for pair in range(pairs):
            lanes = pl.ds(pl.multiple_of(side * cols + pair * 128, 128), 128)
            at = slice(pair * 128, pair * 128 + 128)
            q, k, grad = q_ref[:, lanes], k_ref[:, lanes], ga_ref[:, lanes]
            dqs, dks, dvs = [], [], []
            for head in range(2):
                grad_one = jnp.where(lanes_of(grad.shape, head), grad, jnp.zeros_like(grad))
                grad_probs = dot_nt(grad_one, v_ref[:, lanes])
                low = p_ref[2 * (side * pairs + pair) + head]
                probs = low.astype(F32)
                row = jnp.sum(probs * grad_probs, -1, keepdims=True)
                grad_scores = (probs * (grad_probs - row)).astype(BF)
                dqs.append(dot_nn(grad_scores, k))
                dks.append(dot_tn(q, grad_scores))
                dvs.append(dot_tn(grad, low))
            d_ref[side, 0, :, at] = (jnp.where(lanes_of(dqs[0].shape, 0), dqs[0], dqs[1]) * 0.125).astype(BF)
            first = lax.broadcasted_iota(jnp.int32, dks[0].shape, 0) < HD
            dk = jnp.where(first, dks[0], dks[1]).T.astype(BF)
            dv = jnp.where(first, dvs[0], dvs[1]).T.astype(BF)
            d_ref[side, 1, :, at] = dk[:half]
            d_ref[side, 2, :, at] = dv[:half]
            h_ref[side, 0, :, at] = dk[half:]
            h_ref[side, 1, :, at] = dv[half:]
        return carry

    lax.fori_loop(0, 2, one_side, 0)
    core = blk_ref[0]
    done(
        started(
            [
                (h_ref.at[1 - core], outs[0]),
                (h_ref.at[core], outs[1]),
                (d_ref.at[core], outs[2]),
                (d_ref.at[1 - core, 0], outs[3]),
                (d_ref.at[1 - core, 1], outs[4]),
                (d_ref.at[1 - core, 2], outs[5]),
            ],
            out_sem,
        )
    )


def attend_back(blk, q, k, v, probs, ga, *after):
    half, width = q.shape
    keys = k.shape[0]
    halo = keys - half
    cols = width // 2
    shapes = ((2, halo, cols),) * 2 + ((3, half, cols),) + ((half, cols),) * 3

    def body(blk_ref, *refs):
        ins, refs = refs[:5], refs[5 + len(after) :]
        attend_back_kernel(blk_ref, *ins, *refs)

    return pl.pallas_call(
        body,
        grid_spec=pltpu.PrefetchScalarGridSpec(
            num_scalar_prefetch=1,
            grid=(1,),
            in_specs=[ANYWHERE] * (5 + len(after)),
            out_specs=[ANYWHERE] * 6,
            scratch_shapes=[
                pltpu.VMEM((half, width), BF),
                pltpu.VMEM((keys, width), BF),
                pltpu.VMEM((keys, width), BF),
                pltpu.VMEM((half, width), BF),
                pltpu.VMEM(probs.shape, BF),
                pltpu.VMEM((2, 3, half, cols), BF),
                pltpu.VMEM((2, 2, halo, cols), BF),
                pltpu.SemaphoreType.DMA((4,)),
                pltpu.SemaphoreType.DMA((probs.shape[0] // 4,)),
                pltpu.SemaphoreType.DMA((6,)),
            ],
        ),
        out_shape=[jax.ShapeDtypeStruct(v, BF) for v in shapes],
        compiler_params=params(60),
        cost_estimate=cost(1, 1),
        name="attend_back",
    )(blk, q, k, v, ga, probs, *after)


def add_rows(ref, start, at, cols, extra):
    rows = pl.ds(start, extra.shape[0])
    part = ref[rows, pl.ds(at, cols)].astype(F32) + extra.astype(F32)
    ref[rows, pl.ds(at, cols)] = part.astype(BF)


def attend_weights_kernel(plan, own_ref, blk_ref, *refs):
    count = len(plan.orders["attend"])
    sources, outs, refs = refs[:8], refs[8 : 8 + 2 * count], refs[8 + 2 * count :]
    n1_ref, n1o_ref, hk_ref, ho_ref, mine_ref, other_ref, acc_ref, send_ref, keep_ref, sem, out_sem = refs
    half, width = n1_ref.shape
    halo = hk_ref.shape[1]
    cols = width // 2
    own, blk = own_ref[0], blk_ref[0]
    rows = width // plan.groups
    start = pl.multiple_of((1 - blk) * (half - halo), 16)
    start_other = pl.multiple_of(blk * (half - halo), 16)
    n1, n1o, d, hk, ho = sources[:5]
    pairs = [(d.at[k], mine_ref.at[:, k * cols : (k + 1) * cols]) for k in range(3)]
    pairs += [(sources[5 + k], other_ref.at[:, k * cols : (k + 1) * cols]) for k in range(3)]
    pairs += [(n1, n1_ref), (n1o, n1o_ref), (hk, hk_ref), (ho, ho_ref)]
    done(started(pairs, sem))
    for which in range(2):
        lane = (1 + which) * cols
        add_rows(mine_ref, start, lane, cols, ho_ref[which])
        add_rows(other_ref, start_other, lane, cols, hk_ref[which])
    part = rows // count
    stages = (send_ref, keep_ref)
    for at in (slice(0, width), slice(width, width + cols)):
        acc_ref[:, at] = dot_tn(n1_ref[...], mine_ref[:, at]) + dot_tn(n1o_ref[...], other_ref[:, at])
        for p in range(plan.groups):
            for piece in range(count):
                source = pl.multiple_of((own ^ p) * rows + piece * part, 8)
                kept, place = plan.place("attend", piece, p)
                stages[kept][piece, place, :, at] = acc_ref[pl.ds(source, part), at].astype(BF)
    done(
        started(
            [(stages[kept].at[piece], outs[2 * piece + kept]) for piece in range(count) for kept in range(2)], out_sem
        )
    )


def attend_weights(plan, own, blk, n1, n1o, d, hk, ho, do):
    half, width = n1.shape
    cols = width // 2
    count = len(plan.orders["attend"])
    part = jax.ShapeDtypeStruct((plan.groups // 2, width // plan.groups // count, 3 * cols), BF)
    return pl.pallas_call(
        functools.partial(attend_weights_kernel, plan),
        grid_spec=pltpu.PrefetchScalarGridSpec(
            num_scalar_prefetch=2,
            grid=(1,),
            in_specs=[ANYWHERE] * 8,
            out_specs=[ANYWHERE] * (2 * count),
            scratch_shapes=[pltpu.VMEM((half, width), BF)] * 2
            + [pltpu.VMEM(hk.shape, BF)] * 2
            + [pltpu.VMEM((half, 3 * cols), BF)] * 2
            + [pltpu.VMEM((width, 3 * cols), F32)]
            + [pltpu.VMEM((count,) + part.shape, BF)] * 2
            + [pltpu.SemaphoreType.DMA((10,)), pltpu.SemaphoreType.DMA((2 * count,))],
        ),
        out_shape=(part,) * (2 * count),
        compiler_params=params(60),
        cost_estimate=cost(1, 1),
        name="attend_weights",
    )(own, blk, n1, n1o, d, hk, ho, *do)


def front_back_kernel(places, blk_ref, *refs):
    sources, refs = refs[:13], refs[13:]
    gx_ref, small_mine, small_other = refs[:3]
    gj_ref, w_ref, h0_ref, gh_ref, g1_ref, pos_ref, sums_ref, b1_ref, ho_ref, hl_ref, small_ref, sem = refs[3:]
    half, width = h0_ref.shape
    halo = ho_ref.shape[1]
    cols = width // 2
    blk = blk_ref[0]
    start = pl.multiple_of((1 - blk) * (half - halo), 16)
    lanes = [[pl.multiple_of(which * width + core * cols, 128) for core in (blk, 1 - blk)] for which in range(3)]
    pairs = [(sources[0].at[k], gj_ref.at[:, pl.ds(lanes[k][0], cols)]) for k in range(3)]
    pairs += [(sources[1 + k], gj_ref.at[:, pl.ds(lanes[k][1], cols)]) for k in range(3)]
    pairs += list(zip(sources[4:], (ho_ref, hl_ref, w_ref, h0_ref, gh_ref, g1_ref, pos_ref, sums_ref, b1_ref)))
    loads = started(pairs, sem)
    done(loads[:9])
    for which in range(2):
        add_rows(gj_ref, start, lanes[1 + which][0], cols, ho_ref[which])
        add_rows(gj_ref, start, lanes[1 + which][1], cols, hl_ref[which])
    done(loads[9:])
    total = dot_nt(gj_ref[...], w_ref[...])
    small_ref[places + 2 : places + 3, :] = column_sum(gj_ref[:, :width].astype(F32))
    small_ref[places + 3 : places + 4, :] = column_sum(gj_ref[:, 2 * width :].astype(F32))
    normal, inv = normalise(h0_ref[...])
    small_ref[places : places + 1, :] = column_sum(total * normal)
    small_ref[places + 1 : places + 2, :] = column_sum(total)
    grad = (gh_ref[...] + norm_back(total, normal, inv, line(g1_ref))).astype(BF)
    gx_ref[...] = grad
    hot = (lax.broadcasted_iota(jnp.int32, (places, half), 0) == pos_ref[...]).astype(F32).astype(BF)
    small_ref[:places, :] = dot_nn(hot, grad)
    small_ref[places + 4 : places + 8, :] = sums_ref[...]
    for k in range(4):
        small_ref[places + 8 + k : places + 9 + k, :] = b1_ref[:, k * width : (k + 1) * width]
    for ref, core in ((small_mine, blk), (small_other, 1 - blk)):
        ref[0] = small_ref[:, pl.ds(pl.multiple_of(core * cols, 128), cols)].astype(BF)


def front_back(blk, d, ds, ho, hl, w, h0, gh, g1, pos, sums, b1, places):
    half, width = h0.shape
    extra = (1, places + 12, width // 2)
    rest = (w, h0, gh, g1, pos, sums, b1, ho, hl)
    return pl.pallas_call(
        functools.partial(front_back_kernel, places),
        grid_spec=pltpu.PrefetchScalarGridSpec(
            num_scalar_prefetch=1,
            grid=(1,),
            in_specs=[ANYWHERE] * 13,
            out_specs=[whole((half, width)), whole(extra), whole(extra)],
            scratch_shapes=[pltpu.VMEM((half, 3 * width), BF)]
            + [pltpu.VMEM(v.shape, v.dtype) for v in rest]
            + [pltpu.VMEM((places + 12, width), F32), pltpu.SemaphoreType.DMA((15,))],
        ),
        out_shape=(
            jax.ShapeDtypeStruct((half, width), BF),
            jax.ShapeDtypeStruct(extra, BF),
            jax.ShapeDtypeStruct(extra, BF),
        ),
        compiler_params=params(60),
        cost_estimate=cost(1, 1),
        name="front_back",
    )(blk, d, *ds, ho, hl, *rest[:7])


def swap(v):
    return lax.ppermute(v, "blk", [(0, 1), (1, 0)])


def across(v, ndp, flip):
    return lax.ppermute(v, "dp", [(i, i ^ flip) for i in range(ndp)])


def wide(v):
    return v.astype(F32)


def combine_kernel(plans, *refs):
    outs = refs[-len(plans) :]
    used = 0
    for out, plan in zip(outs, plans):
        at = 0
        for count, terms in plan:
            total = refs[used][...].astype(F32)
            for ref in refs[used + 1 : used + terms]:
                total = total + ref[...].astype(F32)
            used += terms
            out[at : at + count] = total.astype(out.dtype)
            at += count


def combine(arrays, plans, types, before=()):
    block = arrays[0].shape[1:]
    shapes = [(sum(count for count, _ in plan),) + block for plan in plans]
    if before:
        arrays = [behind(arrays[0], *before)] + list(arrays[1:])
    operands, specs, counts = [], [], []
    for plan in plans:
        counts.append([])
        for count, terms in plan:
            counts[-1].append((count, len(terms)))
            for index, start in terms:
                operands.append(arrays[index])
                specs.append(
                    pl.BlockSpec(
                        (count,) + block, functools.partial(lambda at, i: (at,) + (0,) * len(block), start // count)
                    )
                )
    return pl.pallas_call(
        functools.partial(combine_kernel, counts),
        grid=(1,),
        in_specs=specs,
        out_specs=[whole(v) for v in shapes],
        out_shape=[jax.ShapeDtypeStruct(v, t) for v, t in zip(shapes, types)],
        compiler_params=params(24),
        cost_estimate=cost(1, 1),
        name="combine",
    )(*operands)


class Pieces:
    def __init__(self, plan, name, parts):
        self.plan, self.orders, self.phase = plan, plan.orders[name], 0
        self.terms = [[(parts[2 * k + 1], 0, 0)] for k in range(len(self.orders))]
        self.at, self.left = 0, plan.groups // 2
        self.sent = parts[0]
        for k in range(len(self.orders)):
            self.terms[k].append((self.across(parts[2 * k], self.orders[k][0]), 0, 0))
        self.phase = 1

    def across(self, value, bit):
        return across(value, self.plan.ndp, self.plan.rest << bit)

    def collect(self):
        arrays, where = [], []
        for k in range(len(self.orders)):
            where.append([])
            for array, place, start in self.terms[k]:
                if not any(array is v for v in arrays):
                    arrays.append(array)
                index = [array is v for v in arrays].index(True)
                where[k].append((index, start + self.at - place))
        return arrays, where

    def step(self, *before):
        if self.phase >= self.plan.bits:
            return
        h = self.left // 2
        arrays, where = self.collect()
        bits = [order[self.phase] for order in self.orders]
        joined = len(set(bits)) == 1
        plans = [[(h, w)] for w in where]
        values = combine(arrays, [sum(plans, [])] if joined else plans, [BF] * len(self.orders), before)
        self.at, self.left = self.at + h, h
        self.sent = values[0]
        if joined:
            got = [self.across(values[0], bits[0])] * len(bits)
        else:
            got = [self.across(v, bit) for v, bit in zip(values, bits)]
        for k in range(len(self.orders)):
            self.terms[k].append((got[k], self.at, k * h if joined else 0))
        self.phase += 1

    def totals(self, *before):
        arrays, where = self.collect()
        return combine(arrays, [[(1, w) for w in where]], [F32], before)[0]


class Everywhere:
    def __init__(self, plan, mine, other):
        self.plan, self.phase = plan, 0
        self.flips = [plan.rest << b for b in plan.small] + [1 << b for b in range(plan.rest.bit_length() - 1)] + [None]
        self.sent, self.got = mine, swap(other)

    def step(self, *before):
        if self.phase >= len(self.flips):
            return
        (self.sent,) = combine([self.sent, self.got], [[(1, [(0, 0), (1, 0)])]], [BF], before)
        flip = self.flips[self.phase]
        self.got = swap(self.sent) if flip is None else across(self.sent, self.plan.ndp, flip)
        self.phase += 1

    def both(self):
        while self.phase < len(self.flips):
            self.step()
        return self.sent, self.got


def split_feed_kernel(blk_ref, value_ref, fc2_ref, mine, other):
    unit = value_ref.shape[2]
    units = [value_ref[k // 3, k % 3] for k in range(9)]
    cols = units[0].shape[1] // 2
    for k in range(4):
        fc2_ref[k * unit : (k + 1) * unit, :] = units[k]
    low_core = blk_ref[0] == 0
    for k in range(2):
        low, high = units[5 + 2 * k], units[6 + 2 * k]
        mine[k] = jnp.where(low_core, low, high)
        other[k] = jnp.where(low_core, high, low)
    low, high = units[4][:, :cols], units[4][:, cols:]
    mine[2, :, :cols] = jnp.where(low_core, low, high)
    other[2, :, :cols] = jnp.where(low_core, high, low)
    mine[2, :, cols:] = jnp.zeros_like(low)
    other[2, :, cols:] = jnp.zeros_like(low)


def split_feed(blk, value):
    _, _, unit, width = value.shape
    shapes = [(4 * unit, width), (3, unit, width), (3, unit, width)]
    return pl.pallas_call(
        split_feed_kernel,
        grid_spec=pltpu.PrefetchScalarGridSpec(
            num_scalar_prefetch=1, grid=(1,), in_specs=[whole(value.shape)], out_specs=[whole(v) for v in shapes]
        ),
        out_shape=[jax.ShapeDtypeStruct(v, F32) for v in shapes],
        compiler_params=params(24),
        cost_estimate=cost(1, 1),
        name="split_feed",
    )(blk, value)


def join_feed_kernel(blk_ref, mine_ref, got_ref, fc1_ref, out_ref):
    width = mine_ref.shape[2]
    cols = width // 2
    for ref, core in ((mine_ref, blk_ref[0]), (got_ref, 1 - blk_ref[0])):
        for k in range(2):
            fc1_ref[:, pl.ds(pl.multiple_of((core * 2 + k) * width, 128), width)] = ref[k]
        out_ref[:, pl.ds(pl.multiple_of(core * cols, 128), cols)] = ref[2, :, :cols]


def join_feed(blk, mine, got):
    _, rows, width = mine.shape
    shapes = [(rows, 4 * width), (rows, width)]
    return pl.pallas_call(
        join_feed_kernel,
        grid_spec=pltpu.PrefetchScalarGridSpec(
            num_scalar_prefetch=1,
            grid=(1,),
            in_specs=[whole(mine.shape)] * 2,
            out_specs=[whole(v) for v in shapes],
        ),
        out_shape=[jax.ShapeDtypeStruct(v, F32) for v in shapes],
        compiler_params=params(24),
        cost_estimate=cost(1, 1),
        name="join_feed",
    )(blk, mine, got)


def join_attend_kernel(blk_ref, mine_ref, got_ref, qkv_ref):
    cols = mine_ref.shape[1] // 3
    for ref, core in ((mine_ref, blk_ref[0]), (got_ref, 1 - blk_ref[0])):
        for k in range(3):
            at = pl.ds(pl.multiple_of((2 * k + core) * cols, 128), cols)
            qkv_ref[:, at] = ref[:, k * cols : (k + 1) * cols]


def join_attend(blk, mine, got):
    shape = (mine.shape[0], 2 * mine.shape[1])
    return pl.pallas_call(
        join_attend_kernel,
        grid_spec=pltpu.PrefetchScalarGridSpec(
            num_scalar_prefetch=1, grid=(1,), in_specs=[whole(mine.shape)] * 2, out_specs=whole(shape)
        ),
        out_shape=jax.ShapeDtypeStruct(shape, F32),
        compiler_params=params(24),
        cost_estimate=cost(1, 1),
        name="join_attend",
    )(blk, mine, got)


def split_attend_kernel(counts, blk_ref, *refs):
    mine, other, whole_ref = refs[-3:]
    part = whole_ref.shape[0] // len(counts)
    used = 0
    for piece, terms in enumerate(counts):
        total = refs[used][0].astype(F32)
        for ref in refs[used + 1 : used + terms]:
            total = total + ref[0].astype(F32)
        used += terms
        whole_ref[piece * part : (piece + 1) * part, :] = total
    half = mine.shape[0]
    low, high = whole_ref[:half, :], whole_ref[half:, :]
    low_core = blk_ref[0] == 0
    mine[...] = jnp.where(low_core, low, high)
    other[...] = jnp.where(low_core, high, low)


def split_attend(blk, pieces):
    arrays, where = pieces.collect()
    _, part, cols = arrays[0].shape
    shape = (len(where) * part // 2, cols)
    places = [(index, at) for terms in where for index, at in terms]
    return pl.pallas_call(
        functools.partial(split_attend_kernel, [len(terms) for terms in where]),
        grid_spec=pltpu.PrefetchScalarGridSpec(
            num_scalar_prefetch=1,
            grid=(1,),
            in_specs=[
                pl.BlockSpec((1, part, cols), functools.partial(lambda at, i, b: (at, 0, 0), at)) for _, at in places
            ],
            out_specs=[whole(shape)] * 2,
            scratch_shapes=[pltpu.VMEM((len(where) * part, cols), F32)],
        ),
        out_shape=[jax.ShapeDtypeStruct(shape, F32)] * 2,
        compiler_params=params(24),
        cost_estimate=cost(1, 1),
        name="split_attend",
    )(blk, *[arrays[index] for index, _ in places])


def join_small_kernel(blk_ref, mine_ref, got_ref, *outs):
    joined_ref = outs[-1]
    cols = mine_ref.shape[2]
    width = 2 * cols
    places = outs[0].shape[0]
    for ref, core in ((mine_ref, blk_ref[0]), (got_ref, 1 - blk_ref[0])):
        joined_ref[:, pl.ds(pl.multiple_of(core * cols, 128), cols)] = ref[0].astype(F32)
    outs[0][...] = joined_ref[:places, :]
    for k, out in enumerate(outs[1:9]):
        out[...] = joined_ref[places + k, :]
    for k in range(outs[9].shape[0] // width):
        outs[9][k * width : (k + 1) * width] = joined_ref[places + 8 + k, :]


def join_small(blk, mine, got, places, hidden):
    _, rows, cols = mine.shape
    width = 2 * cols
    shapes = [(places, width)] + [(width,)] * 8 + [(hidden,)]
    return pl.pallas_call(
        join_small_kernel,
        grid_spec=pltpu.PrefetchScalarGridSpec(
            num_scalar_prefetch=1,
            grid=(1,),
            in_specs=[whole(mine.shape)] * 2,
            out_specs=[whole(v) for v in shapes],
            scratch_shapes=[pltpu.VMEM((rows, width), F32)],
        ),
        out_shape=[jax.ShapeDtypeStruct(v, F32) for v in shapes],
        compiler_params=params(24),
        cost_estimate=cost(1, 1),
        name="join_small",
    )(blk, mine, got)


def behind(values, *others):
    return lax.optimization_barrier((values, others))[0]


def rest_of(plan, value, blk):
    groups = [[g * plan.rest + i for i in range(plan.rest)] for g in range(plan.groups)]
    value = lax.psum(value, "dp", axis_index_groups=groups)
    rows = value.shape[0] // (2 * plan.rest)
    return lax.dynamic_slice_in_dim(value, ((lax.axis_index("dp") % plan.rest) * 2 + blk) * rows, rows, axis=0)


def per_device(
    ndp, inputs, segments, positions, pos_table, ln1_gain, ln1_shift, qkv_weight, query_bias,
    value_bias, out_weight, out_bias, ln2_gain, ln2_shift, fc1_weight, fc1_bias, fc2_weight,
    fc2_bias, cotangent,
):
    plan = Plan(ndp)
    x, cot = inputs[0], cotangent[0]
    half, width = x.shape
    hidden = fc1_weight.shape[1]
    places = pos_table.shape[0]
    halo = next(h for h in range(SEG_MOST - 1, half + 1) if (half + h) % 128 == 0 and (half - h) % 16 == 0)
    blk = lax.axis_index("blk")
    dp = lax.axis_index("dp")
    blk1 = blk.astype(jnp.int32).reshape(1)
    own1 = (dp // plan.rest).astype(jnp.int32).reshape(1)

    x_other, seg_other, pos_other = swap(x), swap(segments), swap(positions)
    cot_other = swap(cot)
    vectors = (ln1_gain, ln1_shift, query_bias, value_bias, out_bias, ln2_gain, ln2_shift, fc1_bias, fc2_bias)
    (
        hidden0, n1, n1_other, q, k, v, att, probs, n2, grad_send, grad_keep, act_send, act_keep, result, gn2, hidden1,
        b1_grad,
    ) = front(
        plan, halo, blk1, x, x_other, segments, seg_other, positions, pos_other, cot, pos_table, vectors,
        qkv_weight, out_weight, fc1_weight, fc2_weight,
    )
    grad_other, act_other, n2_other = swap(grad_send), swap(act_send), swap(behind(n2, cot_other))
    gh1, gb, ga, sums = mid(gn2, hidden1, cot, out_weight, ln2_gain)
    att_other, gb_other = swap(att), swap(gb)
    parts = feed_weights(
        plan, own1, blk1, behind(n2, ga), n2_other, grad_keep, grad_other, act_keep, act_other, cot, cot_other, att, att_other, gb, gb_other,
    )
    feed_sums = Pieces(plan, "feed", parts)
    h_send, h_keep, d_keep, *d_send = attend_back(blk1, behind(q, parts[0]), k, v, probs, ga)
    h_other, h_late = swap(h_send), swap(h_keep)
    d_other = [swap(v) for v in d_send]
    grad_x, mine, other = front_back(
        blk1, d_keep, d_send, h_other, h_late, qkv_weight, hidden0, gh1, ln1_gain, positions, sums, b1_grad, places
    )
    small = Everywhere(plan, mine, other)
    feed_sums.step(grad_x)
    small.step(feed_sums.sent)
    parts = attend_weights(
        plan, own1, blk1, behind(n1, small.sent), n1_other, d_keep, h_keep, h_other, d_other
    )
    attend_sums = Pieces(plan, "attend", parts)
    before = parts[0]
    for item in (small, feed_sums, attend_sums, small, feed_sums, attend_sums, small, attend_sums, small):
        item.step(before)
        before = item.sent
    unit = width // plan.groups // 2
    value = feed_sums.totals()
    attend_mine, attend_sent = split_attend(blk1, attend_sums)
    if plan.rest == 1:
        fc2_grad, feed_mine, feed_sent = split_feed(blk1, value)
        feed_got = swap(feed_sent)
        qkv_grad = join_attend(blk1, attend_mine, swap(attend_sent))
        fc1_grad, out_grad = join_feed(blk1, feed_mine, feed_got)
    else:
        units = value.reshape(9, unit, width)
        fc2_grad = rest_of(plan, lax.all_gather(units[:4].reshape(-1, width), "blk", axis=0, tiled=True), blk)
        rows = jnp.concatenate([units[5:7].reshape(-1, width), units[7:].reshape(-1, width)], 1)
        fc1_grad = rest_of(plan, lax.all_gather(rows, "blk", axis=1, tiled=True), blk)
        rows = jnp.concatenate([units[4][:, : width // 2], units[4][:, width // 2 :]], 0)
        out_grad = rest_of(plan, lax.all_gather(rows, "blk", axis=1, tiled=True), blk)
        rows = jnp.where(blk == 0, jnp.stack([attend_mine, attend_sent]), jnp.stack([attend_sent, attend_mine]))
        rows = rows.reshape(2 * unit, 3, width // 2)
        qkv_grad = rest_of(plan, lax.all_gather(rows, "blk", axis=2, tiled=True).reshape(2 * unit, -1), blk)
    table, *vec, b1_all = join_small(blk1, *small.both(), places, hidden)
    return (
        result[None], grad_x[None], table, vec[0], vec[1], qkv_grad, vec[2], vec[3], out_grad,
        vec[6], vec[4], vec[5], fc1_grad, b1_all, fc2_grad, vec[7],
    )


def solution(mesh):
    split = P("dp", "blk", None)
    ids = P("dp", "blk")
    both = P(("dp", "blk"), None)
    none = P()
    return jax.shard_map(
        functools.partial(per_device, mesh.shape["dp"]),
        mesh=mesh,
        in_specs=(split, ids, ids) + (none,) * 14 + (split,),
        out_specs=(
            split, split, none, none, none, both, none, none, both, none, none, none, both, none, both, none,
        ),
        check_vma=False,
    )
```

```python
import functools

import jax
import jax.numpy as jnp
from jax import lax
from jax.experimental import pallas as pl
from jax.experimental.pallas import tpu as pltpu
from jax.sharding import PartitionSpec as P

HD = 64
SEG_MOST = 196
EPS = 1e-06
inv_root_two = 0.7071067811865476
inv_root_two_pi = 0.3989422804014327
BF = jnp.bfloat16
F32 = jnp.float32
MIB = 1 << 20


def dot_nn(a, b):
    return jnp.dot(a, b, preferred_element_type=F32)


def dot_nt(a, b):
    return lax.dot_general(a, b, (((1,), (1,)), ((), ())), preferred_element_type=F32)


def dot_tn(a, b):
    return lax.dot_general(a, b, (((0,), (0,)), ((), ())), preferred_element_type=F32)


def normalise(hidden):
    mean = jnp.mean(hidden, -1, keepdims=True)
    centred = hidden - mean
    inv = lax.rsqrt(jnp.mean(centred * centred, -1, keepdims=True) + EPS)
    return centred * inv, inv


def norm_back(grad, normal, inv, gain):
    scaled = grad * gain
    centre = jnp.mean(scaled, -1, keepdims=True)
    along = jnp.mean(scaled * normal, -1, keepdims=True)
    return inv * (scaled - centre - normal * along)


def line(ref):
    return ref[...].reshape(1, -1)


def column_sum(v):
    return jnp.sum(v, axis=0, keepdims=True)


def params(vmem):
    return pltpu.CompilerParams(vmem_limit_bytes=vmem * MIB)


def cost(flops, bytes_accessed, trans=0):
    return pl.CostEstimate(
        flops=int(flops), bytes_accessed=int(bytes_accessed), transcendentals=int(trans)
    )


def whole(shape):
    return pl.BlockSpec(shape, lambda *_: (0,) * len(shape))


ANYWHERE = pl.BlockSpec(memory_space=pl.ANY)


def copies(pairs, sem):
    return [pltpu.make_async_copy(src, dst, sem.at[k]) for k, (src, dst) in enumerate(pairs)]


def started(pairs, sem):
    made = copies(pairs, sem)
    for copy in made:
        copy.start()
    return made


def done(made):
    for copy in made:
        copy.wait()


def lanes_of(shape, head):
    return (lax.broadcasted_iota(jnp.int32, shape, 1) % 128 < HD) == (head % 2 == 0)


def embedded(x_ref, pos_ref, table_ref):
    half = x_ref.shape[0]
    places = table_ref.shape[0]
    hot = (lax.broadcasted_iota(jnp.int32, (places, half), 0) == pos_ref[...]).astype(F32).astype(BF)
    return x_ref[...].astype(F32) + dot_tn(hot, table_ref[...])


def crop_lanes(seg_ref):
    half = seg_ref.shape[1]
    hot = (lax.broadcasted_iota(jnp.int32, (8, half), 0) == seg_ref[...]).astype(F32).astype(BF)
    eye = lax.broadcasted_iota(jnp.int32, (8, 128), 0) == lax.broadcasted_iota(jnp.int32, (8, 128), 1)
    return dot_tn(hot, eye.astype(F32).astype(BF)).astype(BF)


def front_kernel(block, blk_ref, *refs):
    sources, refs = refs[:21], refs[21:]
    (
        h0_out, n1_out, n1o_out, q_out, k_out, v_out, att_out, p_out, n2_out,
        gs_out, gk_out, as_out, ak_out, res_out, gn_out, h1_out, b1g_ref,
    ) = refs[:17]
    targets, refs = refs[17:38], refs[38:]
    (
        x_ref, xo_ref, seg_ref, sego_ref, pos_ref, poso_ref, cot_ref, table_ref,
        g1_ref, s1_ref, qb_ref, vb_ref, bo_ref, g2_ref, s2_ref, b1_ref, b2_ref, wqkv_ref, wo_ref, w1_ref, w2_ref,
    ) = targets
    (
        h0_ref, own_ref, n1_ref, n1o_ref, hoto_ref, q_ref, k_ref, v_ref, bias_ref,
        att_ref, p_ref, h1_ref, n2_ref, gp_ref, act_ref, mixed_ref, gn_ref, res_ref, bias_line_ref,
        in_sem, out_sem, late_sem,
    ) = refs
    half, width = x_ref.shape
    keys = k_ref.shape[0]
    halo = keys - half
    hidden = w1_ref.shape[1]
    blk = blk_ref[0]
    start = pl.multiple_of(blk * (half - halo), 16)
    loads = [pltpu.make_async_copy(src, dst, in_sem.at[k]) for k, (src, dst) in enumerate(zip(sources, targets))]
    outs = [
        pltpu.make_async_copy(src, dst, out_sem.at[k])
        for k, (src, dst) in enumerate(
            (
                (h0_ref, h0_out), (own_ref, n1_out), (n1o_ref, n1o_out), (q_ref, q_out), (k_ref, k_out),
                (v_ref, v_out), (att_ref, att_out), (n2_ref, n2_out), (res_ref, res_out), (gn_ref, gn_out),
                (h1_ref, h1_out), (p_ref, p_out),
            )
        )
    ]
    soon = (0, 4, 7, 1, 5, 8, 9, 17, 2, 3, 10, 11)
    then = (18, 19, 20, 6, 12, 13, 14, 15, 16)
    for k in soon:
        loads[k].start()
    for k in soon[:7]:
        loads[k].wait()
    hidden0 = embedded(x_ref, pos_ref, table_ref)
    h0_ref[...] = hidden0
    normal, _ = normalise(hidden0)
    own_ref[...] = (normal * line(g1_ref) + line(s1_ref)).astype(BF)
    n1_ref[:half, :] = own_ref[...]
    normal, _ = normalise(embedded(xo_ref, poso_ref, table_ref))
    n1o_ref[...] = (normal * line(g1_ref) + line(s1_ref)).astype(BF)
    n1_ref[half:, :] = n1o_ref[pl.ds(start, halo), :]
    for k in soon[7:]:
        loads[k].wait()
    for k in then:
        loads[k].start()
    hot = crop_lanes(seg_ref)
    hoto_ref[...] = crop_lanes(sego_ref)
    bias_ref[:, :half] = (dot_nt(hot, hot) - 1.0) * 1e9
    bias_ref[:, half:] = (dot_nt(hot, hoto_ref[pl.ds(start, halo), :]) - 1.0) * 1e9
    q = dot_nn(own_ref[...], wqkv_ref[:, :width]) + line(qb_ref)
    q_ref[...] = (q.astype(BF).astype(F32) * 0.125).astype(BF)
    k_ref[...] = dot_nn(n1_ref[...], wqkv_ref[:, width : 2 * width]).astype(BF)
    v_ref[...] = (dot_nn(n1_ref[...], wqkv_ref[:, 2 * width :]) + line(vb_ref)).astype(BF)
    for out in outs[:6]:
        out.start()
    rounds = 2
    pairs = width // 128 // rounds

    def heads(i, carry):
        for pair in range(pairs):
            cols = pl.ds(pl.multiple_of((i * pairs + pair) * 128, 128), 128)
            q = q_ref[:, cols]
            both = []
            for head in range(2):
                q_one = jnp.where(lanes_of(q.shape, head), q, jnp.zeros_like(q))
                scores = dot_nt(q_one, k_ref[:, cols]) + bias_ref[...]
                top = jnp.max(scores, -1, keepdims=True)
                weight = jnp.exp(scores - top)
                probs = (weight * (1.0 / jnp.sum(weight, -1, keepdims=True))).astype(BF)
                p_ref[2 * (i * pairs + pair) + head] = probs
                both.append(dot_nn(probs, v_ref[:, cols]))
            att_ref[:, cols] = jnp.where(lanes_of(both[0].shape, 0), both[0], both[1]).astype(BF)
        return carry

    lax.fori_loop(0, rounds, heads, 0)
    outs[6].start()
    outs[11].start()
    for k in then:
        loads[k].wait()
    hidden1 = h0_ref[...] + dot_nn(att_ref[...], wo_ref[...]) + line(bo_ref)
    h1_ref[...] = hidden1
    normal, _ = normalise(hidden1)
    n2_ref[...] = (normal * line(g2_ref) + line(s2_ref)).astype(BF)
    outs[7].start()
    outs[10].start()
    late = []
    chunk = 768
    part = chunk // 2
    mixed_ref[...] = hidden1 + line(b2_ref)
    gn_ref[...] = jnp.zeros_like(gn_ref)
    bias_line_ref[...] = line(b1_ref)

    def chunks(i, carry):
        for j in range(hidden // chunk // 2):
            first = i * (hidden // 2) + j * chunk
            at = pl.ds(pl.multiple_of(first, 128), chunk)
            pre = dot_nn(n2_ref[...], w1_ref[:, at]) + bias_line_ref[:, at]
            grad_act = dot_nt(cot_ref[...], w2_ref[at, :])
            cdf = 0.5 + 0.5 * lax.erf(pre * inv_root_two)
            act = (pre * cdf).astype(BF)
            slope = cdf + pre * jnp.exp(-0.5 * pre * pre) * inv_root_two_pi
            grad_pre = (grad_act * slope).astype(BF)
            b1g_ref[:, at] = column_sum(grad_pre.astype(F32))
            gp_ref[i, :, j * chunk : (j + 1) * chunk] = grad_pre
            mine = pl.ds(pl.multiple_of(i * (hidden // 4) + j * part, 128), part)
            for c in range(2):
                act_ref[c, :, mine] = jnp.concatenate(
                    [act[:, t : t + block] for t in range(c * block, chunk, 2 * block)], 1
                )
            mixed_ref[...] += dot_nn(act, w2_ref[at, :])
            gn_ref[...] += dot_nt(grad_pre, w1_ref[:, at])
        return carry

    lax.fori_loop(0, 2, chunks, 0)
    res_ref[...] = mixed_ref[...].astype(BF)
    for c, dst in enumerate((ak_out, as_out)):
        late.append((act_ref.at[(blk + c) % 2], dst))
    for c, dst in enumerate((gk_out, gs_out)):
        late.append((gp_ref.at[(blk + c) % 2], dst))
    late = [pltpu.make_async_copy(src, dst, late_sem.at[k]) for k, (src, dst) in enumerate(late)]
    for copy in late:
        copy.start()
    outs[8].start()
    outs[9].start()
    for out in outs:
        out.wait()
    for copy in late:
        copy.wait()


def front(plan, halo, blk, x, xo, seg, sego, pos, poso, cot, table, vectors, wqkv, wo, w1, w2):
    half, width = x.shape
    hidden = w1.shape[1]
    keys = half + halo
    heads = width // HD
    anywhere = pl.BlockSpec(memory_space=pl.ANY)
    operands = (x, xo, seg, sego, pos, poso, cot, table, *vectors, wqkv, wo, w1, w2)
    shapes = [
        ((half, width), F32),
        ((half, width), BF),
        ((half, width), BF),
        ((half, width), BF),
        ((keys, width), BF),
        ((keys, width), BF),
        ((half, width), BF),
        ((heads, half, keys), BF),
        ((half, width), BF),
        ((half, hidden // 2), BF),
        ((half, hidden // 2), BF),
        ((half, hidden // 2), BF),
        ((half, hidden // 2), BF),
        ((half, width), BF),
        ((half, width), F32),
        ((half, width), F32),
        ((1, hidden), F32),
    ]
    return pl.pallas_call(
        functools.partial(front_kernel, hidden // plan.groups // 2),
        grid_spec=pltpu.PrefetchScalarGridSpec(
            num_scalar_prefetch=1,
            grid=(1,),
            in_specs=[anywhere] * len(operands),
            out_specs=[anywhere] * 16 + [whole((1, hidden))],
            scratch_shapes=[pltpu.VMEM(v.shape, v.dtype) for v in operands]
            + [
                pltpu.VMEM((half, width), F32),
                pltpu.VMEM((half, width), BF),
                pltpu.VMEM((keys, width), BF),
                pltpu.VMEM((half, width), BF),
                pltpu.VMEM((half, 128), BF),
                pltpu.VMEM((half, width), BF),
                pltpu.VMEM((keys, width), BF),
                pltpu.VMEM((keys, width), BF),
                pltpu.VMEM((half, keys), F32),
                pltpu.VMEM((half, width), BF),
                pltpu.VMEM((heads, half, keys), BF),
                pltpu.VMEM((half, width), F32),
                pltpu.VMEM((half, width), BF),
                pltpu.VMEM((2, half, hidden // 2), BF),
                pltpu.VMEM((2, half, hidden // 2), BF),
                pltpu.VMEM((half, width), F32),
                pltpu.VMEM((half, width), F32),
                pltpu.VMEM((half, width), BF),
                pltpu.VMEM((1, hidden), F32),
                pltpu.SemaphoreType.DMA((len(operands),)),
                pltpu.SemaphoreType.DMA((12,)),
                pltpu.SemaphoreType.DMA((4,)),
            ],
        ),
        out_shape=[jax.ShapeDtypeStruct(*s) for s in shapes],
        compiler_params=params(60),
        cost_estimate=cost(
            2 * half * width * (5 * width + 4 * hidden) + 4 * half * keys * width, 8 * width * hidden
        ),
        name="front",
    )(blk, *operands)


def mid_kernel(gn_hbm, h1_hbm, cot_hbm, wo_hbm, g2_hbm, gh_ref, gb_ref, ga_ref, sums_ref, *refs):
    gn_ref, h1_ref, cot_ref, wo_ref, g2_ref, sem = refs
    done(started(zip((gn_hbm, h1_hbm, cot_hbm, g2_hbm, wo_hbm), (gn_ref, h1_ref, cot_ref, g2_ref, wo_ref)), sem))
    normal, inv = normalise(h1_ref[...])
    total = gn_ref[...]
    cot = cot_ref[...].astype(F32)
    grad_hidden1 = cot + norm_back(total, normal, inv, line(g2_ref))
    gh_ref[...] = grad_hidden1
    branch = grad_hidden1.astype(BF)
    gb_ref[...] = branch
    ga_ref[...] = dot_nt(branch, wo_ref[...]).astype(BF)
    sums_ref[0:1, :] = column_sum(total * normal)
    sums_ref[1:2, :] = column_sum(total)
    sums_ref[2:3, :] = column_sum(branch.astype(F32))
    sums_ref[3:4, :] = column_sum(cot)


def mid(gn, h1, cot, wo, g2):
    half, width = h1.shape
    operands = (gn, h1, cot, wo, g2)
    shapes = [((half, width), F32), ((half, width), BF), ((half, width), BF), ((4, width), F32)]
    return pl.pallas_call(
        mid_kernel,
        grid=(1,),
        in_specs=[ANYWHERE] * 5,
        out_specs=[whole(v[0]) for v in shapes],
        out_shape=[jax.ShapeDtypeStruct(*v) for v in shapes],
        scratch_shapes=[pltpu.VMEM(v.shape, v.dtype) for v in operands] + [pltpu.SemaphoreType.DMA((5,))],
        compiler_params=params(60),
        cost_estimate=cost(1, 1),
        name="mid",
    )(*operands)


class Plan:
    def __init__(self, ndp):
        self.ndp = ndp
        self.groups = min(16, ndp)
        self.bits = self.groups.bit_length() - 1
        self.rest = ndp // self.groups
        wanted = {"feed": ((0, 1, 2, 3), (1, 2, 0, 3), (2, 0, 1, 3)), "attend": ((0, 1, 2, 3), (1, 0, 2, 3))}
        self.orders = {k: [[b for b in o if b < self.bits] for o in v] for k, v in wanted.items()}
        self.small = [b for b in (2, 3, 1, 0) if b < self.bits]

    def place(self, name, piece, p):
        code = 0
        for bit in self.orders[name][piece]:
            code = 2 * code + ((p >> bit) & 1)
        return divmod(self.groups - 1 - code, self.groups // 2)


def feed_weights_kernel(plan, own_ref, blk_ref, *refs):
    sources, refs = refs[:12], refs[-24:]
    outs, targets, stages = refs[:6], refs[6:18], refs[18:20]
    acc_ref, low_ref, in_sem, out_sem = refs[20:]
    n2_ref, n2o_ref, g_ref, go_ref, act_ref, acto_ref, cot_ref, coto_ref, att_ref, atto_ref, gb_ref, gbo_ref = targets
    own = own_ref[0]
    width = n2_ref.shape[1]
    cols = width // 2
    groups, per = plan.groups, plan.groups // 2
    chunk = g_ref.shape[1] // 2
    rows = width // groups
    unit = rows // 2
    at = pl.ds(pl.multiple_of(blk_ref[0] * cols, 128), cols)
    pairs = list(zip(sources[:10], targets)) + [(sources[10].at[:, at], gb_ref), (sources[11].at[:, at], gbo_ref)]
    loads = started(pairs, in_sem)

    def emit(number, p, value):
        piece, slot = divmod(number, 3)
        kept, place = plan.place("feed", piece, p)
        stages[kept][piece, place, slot] = value.astype(BF)

    done(loads[:4])
    for step in range(2):
        lanes = slice(step * chunk, (step + 1) * chunk)
        acc_ref[step] = dot_tn(n2_ref[...], g_ref[:, lanes]) + dot_tn(n2o_ref[...], go_ref[:, lanes])
        for p in range(groups):
            for k in range(2):
                source = pl.multiple_of((own ^ p) * rows + k * unit, 8)
                emit(5 + 2 * step + k, p, acc_ref[step, pl.ds(source, unit), :])
    done(loads[4:])
    low_ref[...] = dot_tn(att_ref[...], gb_ref[...]) + dot_tn(atto_ref[...], gbo_ref[...])
    for p in range(groups):
        source = pl.multiple_of((own ^ p) * rows, 16)
        block = low_ref[pl.ds(source, rows), :]
        emit(4, p, jnp.concatenate([block[:unit], block[unit:]], 1))
    sent = copies([(stages[kept].at[piece], outs[2 * piece + kept]) for piece in range(3) for kept in range(2)], out_sem)
    for copy in sent[4:]:
        copy.start()
    for step in range(2):
        lanes = pl.ds(pl.multiple_of(((own // per) ^ step) * chunk, 128), chunk)
        acc_ref[2 + step] = dot_tn(act_ref[:, lanes], cot_ref[...]) + dot_tn(acto_ref[:, lanes], coto_ref[...])
        for low in range(per):
            for k in range(4):
                source = pl.multiple_of(((own % per) ^ low) * (chunk // per) + k * unit, 8)
                emit(k, step * per + low, acc_ref[2 + step, pl.ds(source, unit), :])
    for copy in sent[:4]:
        copy.start()
    done(sent)


def feed_weights(plan, own, blk, *operands):
    half, width = operands[0].shape
    chunk, cols = operands[2].shape[1] // 2, width // 2
    part = jax.ShapeDtypeStruct((plan.groups // 2, 3, width // plan.groups // 2, width), BF)
    shapes = [v.shape for v in operands[:10]] + [(half, cols)] * 2

    return pl.pallas_call(
        functools.partial(feed_weights_kernel, plan),
        grid_spec=pltpu.PrefetchScalarGridSpec(
            num_scalar_prefetch=2,
            grid=(1,),
            in_specs=[ANYWHERE] * 12,
            out_specs=[ANYWHERE] * 6,
            scratch_shapes=[pltpu.VMEM(v, BF) for v in shapes]
            + [pltpu.VMEM((3,) + part.shape, BF)] * 2
            + [pltpu.VMEM((4, width, chunk), F32), pltpu.VMEM((width, cols), F32)]
            + [pltpu.SemaphoreType.DMA((12,)), pltpu.SemaphoreType.DMA((6,))],
        ),
        out_shape=(part,) * 6,
        compiler_params=params(60),
        cost_estimate=cost(1, 1),
        name="feed_weights",
    )(own, blk, *operands)


def attend_back_kernel(blk_ref, q_hbm, k_hbm, v_hbm, ga_hbm, p_hbm, *refs):
    outs, refs = refs[:6], refs[6:]
    q_ref, k_ref, v_ref, ga_ref, p_ref, d_ref, h_ref, sem, p_sem, out_sem = refs
    half, width = q_ref.shape
    cols = width // 2
    loads = started(
        [(q_hbm, q_ref), (k_hbm, k_ref), (v_hbm, v_ref), (ga_hbm, ga_ref)], sem
    )
    heads = p_ref.shape[0]
    per = heads // 2
    probs_in = started([(p_hbm.at[k : k + per], p_ref.at[k : k + per]) for k in range(0, heads, per)], p_sem)
    done(loads + probs_in[:1])
    pairs = heads // 4

    def one_side(side, carry):
        @pl.when(side == 1)
        def _():
            probs_in[1].wait()

        for pair in range(pairs):
            lanes = pl.ds(pl.multiple_of(side * cols + pair * 128, 128), 128)
            at = slice(pair * 128, pair * 128 + 128)
            q, k, grad = q_ref[:, lanes], k_ref[:, lanes], ga_ref[:, lanes]
            dqs, dks, dvs = [], [], []
            for head in range(2):
                grad_one = jnp.where(lanes_of(grad.shape, head), grad, jnp.zeros_like(grad))
                grad_probs = dot_nt(grad_one, v_ref[:, lanes])
                low = p_ref[2 * (side * pairs + pair) + head]
                probs = low.astype(F32)
                row = jnp.sum(probs * grad_probs, -1, keepdims=True)
                grad_scores = (probs * (grad_probs - row)).astype(BF)
                dqs.append(dot_nn(grad_scores, k))
                dks.append(dot_tn(q, grad_scores))
                dvs.append(dot_tn(grad, low))
            d_ref[side, 0, :, at] = (jnp.where(lanes_of(dqs[0].shape, 0), dqs[0], dqs[1]) * 0.125).astype(BF)
            first = lax.broadcasted_iota(jnp.int32, dks[0].shape, 0) < HD
            dk = jnp.where(first, dks[0], dks[1]).T.astype(BF)
            dv = jnp.where(first, dvs[0], dvs[1]).T.astype(BF)
            d_ref[side, 1, :, at] = dk[:half]
            d_ref[side, 2, :, at] = dv[:half]
            h_ref[side, 0, :, at] = dk[half:]
            h_ref[side, 1, :, at] = dv[half:]
        return carry

    lax.fori_loop(0, 2, one_side, 0)
    core = blk_ref[0]
    done(
        started(
            [
                (h_ref.at[1 - core], outs[0]),
                (h_ref.at[core], outs[1]),
                (d_ref.at[core], outs[2]),
                (d_ref.at[1 - core, 0], outs[3]),
                (d_ref.at[1 - core, 1], outs[4]),
                (d_ref.at[1 - core, 2], outs[5]),
            ],
            out_sem,
        )
    )


def attend_back(blk, q, k, v, probs, ga, *after):
    half, width = q.shape
    keys = k.shape[0]
    halo = keys - half
    cols = width // 2
    shapes = ((2, halo, cols),) * 2 + ((3, half, cols),) + ((half, cols),) * 3

    def body(blk_ref, *refs):
        ins, refs = refs[:5], refs[5 + len(after) :]
        attend_back_kernel(blk_ref, *ins, *refs)

    return pl.pallas_call(
        body,
        grid_spec=pltpu.PrefetchScalarGridSpec(
            num_scalar_prefetch=1,
            grid=(1,),
            in_specs=[ANYWHERE] * (5 + len(after)),
            out_specs=[ANYWHERE] * 6,
            scratch_shapes=[
                pltpu.VMEM((half, width), BF),
                pltpu.VMEM((keys, width), BF),
                pltpu.VMEM((keys, width), BF),
                pltpu.VMEM((half, width), BF),
                pltpu.VMEM(probs.shape, BF),
                pltpu.VMEM((2, 3, half, cols), BF),
                pltpu.VMEM((2, 2, halo, cols), BF),
                pltpu.SemaphoreType.DMA((4,)),
                pltpu.SemaphoreType.DMA((2,)),
                pltpu.SemaphoreType.DMA((6,)),
            ],
        ),
        out_shape=[jax.ShapeDtypeStruct(v, BF) for v in shapes],
        compiler_params=params(60),
        cost_estimate=cost(1, 1),
        name="attend_back",
    )(blk, q, k, v, ga, probs, *after)


def add_rows(ref, start, at, cols, extra):
    rows = pl.ds(start, extra.shape[0])
    part = ref[rows, pl.ds(at, cols)].astype(F32) + extra.astype(F32)
    ref[rows, pl.ds(at, cols)] = part.astype(BF)


def attend_weights_kernel(plan, own_ref, blk_ref, *refs):
    count = len(plan.orders["attend"])
    sources, outs, refs = refs[:8], refs[8 : 8 + 2 * count], refs[8 + 2 * count :]
    n1_ref, n1o_ref, hk_ref, ho_ref, mine_ref, other_ref, acc_ref, send_ref, keep_ref, sem, out_sem = refs
    half, width = n1_ref.shape
    halo = hk_ref.shape[1]
    cols = width // 2
    own, blk = own_ref[0], blk_ref[0]
    rows = width // plan.groups
    start = pl.multiple_of((1 - blk) * (half - halo), 16)
    start_other = pl.multiple_of(blk * (half - halo), 16)
    n1, n1o, d, hk, ho = sources[:5]
    pairs = [(d.at[k], mine_ref.at[:, k * cols : (k + 1) * cols]) for k in range(3)]
    pairs += [(sources[5 + k], other_ref.at[:, k * cols : (k + 1) * cols]) for k in range(3)]
    pairs += [(n1, n1_ref), (n1o, n1o_ref), (hk, hk_ref), (ho, ho_ref)]
    done(started(pairs, sem))
    for which in range(2):
        lane = (1 + which) * cols
        add_rows(mine_ref, start, lane, cols, ho_ref[which])
        add_rows(other_ref, start_other, lane, cols, hk_ref[which])
    part = rows // count
    stages = (send_ref, keep_ref)
    for at in (slice(0, width), slice(width, width + cols)):
        acc_ref[:, at] = dot_tn(n1_ref[...], mine_ref[:, at]) + dot_tn(n1o_ref[...], other_ref[:, at])
        for p in range(plan.groups):
            for piece in range(count):
                source = pl.multiple_of((own ^ p) * rows + piece * part, 8)
                kept, place = plan.place("attend", piece, p)
                stages[kept][piece, place, :, at] = acc_ref[pl.ds(source, part), at].astype(BF)
    done(
        started(
            [(stages[kept].at[piece], outs[2 * piece + kept]) for piece in range(count) for kept in range(2)], out_sem
        )
    )


def attend_weights(plan, own, blk, n1, n1o, d, hk, ho, do):
    half, width = n1.shape
    cols = width // 2
    count = len(plan.orders["attend"])
    part = jax.ShapeDtypeStruct((plan.groups // 2, width // plan.groups // count, 3 * cols), BF)
    return pl.pallas_call(
        functools.partial(attend_weights_kernel, plan),
        grid_spec=pltpu.PrefetchScalarGridSpec(
            num_scalar_prefetch=2,
            grid=(1,),
            in_specs=[ANYWHERE] * 8,
            out_specs=[ANYWHERE] * (2 * count),
            scratch_shapes=[pltpu.VMEM((half, width), BF)] * 2
            + [pltpu.VMEM(hk.shape, BF)] * 2
            + [pltpu.VMEM((half, 3 * cols), BF)] * 2
            + [pltpu.VMEM((width, 3 * cols), F32)]
            + [pltpu.VMEM((count,) + part.shape, BF)] * 2
            + [pltpu.SemaphoreType.DMA((10,)), pltpu.SemaphoreType.DMA((2 * count,))],
        ),
        out_shape=(part,) * (2 * count),
        compiler_params=params(60),
        cost_estimate=cost(1, 1),
        name="attend_weights",
    )(own, blk, n1, n1o, d, hk, ho, *do)


def front_back_kernel(places, blk_ref, *refs):
    sources, refs = refs[:13], refs[13:]
    gx_ref, small_mine, small_other = refs[:3]
    gj_ref, w_ref, h0_ref, gh_ref, g1_ref, pos_ref, sums_ref, b1_ref, ho_ref, hl_ref, small_ref, sem = refs[3:]
    half, width = h0_ref.shape
    halo = ho_ref.shape[1]
    cols = width // 2
    blk = blk_ref[0]
    start = pl.multiple_of((1 - blk) * (half - halo), 16)
    lanes = [[pl.multiple_of(which * width + core * cols, 128) for core in (blk, 1 - blk)] for which in range(3)]
    pairs = [(sources[4 + 2], w_ref)]
    pairs += [(sources[0].at[k], gj_ref.at[:, pl.ds(lanes[k][0], cols)]) for k in range(3)]
    pairs += [(sources[1 + k], gj_ref.at[:, pl.ds(lanes[k][1], cols)]) for k in range(3)]
    pairs += [(sources[4], ho_ref), (sources[5], hl_ref)]
    pairs += list(zip(sources[7:], (h0_ref, gh_ref, g1_ref, pos_ref, sums_ref, b1_ref)))
    loads = started(pairs, sem)
    done(loads[1:9])
    for which in range(2):
        add_rows(gj_ref, start, lanes[1 + which][0], cols, ho_ref[which])
        add_rows(gj_ref, start, lanes[1 + which][1], cols, hl_ref[which])
    done(loads[:1] + loads[9:])
    total = dot_nt(gj_ref[...], w_ref[...])
    small_ref[places + 2 : places + 3, :] = column_sum(gj_ref[:, :width].astype(F32))
    small_ref[places + 3 : places + 4, :] = column_sum(gj_ref[:, 2 * width :].astype(F32))
    normal, inv = normalise(h0_ref[...])
    small_ref[places : places + 1, :] = column_sum(total * normal)
    small_ref[places + 1 : places + 2, :] = column_sum(total)
    grad = (gh_ref[...] + norm_back(total, normal, inv, line(g1_ref))).astype(BF)
    gx_ref[...] = grad
    hot = (lax.broadcasted_iota(jnp.int32, (places, half), 0) == pos_ref[...]).astype(F32).astype(BF)
    small_ref[:places, :] = dot_nn(hot, grad)
    small_ref[places + 4 : places + 8, :] = sums_ref[...]
    for k in range(4):
        small_ref[places + 8 + k : places + 9 + k, :] = b1_ref[:, k * width : (k + 1) * width]
    for ref, core in ((small_mine, blk), (small_other, 1 - blk)):
        ref[0] = small_ref[:, pl.ds(pl.multiple_of(core * cols, 128), cols)].astype(BF)


def front_back(blk, d, ds, ho, hl, w, h0, gh, g1, pos, sums, b1, places):
    half, width = h0.shape
    extra = (1, places + 12, width // 2)
    rest = (w, h0, gh, g1, pos, sums, b1, ho, hl)
    return pl.pallas_call(
        functools.partial(front_back_kernel, places),
        grid_spec=pltpu.PrefetchScalarGridSpec(
            num_scalar_prefetch=1,
            grid=(1,),
            in_specs=[ANYWHERE] * 13,
            out_specs=[whole((half, width)), whole(extra), whole(extra)],
            scratch_shapes=[pltpu.VMEM((half, 3 * width), BF)]
            + [pltpu.VMEM(v.shape, v.dtype) for v in rest]
            + [pltpu.VMEM((places + 12, width), F32), pltpu.SemaphoreType.DMA((15,))],
        ),
        out_shape=(
            jax.ShapeDtypeStruct((half, width), BF),
            jax.ShapeDtypeStruct(extra, BF),
            jax.ShapeDtypeStruct(extra, BF),
        ),
        compiler_params=params(60),
        cost_estimate=cost(1, 1),
        name="front_back",
    )(blk, d, *ds, ho, hl, *rest[:7])


def swap(v):
    return lax.ppermute(v, "blk", [(0, 1), (1, 0)])


def across(v, ndp, flip):
    return lax.ppermute(v, "dp", [(i, i ^ flip) for i in range(ndp)])


def wide(v):
    return v.astype(F32)


def combine_kernel(plans, *refs):
    outs = refs[-len(plans) :]
    used = 0
    for out, plan in zip(outs, plans):
        at = 0
        for count, terms in plan:
            total = refs[used][...].astype(F32)
            for ref in refs[used + 1 : used + terms]:
                total = total + ref[...].astype(F32)
            used += terms
            out[at : at + count] = total.astype(out.dtype)
            at += count


def combine(arrays, plans, types, before=()):
    block = arrays[0].shape[1:]
    shapes = [(sum(count for count, _ in plan),) + block for plan in plans]
    if before:
        arrays = [behind(arrays[0], *before)] + list(arrays[1:])
    operands, specs, counts = [], [], []
    for plan in plans:
        counts.append([])
        for count, terms in plan:
            counts[-1].append((count, len(terms)))
            for index, start in terms:
                operands.append(arrays[index])
                specs.append(
                    pl.BlockSpec(
                        (count,) + block, functools.partial(lambda at, i: (at,) + (0,) * len(block), start // count)
                    )
                )
    return pl.pallas_call(
        functools.partial(combine_kernel, counts),
        grid=(1,),
        in_specs=specs,
        out_specs=[whole(v) for v in shapes],
        out_shape=[jax.ShapeDtypeStruct(v, t) for v, t in zip(shapes, types)],
        compiler_params=params(24),
        cost_estimate=cost(1, 1),
        name="combine",
    )(*operands)


class Pieces:
    def __init__(self, plan, name, parts):
        self.plan, self.orders, self.phase = plan, plan.orders[name], 0
        self.terms = [[(parts[2 * k + 1], 0, 0)] for k in range(len(self.orders))]
        self.at, self.left = 0, plan.groups // 2
        self.sent = parts[0]
        for k in range(len(self.orders)):
            self.terms[k].append((self.across(parts[2 * k], self.orders[k][0]), 0, 0))
        self.phase = 1

    def across(self, value, bit):
        return across(value, self.plan.ndp, self.plan.rest << bit)

    def collect(self):
        arrays, where = [], []
        for k in range(len(self.orders)):
            where.append([])
            for array, place, start in self.terms[k]:
                if not any(array is v for v in arrays):
                    arrays.append(array)
                index = [array is v for v in arrays].index(True)
                where[k].append((index, start + self.at - place))
        return arrays, where

    def step(self, *before):
        if self.phase >= self.plan.bits:
            return
        h = self.left // 2
        arrays, where = self.collect()
        bits = [order[self.phase] for order in self.orders]
        joined = len(set(bits)) == 1
        plans = [[(h, w)] for w in where]
        values = combine(arrays, [sum(plans, [])] if joined else plans, [BF] * len(self.orders), before)
        self.at, self.left = self.at + h, h
        self.sent = values[0]
        if joined:
            got = [self.across(values[0], bits[0])] * len(bits)
        else:
            got = [self.across(v, bit) for v, bit in zip(values, bits)]
        for k in range(len(self.orders)):
            self.terms[k].append((got[k], self.at, k * h if joined else 0))
        self.phase += 1

    def totals(self, *before):
        arrays, where = self.collect()
        return combine(arrays, [[(1, w) for w in where]], [F32], before)[0]


class Everywhere:
    def __init__(self, plan, mine, other):
        self.plan, self.phase = plan, 0
        self.flips = [plan.rest << b for b in plan.small] + [1 << b for b in range(plan.rest.bit_length() - 1)] + [None]
        self.sent, self.got = mine, swap(other)

    def step(self, *before):
        if self.phase >= len(self.flips):
            return
        (self.sent,) = combine([self.sent, self.got], [[(1, [(0, 0), (1, 0)])]], [BF], before)
        flip = self.flips[self.phase]
        self.got = swap(self.sent) if flip is None else across(self.sent, self.plan.ndp, flip)
        self.phase += 1

    def both(self):
        while self.phase < len(self.flips):
            self.step()
        return self.sent, self.got


def split_feed_kernel(counts, blk_ref, *refs):
    fc2_ref, mine, other = refs[-3:]
    units = []
    used = 0
    for terms in counts:
        total = refs[used][0].astype(F32)
        for ref in refs[used + 1 : used + terms]:
            total = total + ref[0].astype(F32)
        used += terms
        units += [total[k] for k in range(3)]
    unit, cols = mine.shape[1], mine.shape[2] // 2
    for k in range(4):
        fc2_ref[k * unit : (k + 1) * unit, :] = units[k]
    low_core = blk_ref[0] == 0
    for k in range(2):
        low, high = units[5 + 2 * k], units[6 + 2 * k]
        mine[k] = jnp.where(low_core, low, high)
        other[k] = jnp.where(low_core, high, low)
    low, high = units[4][:, :cols], units[4][:, cols:]
    mine[2, :, :cols] = jnp.where(low_core, low, high)
    other[2, :, :cols] = jnp.where(low_core, high, low)
    mine[2, :, cols:] = jnp.zeros_like(low)
    other[2, :, cols:] = jnp.zeros_like(low)


def split_feed(blk, pieces):
    arrays, where = pieces.collect()
    block = (1,) + arrays[0].shape[1:]
    unit, width = block[2:]
    shapes = [(4 * unit, width), (3, unit, width), (3, unit, width)]
    places = [(index, at) for terms in where for index, at in terms]
    return pl.pallas_call(
        functools.partial(split_feed_kernel, [len(terms) for terms in where]),
        grid_spec=pltpu.PrefetchScalarGridSpec(
            num_scalar_prefetch=1,
            grid=(1,),
            in_specs=[
                pl.BlockSpec(block, functools.partial(lambda at, i, b: (at, 0, 0, 0), at)) for _, at in places
            ],
            out_specs=[whole(v) for v in shapes],
        ),
        out_shape=[jax.ShapeDtypeStruct(v, F32) for v in shapes],
        compiler_params=params(24),
        cost_estimate=cost(1, 1),
        name="split_feed",
    )(blk, *[arrays[index] for index, _ in places])


def join_feed_kernel(blk_ref, mine_ref, got_ref, fc1_ref, out_ref):
    width = mine_ref.shape[2]
    cols = width // 2
    for ref, core in ((mine_ref, blk_ref[0]), (got_ref, 1 - blk_ref[0])):
        for k in range(2):
            fc1_ref[:, pl.ds(pl.multiple_of((core * 2 + k) * width, 128), width)] = ref[k]
        out_ref[:, pl.ds(pl.multiple_of(core * cols, 128), cols)] = ref[2, :, :cols]


def join_feed(blk, mine, got):
    _, rows, width = mine.shape
    shapes = [(rows, 4 * width), (rows, width)]
    return pl.pallas_call(
        join_feed_kernel,
        grid_spec=pltpu.PrefetchScalarGridSpec(
            num_scalar_prefetch=1,
            grid=(1,),
            in_specs=[whole(mine.shape)] * 2,
            out_specs=[whole(v) for v in shapes],
        ),
        out_shape=[jax.ShapeDtypeStruct(v, F32) for v in shapes],
        compiler_params=params(24),
        cost_estimate=cost(1, 1),
        name="join_feed",
    )(blk, mine, got)


def join_attend_kernel(blk_ref, mine_ref, got_ref, qkv_ref):
    cols = mine_ref.shape[1] // 3
    for ref, core in ((mine_ref, blk_ref[0]), (got_ref, 1 - blk_ref[0])):
        for k in range(3):
            at = pl.ds(pl.multiple_of((2 * k + core) * cols, 128), cols)
            qkv_ref[:, at] = ref[:, k * cols : (k + 1) * cols]


def join_attend(blk, mine, got):
    shape = (mine.shape[0], 2 * mine.shape[1])
    return pl.pallas_call(
        join_attend_kernel,
        grid_spec=pltpu.PrefetchScalarGridSpec(
            num_scalar_prefetch=1, grid=(1,), in_specs=[whole(mine.shape)] * 2, out_specs=whole(shape)
        ),
        out_shape=jax.ShapeDtypeStruct(shape, F32),
        compiler_params=params(24),
        cost_estimate=cost(1, 1),
        name="join_attend",
    )(blk, mine, got)


def split_attend_kernel(counts, blk_ref, *refs):
    mine, other, whole_ref = refs[-3:]
    part = whole_ref.shape[0] // len(counts)
    used = 0
    for piece, terms in enumerate(counts):
        total = refs[used][0].astype(F32)
        for ref in refs[used + 1 : used + terms]:
            total = total + ref[0].astype(F32)
        used += terms
        whole_ref[piece * part : (piece + 1) * part, :] = total
    half = mine.shape[0]
    low, high = whole_ref[:half, :], whole_ref[half:, :]
    low_core = blk_ref[0] == 0
    mine[...] = jnp.where(low_core, low, high)
    other[...] = jnp.where(low_core, high, low)


def split_attend(blk, pieces):
    arrays, where = pieces.collect()
    _, part, cols = arrays[0].shape
    shape = (len(where) * part // 2, cols)
    places = [(index, at) for terms in where for index, at in terms]
    return pl.pallas_call(
        functools.partial(split_attend_kernel, [len(terms) for terms in where]),
        grid_spec=pltpu.PrefetchScalarGridSpec(
            num_scalar_prefetch=1,
            grid=(1,),
            in_specs=[
                pl.BlockSpec((1, part, cols), functools.partial(lambda at, i, b: (at, 0, 0), at)) for _, at in places
            ],
            out_specs=[whole(shape)] * 2,
            scratch_shapes=[pltpu.VMEM((len(where) * part, cols), F32)],
        ),
        out_shape=[jax.ShapeDtypeStruct(shape, F32)] * 2,
        compiler_params=params(24),
        cost_estimate=cost(1, 1),
        name="split_attend",
    )(blk, *[arrays[index] for index, _ in places])


def join_small_kernel(blk_ref, mine_ref, got_ref, *outs):
    joined_ref = outs[-1]
    cols = mine_ref.shape[2]
    width = 2 * cols
    places = outs[0].shape[0]
    for ref, core in ((mine_ref, blk_ref[0]), (got_ref, 1 - blk_ref[0])):
        joined_ref[:, pl.ds(pl.multiple_of(core * cols, 128), cols)] = ref[0].astype(F32)
    outs[0][...] = joined_ref[:places, :]
    for k, out in enumerate(outs[1:9]):
        out[...] = joined_ref[places + k, :]
    for k in range(outs[9].shape[0] // width):
        outs[9][k * width : (k + 1) * width] = joined_ref[places + 8 + k, :]


def join_small(blk, mine, got, places, hidden):
    _, rows, cols = mine.shape
    width = 2 * cols
    shapes = [(places, width)] + [(width,)] * 8 + [(hidden,)]
    return pl.pallas_call(
        join_small_kernel,
        grid_spec=pltpu.PrefetchScalarGridSpec(
            num_scalar_prefetch=1,
            grid=(1,),
            in_specs=[whole(mine.shape)] * 2,
            out_specs=[whole(v) for v in shapes],
            scratch_shapes=[pltpu.VMEM((rows, width), F32)],
        ),
        out_shape=[jax.ShapeDtypeStruct(v, F32) for v in shapes],
        compiler_params=params(24),
        cost_estimate=cost(1, 1),
        name="join_small",
    )(blk, mine, got)


def join(blk, attend_mine, attend_got, feed_mine, feed_got, mine, got, places, hidden):
    unit, cols = attend_mine.shape
    rows, width = mine.shape[1], feed_mine.shape[2]
    shapes = [(unit, 2 * cols), (unit, 4 * width), (unit, width), (places, width)] + [(width,)] * 8 + [(hidden,)]
    operands = (attend_mine, attend_got, feed_mine, feed_got, mine, got)

    def kernel(blk_ref, *refs):
        join_attend_kernel(blk_ref, refs[0], refs[1], refs[6])
        join_feed_kernel(blk_ref, refs[2], refs[3], refs[7], refs[8])
        join_small_kernel(blk_ref, refs[4], refs[5], *refs[9:])

    return pl.pallas_call(
        kernel,
        grid_spec=pltpu.PrefetchScalarGridSpec(
            num_scalar_prefetch=1,
            grid=(1,),
            in_specs=[whole(v.shape) for v in operands],
            out_specs=[whole(v) for v in shapes],
            scratch_shapes=[pltpu.VMEM((rows, width), F32)],
        ),
        out_shape=[jax.ShapeDtypeStruct(v, F32) for v in shapes],
        compiler_params=params(24),
        cost_estimate=cost(1, 1),
        name="join",
    )(blk, *operands)


def behind(values, *others):
    return lax.optimization_barrier((values, others))[0]


def rest_of(plan, value, blk):
    groups = [[g * plan.rest + i for i in range(plan.rest)] for g in range(plan.groups)]
    value = lax.psum(value, "dp", axis_index_groups=groups)
    rows = value.shape[0] // (2 * plan.rest)
    return lax.dynamic_slice_in_dim(value, ((lax.axis_index("dp") % plan.rest) * 2 + blk) * rows, rows, axis=0)


def per_device(
    ndp, inputs, segments, positions, pos_table, ln1_gain, ln1_shift, qkv_weight, query_bias,
    value_bias, out_weight, out_bias, ln2_gain, ln2_shift, fc1_weight, fc1_bias, fc2_weight,
    fc2_bias, cotangent,
):
    plan = Plan(ndp)
    x, cot = inputs[0], cotangent[0]
    half, width = x.shape
    hidden = fc1_weight.shape[1]
    places = pos_table.shape[0]
    halo = next(h for h in range(SEG_MOST - 1, half + 1) if (half + h) % 128 == 0 and (half - h) % 16 == 0)
    blk = lax.axis_index("blk")
    dp = lax.axis_index("dp")
    blk1 = blk.astype(jnp.int32).reshape(1)
    own1 = (dp // plan.rest).astype(jnp.int32).reshape(1)

    x_other, seg_other, pos_other = swap(x), swap(segments), swap(positions)
    cot_other = swap(cot)
    vectors = (ln1_gain, ln1_shift, query_bias, value_bias, out_bias, ln2_gain, ln2_shift, fc1_bias, fc2_bias)
    (
        hidden0, n1, n1_other, q, k, v, att, probs, n2, grad_send, grad_keep, act_send, act_keep, result, gn2, hidden1,
        b1_grad,
    ) = front(
        plan, halo, blk1, x, x_other, segments, seg_other, positions, pos_other, cot, pos_table, vectors,
        qkv_weight, out_weight, fc1_weight, fc2_weight,
    )
    grad_other, act_other, n2_other = swap(grad_send), swap(act_send), swap(behind(n2, cot_other))
    gh1, gb, ga, sums = mid(gn2, hidden1, cot, out_weight, ln2_gain)
    att_other, gb_other = swap(att), swap(gb)
    parts = feed_weights(
        plan, own1, blk1, behind(n2, ga), n2_other, grad_keep, grad_other, act_keep, act_other, cot, cot_other, att, att_other, gb, gb_other,
    )
    feed_sums = Pieces(plan, "feed", parts)
    h_send, h_keep, d_keep, *d_send = attend_back(blk1, behind(q, parts[0]), k, v, probs, ga)
    h_other, h_late = swap(h_send), swap(h_keep)
    d_other = [swap(v) for v in d_send]
    grad_x, mine, other = front_back(
        blk1, d_keep, d_send, h_other, h_late, qkv_weight, hidden0, gh1, ln1_gain, positions, sums, b1_grad, places
    )
    small = Everywhere(plan, mine, other)
    feed_sums.step(grad_x)
    small.step(feed_sums.sent)
    parts = attend_weights(
        plan, own1, blk1, behind(n1, small.sent), n1_other, d_keep, h_keep, h_other, d_other
    )
    attend_sums = Pieces(plan, "attend", parts)
    before = parts[0]
    for item in (small, feed_sums, attend_sums, small, feed_sums, attend_sums, small, attend_sums, small):
        item.step(before)
        before = item.sent
    unit = width // plan.groups // 2
    attend_mine, attend_sent = split_attend(blk1, attend_sums)
    if plan.rest == 1:
        fc2_grad, feed_mine, feed_sent = split_feed(blk1, feed_sums)
        feed_got = swap(feed_sent)
        qkv_grad, fc1_grad, out_grad, table, *vec, b1_all = join(
            blk1, attend_mine, swap(attend_sent), feed_mine, feed_got, *small.both(), places, hidden
        )
    else:
        units = feed_sums.totals().reshape(9, unit, width)
        fc2_grad = rest_of(plan, lax.all_gather(units[:4].reshape(-1, width), "blk", axis=0, tiled=True), blk)
        rows = jnp.concatenate([units[5:7].reshape(-1, width), units[7:].reshape(-1, width)], 1)
        fc1_grad = rest_of(plan, lax.all_gather(rows, "blk", axis=1, tiled=True), blk)
        rows = jnp.concatenate([units[4][:, : width // 2], units[4][:, width // 2 :]], 0)
        out_grad = rest_of(plan, lax.all_gather(rows, "blk", axis=1, tiled=True), blk)
        rows = jnp.where(blk == 0, jnp.stack([attend_mine, attend_sent]), jnp.stack([attend_sent, attend_mine]))
        rows = rows.reshape(2 * unit, 3, width // 2)
        qkv_grad = rest_of(plan, lax.all_gather(rows, "blk", axis=2, tiled=True).reshape(2 * unit, -1), blk)
        table, *vec, b1_all = join_small(blk1, *small.both(), places, hidden)
    return (
        result[None], grad_x[None], table, vec[0], vec[1], qkv_grad, vec[2], vec[3], out_grad,
        vec[6], vec[4], vec[5], fc1_grad, b1_all, fc2_grad, vec[7],
    )


def solution(mesh):
    split = P("dp", "blk", None)
    ids = P("dp", "blk")
    both = P(("dp", "blk"), None)
    none = P()
    return jax.shard_map(
        functools.partial(per_device, mesh.shape["dp"]),
        mesh=mesh,
        in_specs=(split, ids, ids) + (none,) * 14 + (split,),
        out_specs=(
            split, split, none, none, none, both, none, none, both, none, none, none, both, none, both, none,
        ),
        check_vma=False,
    )
```

```python
import functools

import jax
import jax.numpy as jnp
from jax import lax
from jax.experimental import pallas as pl
from jax.experimental.pallas import tpu as pltpu
from jax.sharding import PartitionSpec as P

HD = 64
SEG_MOST = 196
EPS = 1e-06
inv_root_two = 0.7071067811865476
inv_root_two_pi = 0.3989422804014327
BF = jnp.bfloat16
F32 = jnp.float32
MIB = 1 << 20


def dot_nn(a, b):
    return jnp.dot(a, b, preferred_element_type=F32)


def dot_nt(a, b):
    return lax.dot_general(a, b, (((1,), (1,)), ((), ())), preferred_element_type=F32)


def dot_tn(a, b):
    return lax.dot_general(a, b, (((0,), (0,)), ((), ())), preferred_element_type=F32)


def normalise(hidden):
    mean = jnp.mean(hidden, -1, keepdims=True)
    centred = hidden - mean
    inv = lax.rsqrt(jnp.mean(centred * centred, -1, keepdims=True) + EPS)
    return centred * inv, inv


def norm_back(grad, normal, inv, gain):
    scaled = grad * gain
    centre = jnp.mean(scaled, -1, keepdims=True)
    along = jnp.mean(scaled * normal, -1, keepdims=True)
    return inv * (scaled - centre - normal * along)


def line(ref):
    return ref[...].reshape(1, -1)


def column_sum(v):
    return jnp.sum(v, axis=0, keepdims=True)


def params(vmem):
    return pltpu.CompilerParams(vmem_limit_bytes=vmem * MIB)


def cost(flops, bytes_accessed, trans=0):
    return pl.CostEstimate(
        flops=int(flops), bytes_accessed=int(bytes_accessed), transcendentals=int(trans)
    )


def whole(shape):
    return pl.BlockSpec(shape, lambda *_: (0,) * len(shape))


ANYWHERE = pl.BlockSpec(memory_space=pl.ANY)


def copies(pairs, sem):
    return [pltpu.make_async_copy(src, dst, sem.at[k]) for k, (src, dst) in enumerate(pairs)]


def started(pairs, sem):
    made = copies(pairs, sem)
    for copy in made:
        copy.start()
    return made


def done(made):
    for copy in made:
        copy.wait()


def lanes_of(shape, head):
    return (lax.broadcasted_iota(jnp.int32, shape, 1) % 128 < HD) == (head % 2 == 0)


def embedded(x_ref, pos_ref, table_ref):
    half = x_ref.shape[0]
    places = table_ref.shape[0]
    hot = (lax.broadcasted_iota(jnp.int32, (places, half), 0) == pos_ref[...]).astype(F32).astype(BF)
    return x_ref[...].astype(F32) + dot_tn(hot, table_ref[...])


def crop_lanes(seg_ref):
    half = seg_ref.shape[1]
    hot = (lax.broadcasted_iota(jnp.int32, (8, half), 0) == seg_ref[...]).astype(F32).astype(BF)
    eye = lax.broadcasted_iota(jnp.int32, (8, 128), 0) == lax.broadcasted_iota(jnp.int32, (8, 128), 1)
    return dot_tn(hot, eye.astype(F32).astype(BF)).astype(BF)


def front_kernel(block, blk_ref, *refs):
    sources, refs = refs[:21], refs[21:]
    (
        h0_out, n1_out, n1o_out, q_out, k_out, v_out, att_out, p_out, n2_out,
        gs_out, gk_out, as_out, ak_out, res_out, gn_out, h1_out, b1g_ref,
    ) = refs[:17]
    targets, refs = refs[17:38], refs[38:]
    (
        x_ref, xo_ref, seg_ref, sego_ref, pos_ref, poso_ref, cot_ref, table_ref,
        g1_ref, s1_ref, qb_ref, vb_ref, bo_ref, g2_ref, s2_ref, b1_ref, b2_ref, wqkv_ref, wo_ref, w1_ref, w2_ref,
    ) = targets
    (
        h0_ref, own_ref, n1_ref, n1o_ref, hoto_ref, q_ref, k_ref, v_ref, bias_ref,
        att_ref, p_ref, h1_ref, n2_ref, gp_ref, act_ref, mixed_ref, gn_ref, res_ref, bias_line_ref,
        in_sem, out_sem, late_sem,
    ) = refs
    half, width = x_ref.shape
    keys = k_ref.shape[0]
    halo = keys - half
    hidden = w1_ref.shape[1]
    blk = blk_ref[0]
    start = pl.multiple_of(blk * (half - halo), 16)
    loads = [pltpu.make_async_copy(src, dst, in_sem.at[k]) for k, (src, dst) in enumerate(zip(sources, targets))]
    outs = [
        pltpu.make_async_copy(src, dst, out_sem.at[k])
        for k, (src, dst) in enumerate(
            (
                (h0_ref, h0_out), (own_ref, n1_out), (n1o_ref, n1o_out), (q_ref, q_out), (k_ref, k_out),
                (v_ref, v_out), (att_ref, att_out), (n2_ref, n2_out), (res_ref, res_out), (gn_ref, gn_out),
                (h1_ref, h1_out), (p_ref, p_out),
            )
        )
    ]
    soon = (0, 4, 7, 1, 5, 8, 9, 17, 2, 3, 10, 11)
    then = (18, 19, 20, 6, 12, 13, 14, 15, 16)
    for k in soon:
        loads[k].start()
    for k in soon[:7]:
        loads[k].wait()
    hidden0 = embedded(x_ref, pos_ref, table_ref)
    h0_ref[...] = hidden0
    normal, _ = normalise(hidden0)
    own_ref[...] = (normal * line(g1_ref) + line(s1_ref)).astype(BF)
    n1_ref[:half, :] = own_ref[...]
    normal, _ = normalise(embedded(xo_ref, poso_ref, table_ref))
    n1o_ref[...] = (normal * line(g1_ref) + line(s1_ref)).astype(BF)
    n1_ref[half:, :] = n1o_ref[pl.ds(start, halo), :]
    for k in soon[7:]:
        loads[k].wait()
    for k in then:
        loads[k].start()
    hot = crop_lanes(seg_ref)
    hoto_ref[...] = crop_lanes(sego_ref)
    bias_ref[:, :half] = (dot_nt(hot, hot) - 1.0) * 1e9
    bias_ref[:, half:] = (dot_nt(hot, hoto_ref[pl.ds(start, halo), :]) - 1.0) * 1e9
    q = dot_nn(own_ref[...], wqkv_ref[:, :width]) + line(qb_ref)
    q_ref[...] = (q.astype(BF).astype(F32) * 0.125).astype(BF)
    k_ref[...] = dot_nn(n1_ref[...], wqkv_ref[:, width : 2 * width]).astype(BF)
    v_ref[...] = (dot_nn(n1_ref[...], wqkv_ref[:, 2 * width :]) + line(vb_ref)).astype(BF)
    for out in outs[:6]:
        out.start()
    rounds = 2
    pairs = width // 128 // rounds

    def heads(i, carry):
        for pair in range(pairs):
            cols = pl.ds(pl.multiple_of((i * pairs + pair) * 128, 128), 128)
            q = q_ref[:, cols]
            both = []
            for head in range(2):
                q_one = jnp.where(lanes_of(q.shape, head), q, jnp.zeros_like(q))
                scores = dot_nt(q_one, k_ref[:, cols]) + bias_ref[...]
                top = jnp.max(scores, -1, keepdims=True)
                weight = jnp.exp(scores - top)
                probs = (weight * (1.0 / jnp.sum(weight, -1, keepdims=True))).astype(BF)
                p_ref[2 * (i * pairs + pair) + head] = probs
                both.append(dot_nn(probs, v_ref[:, cols]))
            att_ref[:, cols] = jnp.where(lanes_of(both[0].shape, 0), both[0], both[1]).astype(BF)
        return carry

    lax.fori_loop(0, rounds, heads, 0)
    outs[6].start()
    outs[11].start()
    for k in then:
        loads[k].wait()
    hidden1 = h0_ref[...] + dot_nn(att_ref[...], wo_ref[...]) + line(bo_ref)
    h1_ref[...] = hidden1
    normal, _ = normalise(hidden1)
    n2_ref[...] = (normal * line(g2_ref) + line(s2_ref)).astype(BF)
    outs[7].start()
    outs[10].start()
    late = []
    chunk = 768
    part = chunk // 2
    mixed_ref[...] = hidden1 + line(b2_ref)
    gn_ref[...] = jnp.zeros_like(gn_ref)
    bias_line_ref[...] = line(b1_ref)

    def chunks(i, carry):
        for j in range(hidden // chunk // 2):
            first = i * (hidden // 2) + j * chunk
            at = pl.ds(pl.multiple_of(first, 128), chunk)
            pre = dot_nn(n2_ref[...], w1_ref[:, at]) + bias_line_ref[:, at]
            grad_act = dot_nt(cot_ref[...], w2_ref[at, :])
            cdf = 0.5 + 0.5 * lax.erf(pre * inv_root_two)
            act = (pre * cdf).astype(BF)
            slope = cdf + pre * jnp.exp(-0.5 * pre * pre) * inv_root_two_pi
            grad_pre = (grad_act * slope).astype(BF)
            b1g_ref[:, at] = column_sum(grad_pre.astype(F32))
            gp_ref[i, :, j * chunk : (j + 1) * chunk] = grad_pre
            mine = pl.ds(pl.multiple_of(i * (hidden // 4) + j * part, 128), part)
            for c in range(2):
                act_ref[c, :, mine] = jnp.concatenate(
                    [act[:, t : t + block] for t in range(c * block, chunk, 2 * block)], 1
                )
            mixed_ref[...] += dot_nn(act, w2_ref[at, :])
            gn_ref[...] += dot_nt(grad_pre, w1_ref[:, at])
        return carry

    lax.fori_loop(0, 2, chunks, 0)
    res_ref[...] = mixed_ref[...].astype(BF)
    for c, dst in enumerate((ak_out, as_out)):
        late.append((act_ref.at[(blk + c) % 2], dst))
    for c, dst in enumerate((gk_out, gs_out)):
        late.append((gp_ref.at[(blk + c) % 2], dst))
    late = [pltpu.make_async_copy(src, dst, late_sem.at[k]) for k, (src, dst) in enumerate(late)]
    for copy in late:
        copy.start()
    outs[8].start()
    outs[9].start()
    for out in outs:
        out.wait()
    for copy in late:
        copy.wait()


def front(plan, halo, blk, x, xo, seg, sego, pos, poso, cot, table, vectors, wqkv, wo, w1, w2):
    half, width = x.shape
    hidden = w1.shape[1]
    keys = half + halo
    heads = width // HD
    anywhere = pl.BlockSpec(memory_space=pl.ANY)
    operands = (x, xo, seg, sego, pos, poso, cot, table, *vectors, wqkv, wo, w1, w2)
    shapes = [
        ((half, width), F32),
        ((half, width), BF),
        ((half, width), BF),
        ((half, width), BF),
        ((keys, width), BF),
        ((keys, width), BF),
        ((half, width), BF),
        ((heads, half, keys), BF),
        ((half, width), BF),
        ((half, hidden // 2), BF),
        ((half, hidden // 2), BF),
        ((half, hidden // 2), BF),
        ((half, hidden // 2), BF),
        ((half, width), BF),
        ((half, width), F32),
        ((half, width), F32),
        ((1, hidden), F32),
    ]
    return pl.pallas_call(
        functools.partial(front_kernel, hidden // plan.groups // 2),
        grid_spec=pltpu.PrefetchScalarGridSpec(
            num_scalar_prefetch=1,
            grid=(1,),
            in_specs=[anywhere] * len(operands),
            out_specs=[anywhere] * 16 + [whole((1, hidden))],
            scratch_shapes=[pltpu.VMEM(v.shape, v.dtype) for v in operands]
            + [
                pltpu.VMEM((half, width), F32),
                pltpu.VMEM((half, width), BF),
                pltpu.VMEM((keys, width), BF),
                pltpu.VMEM((half, width), BF),
                pltpu.VMEM((half, 128), BF),
                pltpu.VMEM((half, width), BF),
                pltpu.VMEM((keys, width), BF),
                pltpu.VMEM((keys, width), BF),
                pltpu.VMEM((half, keys), F32),
                pltpu.VMEM((half, width), BF),
                pltpu.VMEM((heads, half, keys), BF),
                pltpu.VMEM((half, width), F32),
                pltpu.VMEM((half, width), BF),
                pltpu.VMEM((2, half, hidden // 2), BF),
                pltpu.VMEM((2, half, hidden // 2), BF),
                pltpu.VMEM((half, width), F32),
                pltpu.VMEM((half, width), F32),
                pltpu.VMEM((half, width), BF),
                pltpu.VMEM((1, hidden), F32),
                pltpu.SemaphoreType.DMA((len(operands),)),
                pltpu.SemaphoreType.DMA((12,)),
                pltpu.SemaphoreType.DMA((4,)),
            ],
        ),
        out_shape=[jax.ShapeDtypeStruct(*s) for s in shapes],
        compiler_params=params(60),
        cost_estimate=cost(
            2 * half * width * (5 * width + 4 * hidden) + 4 * half * keys * width, 8 * width * hidden
        ),
        name="front",
    )(blk, *operands)


def mid_kernel(blk_ref, gn_hbm, h1_hbm, cot_hbm, wo_hbm, g2_hbm, *refs):
    gh_ref, keep_ref, send_ref, ga_ref, sums_ref = refs[:5]
    gn_ref, h1_ref, cot_ref, wo_ref, g2_ref, gb_ref, sem = refs[5:]
    width = gb_ref.shape[1]
    cols = width // 2
    loads = started(zip((gn_hbm, h1_hbm, cot_hbm, g2_hbm, wo_hbm), (gn_ref, h1_ref, cot_ref, g2_ref, wo_ref)), sem)
    done(loads)
    normal, inv = normalise(h1_ref[...])
    total = gn_ref[...]
    cot = cot_ref[...].astype(F32)
    grad_hidden1 = cot + norm_back(total, normal, inv, line(g2_ref))
    gh_ref[...] = grad_hidden1
    branch = grad_hidden1.astype(BF)
    gb_ref[...] = branch
    for ref, core in ((keep_ref, blk_ref[0]), (send_ref, 1 - blk_ref[0])):
        ref[...] = gb_ref[:, pl.ds(pl.multiple_of(core * cols, 128), cols)]
    ga_ref[...] = dot_nt(branch, wo_ref[...]).astype(BF)
    sums_ref[0:1, :] = column_sum(total * normal)
    sums_ref[1:2, :] = column_sum(total)
    sums_ref[2:3, :] = column_sum(branch.astype(F32))
    sums_ref[3:4, :] = column_sum(cot)


def mid(blk, gn, h1, cot, wo, g2):
    half, width = h1.shape
    operands = (gn, h1, cot, wo, g2)
    part = ((half, width // 2), BF)
    shapes = [((half, width), F32), part, part, ((half, width), BF), ((4, width), F32)]
    return pl.pallas_call(
        mid_kernel,
        grid_spec=pltpu.PrefetchScalarGridSpec(
            num_scalar_prefetch=1,
            grid=(1,),
            in_specs=[ANYWHERE] * 5,
            out_specs=[whole(v[0]) for v in shapes],
            scratch_shapes=[pltpu.VMEM(v.shape, v.dtype) for v in operands]
            + [pltpu.VMEM((half, width), BF), pltpu.SemaphoreType.DMA((5,))],
        ),
        out_shape=[jax.ShapeDtypeStruct(*v) for v in shapes],
        compiler_params=params(60),
        cost_estimate=cost(1, 1),
        name="mid",
    )(blk, *operands)


class Plan:
    def __init__(self, ndp):
        self.ndp = ndp
        self.groups = min(16, ndp)
        self.bits = self.groups.bit_length() - 1
        self.rest = ndp // self.groups
        wanted = {"feed": ((0, 1, 2, 3), (1, 2, 0, 3), (2, 0, 1, 3)), "attend": ((0, 1, 2, 3), (1, 0, 2, 3))}
        self.orders = {k: [[b for b in o if b < self.bits] for o in v] for k, v in wanted.items()}
        self.small = [b for b in (2, 3, 1, 0) if b < self.bits]

    def place(self, name, piece, p):
        code = 0
        for bit in self.orders[name][piece]:
            code = 2 * code + ((p >> bit) & 1)
        return divmod(self.groups - 1 - code, self.groups // 2)


def feed_weights_kernel(plan, own_ref, blk_ref, *refs):
    sources, refs = refs[:12], refs[-24:]
    outs, targets, stages = refs[:6], refs[6:18], refs[18:20]
    acc_ref, low_ref, in_sem, out_sem = refs[20:]
    n2_ref, n2o_ref, g_ref, go_ref, act_ref, acto_ref, cot_ref, coto_ref, att_ref, atto_ref, gb_ref, gbo_ref = targets
    own = own_ref[0]
    width = n2_ref.shape[1]
    cols = width // 2
    groups, per = plan.groups, plan.groups // 2
    chunk = g_ref.shape[1] // 2
    rows = width // groups
    unit = rows // 2
    pairs = list(zip(sources, targets))
    loads = started(pairs, in_sem)

    def emit(number, p, value):
        piece, slot = divmod(number, 3)
        kept, place = plan.place("feed", piece, p)
        stages[kept][piece, place, slot] = value.astype(BF)

    done(loads[:4])
    for step in range(2):
        lanes = slice(step * chunk, (step + 1) * chunk)
        acc_ref[step] = dot_tn(n2_ref[...], g_ref[:, lanes]) + dot_tn(n2o_ref[...], go_ref[:, lanes])
        for p in range(groups):
            for k in range(2):
                source = pl.multiple_of((own ^ p) * rows + k * unit, 8)
                emit(5 + 2 * step + k, p, acc_ref[step, pl.ds(source, unit), :])
    done(loads[4:])
    low_ref[...] = dot_tn(att_ref[...], gb_ref[...]) + dot_tn(atto_ref[...], gbo_ref[...])
    for p in range(groups):
        source = pl.multiple_of((own ^ p) * rows, 16)
        block = low_ref[pl.ds(source, rows), :]
        emit(4, p, jnp.concatenate([block[:unit], block[unit:]], 1))
    sent = copies([(stages[kept].at[piece], outs[2 * piece + kept]) for piece in range(3) for kept in range(2)], out_sem)
    for copy in sent[4:]:
        copy.start()
    for step in range(2):
        lanes = pl.ds(pl.multiple_of(((own // per) ^ step) * chunk, 128), chunk)
        acc_ref[2 + step] = dot_tn(act_ref[:, lanes], cot_ref[...]) + dot_tn(acto_ref[:, lanes], coto_ref[...])
        for low in range(per):
            for k in range(4):
                source = pl.multiple_of(((own % per) ^ low) * (chunk // per) + k * unit, 8)
                emit(k, step * per + low, acc_ref[2 + step, pl.ds(source, unit), :])
    for copy in sent[:4]:
        copy.start()
    done(sent)


def feed_weights(plan, own, blk, *operands):
    half, width = operands[0].shape
    chunk, cols = operands[2].shape[1] // 2, width // 2
    part = jax.ShapeDtypeStruct((plan.groups // 2, 3, width // plan.groups // 2, width), BF)
    shapes = [v.shape for v in operands[:10]] + [(half, cols)] * 2

    return pl.pallas_call(
        functools.partial(feed_weights_kernel, plan),
        grid_spec=pltpu.PrefetchScalarGridSpec(
            num_scalar_prefetch=2,
            grid=(1,),
            in_specs=[ANYWHERE] * 12,
            out_specs=[ANYWHERE] * 6,
            scratch_shapes=[pltpu.VMEM(v, BF) for v in shapes]
            + [pltpu.VMEM((3,) + part.shape, BF)] * 2
            + [pltpu.VMEM((4, width, chunk), F32), pltpu.VMEM((width, cols), F32)]
            + [pltpu.SemaphoreType.DMA((12,)), pltpu.SemaphoreType.DMA((6,))],
        ),
        out_shape=(part,) * 6,
        compiler_params=params(60),
        cost_estimate=cost(1, 1),
        name="feed_weights",
    )(own, blk, *operands)


def attend_back_kernel(blk_ref, q_hbm, k_hbm, v_hbm, ga_hbm, p_hbm, *refs):
    outs, refs = refs[:6], refs[6:]
    q_ref, k_ref, v_ref, ga_ref, p_ref, d_ref, h_ref, sem, out_sem = refs
    half, width = q_ref.shape
    cols = width // 2
    heads = p_ref.shape[0]
    per = heads // 2
    fetch = []
    for side in range(2):
        at = slice(side * cols, (side + 1) * cols)
        arrays = [(src.at[:, at], dst.at[:, at]) for src, dst in ((q_hbm, q_ref), (k_hbm, k_ref), (v_hbm, v_ref), (ga_hbm, ga_ref))]
        fetch.append(copies(arrays + [(p_hbm.at[side * per : (side + 1) * per], p_ref.at[side * per : (side + 1) * per])], sem.at[side]))
    for copy in fetch[0]:
        copy.start()
    done(fetch[0])
    for copy in fetch[1]:
        copy.start()
    pairs = heads // 4

    def one_side(side, carry):
        @pl.when(side == 1)
        def _():
            done(fetch[1])

        for pair in range(pairs):
            lanes = pl.ds(pl.multiple_of(side * cols + pair * 128, 128), 128)
            at = slice(pair * 128, pair * 128 + 128)
            q, k, grad = q_ref[:, lanes], k_ref[:, lanes], ga_ref[:, lanes]
            dqs, dks, dvs = [], [], []
            for head in range(2):
                grad_one = jnp.where(lanes_of(grad.shape, head), grad, jnp.zeros_like(grad))
                grad_probs = dot_nt(grad_one, v_ref[:, lanes])
                low = p_ref[2 * (side * pairs + pair) + head]
                probs = low.astype(F32)
                row = jnp.sum(probs * grad_probs, -1, keepdims=True)
                grad_scores = (probs * (grad_probs - row)).astype(BF)
                dqs.append(dot_nn(grad_scores, k))
                dks.append(dot_tn(q, grad_scores))
                dvs.append(dot_tn(grad, low))
            d_ref[side, 0, :, at] = (jnp.where(lanes_of(dqs[0].shape, 0), dqs[0], dqs[1]) * 0.125).astype(BF)
            first = lax.broadcasted_iota(jnp.int32, dks[0].shape, 0) < HD
            dk = jnp.where(first, dks[0], dks[1]).T.astype(BF)
            dv = jnp.where(first, dvs[0], dvs[1]).T.astype(BF)
            d_ref[side, 1, :, at] = dk[:half]
            d_ref[side, 2, :, at] = dv[:half]
            h_ref[side, 0, :, at] = dk[half:]
            h_ref[side, 1, :, at] = dv[half:]
        return carry

    lax.fori_loop(0, 2, one_side, 0)
    core = blk_ref[0]
    done(
        started(
            [
                (h_ref.at[1 - core], outs[0]),
                (h_ref.at[core], outs[1]),
                (d_ref.at[core], outs[2]),
                (d_ref.at[1 - core, 0], outs[3]),
                (d_ref.at[1 - core, 1], outs[4]),
                (d_ref.at[1 - core, 2], outs[5]),
            ],
            out_sem,
        )
    )


def attend_back(blk, q, k, v, probs, ga, *after):
    half, width = q.shape
    keys = k.shape[0]
    halo = keys - half
    cols = width // 2
    shapes = ((2, halo, cols),) * 2 + ((3, half, cols),) + ((half, cols),) * 3

    def body(blk_ref, *refs):
        ins, refs = refs[:5], refs[5 + len(after) :]
        attend_back_kernel(blk_ref, *ins, *refs)

    return pl.pallas_call(
        body,
        grid_spec=pltpu.PrefetchScalarGridSpec(
            num_scalar_prefetch=1,
            grid=(1,),
            in_specs=[ANYWHERE] * (5 + len(after)),
            out_specs=[ANYWHERE] * 6,
            scratch_shapes=[
                pltpu.VMEM((half, width), BF),
                pltpu.VMEM((keys, width), BF),
                pltpu.VMEM((keys, width), BF),
                pltpu.VMEM((half, width), BF),
                pltpu.VMEM(probs.shape, BF),
                pltpu.VMEM((2, 3, half, cols), BF),
                pltpu.VMEM((2, 2, halo, cols), BF),
                pltpu.SemaphoreType.DMA((2, 5)),
                pltpu.SemaphoreType.DMA((6,)),
            ],
        ),
        out_shape=[jax.ShapeDtypeStruct(v, BF) for v in shapes],
        compiler_params=params(60),
        cost_estimate=cost(1, 1),
        name="attend_back",
    )(blk, q, k, v, ga, probs, *after)


def add_rows(ref, start, at, cols, extra):
    rows = pl.ds(start, extra.shape[0])
    part = ref[rows, pl.ds(at, cols)].astype(F32) + extra.astype(F32)
    ref[rows, pl.ds(at, cols)] = part.astype(BF)


def attend_weights_kernel(plan, own_ref, blk_ref, *refs):
    count = len(plan.orders["attend"])
    sources, outs, refs = refs[:8], refs[8 : 8 + 2 * count], refs[8 + 2 * count :]
    n1_ref, n1o_ref, hk_ref, ho_ref, mine_ref, other_ref, acc_ref, send_ref, keep_ref, sem, out_sem = refs
    half, width = n1_ref.shape
    halo = hk_ref.shape[1]
    cols = width // 2
    own, blk = own_ref[0], blk_ref[0]
    rows = width // plan.groups
    start = pl.multiple_of((1 - blk) * (half - halo), 16)
    start_other = pl.multiple_of(blk * (half - halo), 16)
    n1, n1o, d, hk, ho = sources[:5]
    pairs = [(d.at[k], mine_ref.at[:, k * cols : (k + 1) * cols]) for k in range(3)]
    pairs += [(sources[5 + k], other_ref.at[:, k * cols : (k + 1) * cols]) for k in range(3)]
    pairs += [(n1, n1_ref), (n1o, n1o_ref), (hk, hk_ref), (ho, ho_ref)]
    done(started(pairs, sem))
    for which in range(2):
        lane = (1 + which) * cols
        add_rows(mine_ref, start, lane, cols, ho_ref[which])
        add_rows(other_ref, start_other, lane, cols, hk_ref[which])
    part = rows // count
    stages = (send_ref, keep_ref)
    for at in (slice(0, width), slice(width, width + cols)):
        acc_ref[:, at] = dot_tn(n1_ref[...], mine_ref[:, at]) + dot_tn(n1o_ref[...], other_ref[:, at])
        for p in range(plan.groups):
            for piece in range(count):
                source = pl.multiple_of((own ^ p) * rows + piece * part, 8)
                kept, place = plan.place("attend", piece, p)
                stages[kept][piece, place, :, at] = acc_ref[pl.ds(source, part), at].astype(BF)
    done(
        started(
            [(stages[kept].at[piece], outs[2 * piece + kept]) for piece in range(count) for kept in range(2)], out_sem
        )
    )


def attend_weights(plan, own, blk, n1, n1o, d, hk, ho, do):
    half, width = n1.shape
    cols = width // 2
    count = len(plan.orders["attend"])
    part = jax.ShapeDtypeStruct((plan.groups // 2, width // plan.groups // count, 3 * cols), BF)
    return pl.pallas_call(
        functools.partial(attend_weights_kernel, plan),
        grid_spec=pltpu.PrefetchScalarGridSpec(
            num_scalar_prefetch=2,
            grid=(1,),
            in_specs=[ANYWHERE] * 8,
            out_specs=[ANYWHERE] * (2 * count),
            scratch_shapes=[pltpu.VMEM((half, width), BF)] * 2
            + [pltpu.VMEM(hk.shape, BF)] * 2
            + [pltpu.VMEM((half, 3 * cols), BF)] * 2
            + [pltpu.VMEM((width, 3 * cols), F32)]
            + [pltpu.VMEM((count,) + part.shape, BF)] * 2
            + [pltpu.SemaphoreType.DMA((10,)), pltpu.SemaphoreType.DMA((2 * count,))],
        ),
        out_shape=(part,) * (2 * count),
        compiler_params=params(60),
        cost_estimate=cost(1, 1),
        name="attend_weights",
    )(own, blk, n1, n1o, d, hk, ho, *do)


def front_back_kernel(places, blk_ref, *refs):
    sources, refs = refs[:13], refs[13:]
    gx_ref, small_mine, small_other = refs[:3]
    gj_ref, w_ref, h0_ref, gh_ref, g1_ref, pos_ref, sums_ref, b1_ref, ho_ref, hl_ref, small_ref, sem = refs[3:]
    half, width = h0_ref.shape
    halo = ho_ref.shape[1]
    cols = width // 2
    blk = blk_ref[0]
    start = pl.multiple_of((1 - blk) * (half - halo), 16)
    lanes = [[pl.multiple_of(which * width + core * cols, 128) for core in (blk, 1 - blk)] for which in range(3)]
    pairs = [(sources[4 + 2], w_ref)]
    pairs += [(sources[0].at[k], gj_ref.at[:, pl.ds(lanes[k][0], cols)]) for k in range(3)]
    pairs += [(sources[1 + k], gj_ref.at[:, pl.ds(lanes[k][1], cols)]) for k in range(3)]
    pairs += [(sources[4], ho_ref), (sources[5], hl_ref)]
    pairs += list(zip(sources[7:], (h0_ref, gh_ref, g1_ref, pos_ref, sums_ref, b1_ref)))
    loads = started(pairs, sem)
    done(loads[1:9])
    for which in range(2):
        add_rows(gj_ref, start, lanes[1 + which][0], cols, ho_ref[which])
        add_rows(gj_ref, start, lanes[1 + which][1], cols, hl_ref[which])
    done(loads[:1] + loads[9:])
    total = dot_nt(gj_ref[...], w_ref[...])
    small_ref[places + 2 : places + 3, :] = column_sum(gj_ref[:, :width].astype(F32))
    small_ref[places + 3 : places + 4, :] = column_sum(gj_ref[:, 2 * width :].astype(F32))
    normal, inv = normalise(h0_ref[...])
    small_ref[places : places + 1, :] = column_sum(total * normal)
    small_ref[places + 1 : places + 2, :] = column_sum(total)
    grad = (gh_ref[...] + norm_back(total, normal, inv, line(g1_ref))).astype(BF)
    gx_ref[...] = grad
    hot = (lax.broadcasted_iota(jnp.int32, (places, half), 0) == pos_ref[...]).astype(F32).astype(BF)
    small_ref[:places, :] = dot_nn(hot, grad)
    small_ref[places + 4 : places + 8, :] = sums_ref[...]
    for k in range(4):
        small_ref[places + 8 + k : places + 9 + k, :] = b1_ref[:, k * width : (k + 1) * width]
    for ref, core in ((small_mine, blk), (small_other, 1 - blk)):
        ref[0] = small_ref[:, pl.ds(pl.multiple_of(core * cols, 128), cols)].astype(BF)


def front_back(blk, d, ds, ho, hl, w, h0, gh, g1, pos, sums, b1, places):
    half, width = h0.shape
    extra = (1, places + 12, width // 2)
    rest = (w, h0, gh, g1, pos, sums, b1, ho, hl)
    return pl.pallas_call(
        functools.partial(front_back_kernel, places),
        grid_spec=pltpu.PrefetchScalarGridSpec(
            num_scalar_prefetch=1,
            grid=(1,),
            in_specs=[ANYWHERE] * 13,
            out_specs=[whole((half, width)), whole(extra), whole(extra)],
            scratch_shapes=[pltpu.VMEM((half, 3 * width), BF)]
            + [pltpu.VMEM(v.shape, v.dtype) for v in rest]
            + [pltpu.VMEM((places + 12, width), F32), pltpu.SemaphoreType.DMA((15,))],
        ),
        out_shape=(
            jax.ShapeDtypeStruct((half, width), BF),
            jax.ShapeDtypeStruct(extra, BF),
            jax.ShapeDtypeStruct(extra, BF),
        ),
        compiler_params=params(60),
        cost_estimate=cost(1, 1),
        name="front_back",
    )(blk, d, *ds, ho, hl, *rest[:7])


def swap(v):
    return lax.ppermute(v, "blk", [(0, 1), (1, 0)])


def across(v, ndp, flip):
    return lax.ppermute(v, "dp", [(i, i ^ flip) for i in range(ndp)])


def wide(v):
    return v.astype(F32)


def combine_kernel(plans, *refs):
    outs = refs[-len(plans) :]
    used = 0
    for out, plan in zip(outs, plans):
        at = 0
        for count, terms in plan:
            total = refs[used][...].astype(F32)
            for ref in refs[used + 1 : used + terms]:
                total = total + ref[...].astype(F32)
            used += terms
            out[at : at + count] = total.astype(out.dtype)
            at += count


def combine(arrays, plans, types, before=()):
    block = arrays[0].shape[1:]
    shapes = [(sum(count for count, _ in plan),) + block for plan in plans]
    if before:
        arrays = [behind(arrays[0], *before)] + list(arrays[1:])
    operands, specs, counts = [], [], []
    for plan in plans:
        counts.append([])
        for count, terms in plan:
            counts[-1].append((count, len(terms)))
            for index, start in terms:
                operands.append(arrays[index])
                specs.append(
                    pl.BlockSpec(
                        (count,) + block, functools.partial(lambda at, i: (at,) + (0,) * len(block), start // count)
                    )
                )
    return pl.pallas_call(
        functools.partial(combine_kernel, counts),
        grid=(1,),
        in_specs=specs,
        out_specs=[whole(v) for v in shapes],
        out_shape=[jax.ShapeDtypeStruct(v, t) for v, t in zip(shapes, types)],
        compiler_params=params(24),
        cost_estimate=cost(1, 1),
        name="combine",
    )(*operands)


class Pieces:
    def __init__(self, plan, name, parts):
        self.plan, self.orders, self.phase = plan, plan.orders[name], 0
        self.terms = [[(parts[2 * k + 1], 0, 0)] for k in range(len(self.orders))]
        self.at, self.left = 0, plan.groups // 2
        self.sent = parts[0]
        for k in range(len(self.orders)):
            self.terms[k].append((self.across(parts[2 * k], self.orders[k][0]), 0, 0))
        self.phase = 1

    def across(self, value, bit):
        return across(value, self.plan.ndp, self.plan.rest << bit)

    def collect(self):
        arrays, where = [], []
        for k in range(len(self.orders)):
            where.append([])
            for array, place, start in self.terms[k]:
                if not any(array is v for v in arrays):
                    arrays.append(array)
                index = [array is v for v in arrays].index(True)
                where[k].append((index, start + self.at - place))
        return arrays, where

    def step(self, *before):
        if self.phase >= self.plan.bits:
            return
        h = self.left // 2
        arrays, where = self.collect()
        bits = [order[self.phase] for order in self.orders]
        joined = len(set(bits)) == 1
        plans = [[(h, w)] for w in where]
        values = combine(arrays, [sum(plans, [])] if joined else plans, [BF] * len(self.orders), before)
        self.at, self.left = self.at + h, h
        self.sent = values[0]
        if joined:
            got = [self.across(values[0], bits[0])] * len(bits)
        else:
            got = [self.across(v, bit) for v, bit in zip(values, bits)]
        for k in range(len(self.orders)):
            self.terms[k].append((got[k], self.at, k * h if joined else 0))
        self.phase += 1

    def totals(self, *before):
        arrays, where = self.collect()
        return combine(arrays, [[(1, w) for w in where]], [F32], before)[0]


class Everywhere:
    def __init__(self, plan, mine, other):
        self.plan, self.phase = plan, 0
        self.flips = [plan.rest << b for b in plan.small] + [1 << b for b in range(plan.rest.bit_length() - 1)] + [None]
        self.sent, self.got = mine, swap(other)

    def step(self, *before):
        if self.phase >= len(self.flips):
            return
        (self.sent,) = combine([self.sent, self.got], [[(1, [(0, 0), (1, 0)])]], [BF], before)
        flip = self.flips[self.phase]
        self.got = swap(self.sent) if flip is None else across(self.sent, self.plan.ndp, flip)
        self.phase += 1

    def both(self):
        while self.phase < len(self.flips):
            self.step()
        return self.sent, self.got


def split_feed_kernel(counts, blk_ref, *refs):
    fc2_ref, mine, other = refs[-3:]
    units = []
    used = 0
    for terms in counts:
        total = refs[used][0].astype(F32)
        for ref in refs[used + 1 : used + terms]:
            total = total + ref[0].astype(F32)
        used += terms
        units += [total[k] for k in range(3)]
    unit, cols = mine.shape[1], mine.shape[2] // 2
    for k in range(4):
        fc2_ref[k * unit : (k + 1) * unit, :] = units[k]
    low_core = blk_ref[0] == 0
    for k in range(2):
        low, high = units[5 + 2 * k], units[6 + 2 * k]
        mine[k] = jnp.where(low_core, low, high)
        other[k] = jnp.where(low_core, high, low)
    low, high = units[4][:, :cols], units[4][:, cols:]
    mine[2, :, :cols] = jnp.where(low_core, low, high)
    other[2, :, :cols] = jnp.where(low_core, high, low)
    mine[2, :, cols:] = jnp.zeros_like(low)
    other[2, :, cols:] = jnp.zeros_like(low)


def split_feed(blk, pieces):
    arrays, where = pieces.collect()
    block = (1,) + arrays[0].shape[1:]
    unit, width = block[2:]
    shapes = [(4 * unit, width), (3, unit, width), (3, unit, width)]
    places = [(index, at) for terms in where for index, at in terms]
    return pl.pallas_call(
        functools.partial(split_feed_kernel, [len(terms) for terms in where]),
        grid_spec=pltpu.PrefetchScalarGridSpec(
            num_scalar_prefetch=1,
            grid=(1,),
            in_specs=[
                pl.BlockSpec(block, functools.partial(lambda at, i, b: (at, 0, 0, 0), at)) for _, at in places
            ],
            out_specs=[whole(v) for v in shapes],
        ),
        out_shape=[jax.ShapeDtypeStruct(v, F32) for v in shapes],
        compiler_params=params(24),
        cost_estimate=cost(1, 1),
        name="split_feed",
    )(blk, *[arrays[index] for index, _ in places])


def join_feed_kernel(blk_ref, mine_ref, got_ref, fc1_ref, out_ref):
    width = mine_ref.shape[2]
    cols = width // 2
    for ref, core in ((mine_ref, blk_ref[0]), (got_ref, 1 - blk_ref[0])):
        for k in range(2):
            fc1_ref[:, pl.ds(pl.multiple_of((core * 2 + k) * width, 128), width)] = ref[k]
        out_ref[:, pl.ds(pl.multiple_of(core * cols, 128), cols)] = ref[2, :, :cols]


def join_feed(blk, mine, got):
    _, rows, width = mine.shape
    shapes = [(rows, 4 * width), (rows, width)]
    return pl.pallas_call(
        join_feed_kernel,
        grid_spec=pltpu.PrefetchScalarGridSpec(
            num_scalar_prefetch=1,
            grid=(1,),
            in_specs=[whole(mine.shape)] * 2,
            out_specs=[whole(v) for v in shapes],
        ),
        out_shape=[jax.ShapeDtypeStruct(v, F32) for v in shapes],
        compiler_params=params(24),
        cost_estimate=cost(1, 1),
        name="join_feed",
    )(blk, mine, got)


def join_attend_kernel(blk_ref, mine_ref, got_ref, qkv_ref):
    cols = mine_ref.shape[1] // 3
    for ref, core in ((mine_ref, blk_ref[0]), (got_ref, 1 - blk_ref[0])):
        for k in range(3):
            at = pl.ds(pl.multiple_of((2 * k + core) * cols, 128), cols)
            qkv_ref[:, at] = ref[:, k * cols : (k + 1) * cols]


def join_attend(blk, mine, got):
    shape = (mine.shape[0], 2 * mine.shape[1])
    return pl.pallas_call(
        join_attend_kernel,
        grid_spec=pltpu.PrefetchScalarGridSpec(
            num_scalar_prefetch=1, grid=(1,), in_specs=[whole(mine.shape)] * 2, out_specs=whole(shape)
        ),
        out_shape=jax.ShapeDtypeStruct(shape, F32),
        compiler_params=params(24),
        cost_estimate=cost(1, 1),
        name="join_attend",
    )(blk, mine, got)


def split_attend_kernel(counts, blk_ref, *refs):
    mine, other, whole_ref = refs[-3:]
    part = whole_ref.shape[0] // len(counts)
    used = 0
    for piece, terms in enumerate(counts):
        total = refs[used][0].astype(F32)
        for ref in refs[used + 1 : used + terms]:
            total = total + ref[0].astype(F32)
        used += terms
        whole_ref[piece * part : (piece + 1) * part, :] = total
    half = mine.shape[0]
    low, high = whole_ref[:half, :], whole_ref[half:, :]
    low_core = blk_ref[0] == 0
    mine[...] = jnp.where(low_core, low, high)
    other[...] = jnp.where(low_core, high, low)


def split_attend(blk, pieces):
    arrays, where = pieces.collect()
    _, part, cols = arrays[0].shape
    shape = (len(where) * part // 2, cols)
    places = [(index, at) for terms in where for index, at in terms]
    return pl.pallas_call(
        functools.partial(split_attend_kernel, [len(terms) for terms in where]),
        grid_spec=pltpu.PrefetchScalarGridSpec(
            num_scalar_prefetch=1,
            grid=(1,),
            in_specs=[
                pl.BlockSpec((1, part, cols), functools.partial(lambda at, i, b: (at, 0, 0), at)) for _, at in places
            ],
            out_specs=[whole(shape)] * 2,
            scratch_shapes=[pltpu.VMEM((len(where) * part, cols), F32)],
        ),
        out_shape=[jax.ShapeDtypeStruct(shape, F32)] * 2,
        compiler_params=params(24),
        cost_estimate=cost(1, 1),
        name="split_attend",
    )(blk, *[arrays[index] for index, _ in places])


def join_small_kernel(blk_ref, mine_ref, got_ref, *outs):
    joined_ref = outs[-1]
    cols = mine_ref.shape[2]
    width = 2 * cols
    places = outs[0].shape[0]
    for ref, core in ((mine_ref, blk_ref[0]), (got_ref, 1 - blk_ref[0])):
        joined_ref[:, pl.ds(pl.multiple_of(core * cols, 128), cols)] = ref[0].astype(F32)
    outs[0][...] = joined_ref[:places, :]
    for k, out in enumerate(outs[1:9]):
        out[...] = joined_ref[places + k, :]
    for k in range(outs[9].shape[0] // width):
        outs[9][k * width : (k + 1) * width] = joined_ref[places + 8 + k, :]


def join_small(blk, mine, got, places, hidden):
    _, rows, cols = mine.shape
    width = 2 * cols
    shapes = [(places, width)] + [(width,)] * 8 + [(hidden,)]
    return pl.pallas_call(
        join_small_kernel,
        grid_spec=pltpu.PrefetchScalarGridSpec(
            num_scalar_prefetch=1,
            grid=(1,),
            in_specs=[whole(mine.shape)] * 2,
            out_specs=[whole(v) for v in shapes],
            scratch_shapes=[pltpu.VMEM((rows, width), F32)],
        ),
        out_shape=[jax.ShapeDtypeStruct(v, F32) for v in shapes],
        compiler_params=params(24),
        cost_estimate=cost(1, 1),
        name="join_small",
    )(blk, mine, got)


def join(blk, attend_mine, attend_got, feed_mine, feed_got, mine, got, places, hidden):
    unit, cols = attend_mine.shape
    rows, width = mine.shape[1], feed_mine.shape[2]
    shapes = [(unit, 2 * cols), (unit, 4 * width), (unit, width), (places, width)] + [(width,)] * 8 + [(hidden,)]
    operands = (attend_mine, attend_got, feed_mine, feed_got, mine, got)

    def kernel(blk_ref, *refs):
        join_attend_kernel(blk_ref, refs[0], refs[1], refs[6])
        join_feed_kernel(blk_ref, refs[2], refs[3], refs[7], refs[8])
        join_small_kernel(blk_ref, refs[4], refs[5], *refs[9:])

    return pl.pallas_call(
        kernel,
        grid_spec=pltpu.PrefetchScalarGridSpec(
            num_scalar_prefetch=1,
            grid=(1,),
            in_specs=[whole(v.shape) for v in operands],
            out_specs=[whole(v) for v in shapes],
            scratch_shapes=[pltpu.VMEM((rows, width), F32)],
        ),
        out_shape=[jax.ShapeDtypeStruct(v, F32) for v in shapes],
        compiler_params=params(24),
        cost_estimate=cost(1, 1),
        name="join",
    )(blk, *operands)


def behind(values, *others):
    return lax.optimization_barrier((values, others))[0]


def rest_of(plan, value, blk):
    groups = [[g * plan.rest + i for i in range(plan.rest)] for g in range(plan.groups)]
    value = lax.psum(value, "dp", axis_index_groups=groups)
    rows = value.shape[0] // (2 * plan.rest)
    return lax.dynamic_slice_in_dim(value, ((lax.axis_index("dp") % plan.rest) * 2 + blk) * rows, rows, axis=0)


def per_device(
    ndp, inputs, segments, positions, pos_table, ln1_gain, ln1_shift, qkv_weight, query_bias,
    value_bias, out_weight, out_bias, ln2_gain, ln2_shift, fc1_weight, fc1_bias, fc2_weight,
    fc2_bias, cotangent,
):
    plan = Plan(ndp)
    x, cot = inputs[0], cotangent[0]
    half, width = x.shape
    hidden = fc1_weight.shape[1]
    places = pos_table.shape[0]
    halo = next(h for h in range(SEG_MOST - 1, half + 1) if (half + h) % 128 == 0 and (half - h) % 16 == 0)
    blk = lax.axis_index("blk")
    dp = lax.axis_index("dp")
    blk1 = blk.astype(jnp.int32).reshape(1)
    own1 = (dp // plan.rest).astype(jnp.int32).reshape(1)

    x_other, seg_other, pos_other = swap(x), swap(segments), swap(positions)
    cot_other = swap(cot)
    vectors = (ln1_gain, ln1_shift, query_bias, value_bias, out_bias, ln2_gain, ln2_shift, fc1_bias, fc2_bias)
    (
        hidden0, n1, n1_other, q, k, v, att, probs, n2, grad_send, grad_keep, act_send, act_keep, result, gn2, hidden1,
        b1_grad,
    ) = front(
        plan, halo, blk1, x, x_other, segments, seg_other, positions, pos_other, cot, pos_table, vectors,
        qkv_weight, out_weight, fc1_weight, fc2_weight,
    )
    grad_other, act_other, n2_other = swap(grad_send), swap(act_send), swap(behind(n2, cot_other))
    gh1, gb, gb_send, ga, sums = mid(blk1, gn2, hidden1, cot, out_weight, ln2_gain)
    att_other, gb_other = swap(att), swap(gb_send)
    parts = feed_weights(
        plan, own1, blk1, behind(n2, ga), n2_other, grad_keep, grad_other, act_keep, act_other, cot, cot_other, att, att_other, gb, gb_other,
    )
    feed_sums = Pieces(plan, "feed", parts)
    h_send, h_keep, d_keep, *d_send = attend_back(blk1, behind(q, parts[0]), k, v, probs, ga)
    h_other, h_late = swap(h_send), swap(h_keep)
    d_other = [swap(v) for v in d_send]
    grad_x, mine, other = front_back(
        blk1, d_keep, d_send, h_other, h_late, qkv_weight, hidden0, gh1, ln1_gain, positions, sums, b1_grad, places
    )
    small = Everywhere(plan, mine, other)
    feed_sums.step(grad_x)
    small.step(feed_sums.sent)
    parts = attend_weights(
        plan, own1, blk1, behind(n1, small.sent), n1_other, d_keep, h_keep, h_other, d_other
    )
    attend_sums = Pieces(plan, "attend", parts)
    before = parts[0]
    for item in (small, feed_sums, attend_sums, small, feed_sums, attend_sums, small, attend_sums, small):
        item.step(before)
        before = item.sent
    unit = width // plan.groups // 2
    attend_mine, attend_sent = split_attend(blk1, attend_sums)
    if plan.rest == 1:
        fc2_grad, feed_mine, feed_sent = split_feed(blk1, feed_sums)
        feed_got = swap(feed_sent)
        qkv_grad, fc1_grad, out_grad, table, *vec, b1_all = join(
            blk1, attend_mine, swap(attend_sent), feed_mine, feed_got, *small.both(), places, hidden
        )
    else:
        units = feed_sums.totals().reshape(9, unit, width)
        fc2_grad = rest_of(plan, lax.all_gather(units[:4].reshape(-1, width), "blk", axis=0, tiled=True), blk)
        rows = jnp.concatenate([units[5:7].reshape(-1, width), units[7:].reshape(-1, width)], 1)
        fc1_grad = rest_of(plan, lax.all_gather(rows, "blk", axis=1, tiled=True), blk)
        rows = jnp.concatenate([units[4][:, : width // 2], units[4][:, width // 2 :]], 0)
        out_grad = rest_of(plan, lax.all_gather(rows, "blk", axis=1, tiled=True), blk)
        rows = jnp.where(blk == 0, jnp.stack([attend_mine, attend_sent]), jnp.stack([attend_sent, attend_mine]))
        rows = rows.reshape(2 * unit, 3, width // 2)
        qkv_grad = rest_of(plan, lax.all_gather(rows, "blk", axis=2, tiled=True).reshape(2 * unit, -1), blk)
        table, *vec, b1_all = join_small(blk1, *small.both(), places, hidden)
    return (
        result[None], grad_x[None], table, vec[0], vec[1], qkv_grad, vec[2], vec[3], out_grad,
        vec[6], vec[4], vec[5], fc1_grad, b1_all, fc2_grad, vec[7],
    )


def solution(mesh):
    split = P("dp", "blk", None)
    ids = P("dp", "blk")
    both = P(("dp", "blk"), None)
    none = P()
    return jax.shard_map(
        functools.partial(per_device, mesh.shape["dp"]),
        mesh=mesh,
        in_specs=(split, ids, ids) + (none,) * 14 + (split,),
        out_specs=(
            split, split, none, none, none, both, none, none, both, none, none, none, both, none, both, none,
        ),
        check_vma=False,
    )
```
